32 devices in a mesh: rep: 8 (over y, x, core), grp: 4 (over z).
Axes of the slice: x: 2, y: 2, z: 4, core: 2. Of those that a mesh axis runs over, the one named last changes fastest.
Arguments:
- row_ids: int32 [16384, 26, 30], P(('rep', 'grp')), may hold values from 0 to 2047
- bag_counts: int32 [16384, 26], P(('rep', 'grp')), may hold values from 1 to 30
- labels: int32 [16384], P(('rep', 'grp')), may hold values from 0 to 1
- dense_input: float32 [16384, 128], P(('rep', 'grp')), may hold values from -6 to 6
- tables: float32 [26, 2048, 128], P(None, 'grp'), may hold values from -6 to 6
- table_first: float32 [26, 2048, 128], P(None, 'grp'), may hold values from -1.1920929e-07 to 1.1920929e-07
- table_second: float32 [26, 2048, 128], P(None, 'grp'), may hold values from 1.490116e-17 to 2.3841857e-16
- cross_down: float32 [3, 3456, 512], P(None, 'rep'), may hold values from -0.109375 to 0.109375
- down_first: float32 [3, 3456, 512], P(None, 'rep'), may hold values from -9.536743e-06 to 9.536743e-06
- down_second: float32 [3, 3456, 512], P(None, 'rep'), may hold values from 1.2207031e-13 to 1.953125e-12
- cross_up: float32 [3, 512, 3456], P(None, 'rep'), may hold values from -0.25 to 0.25
- up_first: float32 [3, 512, 3456], P(None, 'rep'), may hold values from -4.7683716e-06 to 4.7683716e-06
- up_second: float32 [3, 512, 3456], P(None, 'rep'), may hold values from 3.0517577e-14 to 4.8828124e-13
- hidden_one: float32 [3456, 1024], P('rep'), may hold values from -0.109375 to 0.109375
- one_first: float32 [3456, 1024], P('rep'), may hold values from -3.8146973e-05 to 3.8146973e-05
- one_second: float32 [3456, 1024], P('rep'), may hold values from 1.4953613e-12 to 2.380371e-11
- hidden_two: float32 [1024, 1024], P('rep'), may hold values from -0.1875 to 0.1875
- two_first: float32 [1024, 1024], P('rep'), may hold values from -2.2888184e-05 to 2.2888184e-05
- two_second: float32 [1024, 1024], P('rep'), may hold values from 6.1035156e-13 to 9.765625e-12
- hidden_three: float32 [1024, 512], P('rep'), may hold values from -0.1875 to 0.1875
- three_first: float32 [1024, 512], P('rep'), may hold values from -6.1035156e-05 to 6.1035156e-05
- three_second: float32 [1024, 512], P('rep'), may hold values from 4.394531e-12 to 7.019043e-11
- smalls: float32 [13441], replicated, may hold values from -0.625 to 0.625
- small_first: float32 [13441], replicated, may hold values from -1 to 1
- small_second: float32 [13441], replicated, may hold values from 0 to 1
Outputs:
- loss_sum: float32 [], replicated
- new_tables: float32 [26, 2048, 128], P(None, 'grp')
- new_table_first: float32 [26, 2048, 128], P(None, 'grp')
- new_table_second: float32 [26, 2048, 128], P(None, 'grp')
- new_down: float32 [3, 3456, 512], P(None, 'rep')
- new_down_first: float32 [3, 3456, 512], P(None, 'rep')
- new_down_second: float32 [3, 3456, 512], P(None, 'rep')
- new_up: float32 [3, 512, 3456], P(None, 'rep')
- new_up_first: float32 [3, 512, 3456], P(None, 'rep')
- new_up_second: float32 [3, 512, 3456], P(None, 'rep')
- new_one: float32 [3456, 1024], P('rep')
- new_one_first: float32 [3456, 1024], P('rep')
- new_one_second: float32 [3456, 1024], P('rep')
- new_two: float32 [1024, 1024], P('rep')
- new_two_first: float32 [1024, 1024], P('rep')
- new_two_second: float32 [1024, 1024], P('rep')
- new_three: float32 [1024, 512], P('rep')
- new_three_first: float32 [1024, 512], P('rep')
- new_three_second: float32 [1024, 512], P('rep')
- new_smalls: float32 [13441], replicated
- new_small_first: float32 [13441], replicated
- new_small_second: float32 [13441], replicated
The draws below stay inside these ranges and needn't reach their ends.
All inputs are finite; a program needn't handle non-finite values.
Results may differ from the reference program's by a relative error of at most 0.019.
Values may be sent and summed in bfloat16 or wider, within the bound.
No kernel may reach another device: no remote copies, remote signals or barrier semaphores. Data moves between devices by JAX's collectives and lax.ppermute only.
A program may use at most 384 MiB of HBM per device.

```python
import math
import jax
import jax.numpy as jnp
from jax import lax

FEATURES = 26
EMB = 128
DENSE = 128
D_IN = 3456
RANK = 512
CROSS = 3
H1 = 1024
H2 = 1024
H3 = 512
BAG = 30
STEP = 10
SAMPLES = 16384
ROWS = 2048
SMALL = 13441


def small_scales():
    return jnp.concatenate([jnp.full((CROSS * D_IN,), 0.0006, jnp.float32), jnp.full((H1,), 0.0045, jnp.float32), jnp.full((H2,), 0.009, jnp.float32), jnp.full((H3,), 0.025, jnp.float32), jnp.full((H3,), 0.2, jnp.float32), jnp.full((1,), 0.5, jnp.float32)]) * SAMPLES ** (-0.5)


def draw_small_first(key, part):
    key = jax.random.fold_in(key, 11)
    return 0.111 * small_scales() * jax.random.normal(key, (SMALL,), jnp.float32)


def draw_small_second(key, part):
    key = jax.random.fold_in(key, 12)
    scales = small_scales()
    factor = jnp.exp(jax.random.uniform(key, (SMALL,), jnp.float32, jnp.log(0.0005), jnp.log(0.008)))
    return factor * scales * scales


def touch_ends(result, stream_key, smallest, top_value):
    dims = result.shape
    index_at = [jax.random.randint(jax.random.fold_in(stream_key, axis), (), 0, dims[axis]) for axis in range(len(dims))]
    result = result.at[tuple(index_at)].set(smallest)
    longest = dims.index(max(dims))
    index_at[longest] = (index_at[longest] + 1) % dims[longest]
    return result.at[tuple(index_at)].set(top_value)


def level_of(stream_key, dims, cuts, least, high):
    level, own = 1.0, jax.random.fold_in(stream_key, 6)
    for position, shards_of in cuts:
        draws = jnp.exp(jax.random.uniform(jax.random.fold_in(own, position), (shards_of,), jnp.float32, least / len(cuts), high / len(cuts)))
        level = level * jnp.repeat(draws, dims[position] // shards_of).reshape([-1 if axis == position else 1 for axis in range(len(dims))])
    return level


def noise(rng, dims, scale, reach, cuts=(), held_as=jnp.bfloat16):
    result = scale * jax.random.normal(rng, dims, jnp.float32)
    if cuts:
        result = result * level_of(rng, dims, cuts, -0.22, 0.18)
    return jnp.clip(result, -reach, reach).astype(held_as)


def setup_inputs(seed: int = 0) -> dict:
    splits = jax.random.split(jax.random.key(seed), 26)
    row_ids = touch_ends(jax.random.randint(splits[0], (SAMPLES, FEATURES, BAG), 0, ROWS), jax.random.fold_in(splits[0], 1), 0, ROWS - 1).astype(jnp.int32)
    bag_counts = touch_ends(jax.random.randint(splits[1], (SAMPLES, FEATURES), 1, BAG + 1), jax.random.fold_in(splits[1], 1), 1, BAG).astype(jnp.int32)
    labels = touch_ends(jax.random.randint(splits[2], (SAMPLES,), 0, 2), jax.random.fold_in(splits[2], 1), 0, 1).astype(jnp.int32)
    dense_input = noise(splits[3], (SAMPLES, DENSE), 1.0, 6.0, ((0, 32),), jnp.float32)
    tables = noise(splits[4], (FEATURES, ROWS, EMB), 1.0, 6.0, ((1, 4),), jnp.float32)
    table_first = noise(splits[5], (FEATURES, ROWS, EMB), (0.000111 * (SAMPLES * ROWS) ** -0.5), 1.1920928955078125e-07, ((1, 4),), jnp.float32)
    table_second = jnp.clip(jnp.exp(math.log(2.384185723586246e-16) - 2.7725887 * jax.random.uniform(splits[6], (FEATURES, ROWS, EMB), jnp.float32) ** level_of(splits[6], (FEATURES, ROWS, EMB), ((1, 4),), -0.2, 0.2)), 1.4901160772414037e-17, 2.384185723586246e-16)
    cross_down = noise(splits[7], (CROSS, D_IN, RANK), D_IN ** -0.5, 0.109375, ((1, 8),), jnp.float32)
    down_first = noise(splits[8], (CROSS, D_IN, RANK), (0.00022 * SAMPLES ** -0.5), 9.5367431640625e-06, ((1, 8),), jnp.float32)
    down_second = jnp.clip(jnp.exp(math.log(1.9531249447618526e-12) - 2.7725887 * jax.random.uniform(splits[9], (CROSS, D_IN, RANK), jnp.float32) ** level_of(splits[9], (CROSS, D_IN, RANK), ((1, 8),), -0.2, 0.2)), 1.220703090476158e-13, 1.9531249447618526e-12)
    cross_up = noise(splits[10], (CROSS, RANK, D_IN), RANK ** -0.5, 0.25, ((1, 8),), jnp.float32)
    up_first = noise(splits[11], (CROSS, RANK, D_IN), (0.000111 * SAMPLES ** -0.5), 4.76837158203125e-06, ((1, 8),), jnp.float32)
    up_second = jnp.clip(jnp.exp(math.log(4.882812361904632e-13) - 2.7725887 * jax.random.uniform(splits[12], (CROSS, RANK, D_IN), jnp.float32) ** level_of(splits[12], (CROSS, RANK, D_IN), ((1, 8),), -0.2, 0.2)), 3.051757726190395e-14, 4.882812361904632e-13)
    hidden_one = noise(splits[13], (D_IN, H1), D_IN ** -0.5, 0.109375, ((0, 8),), jnp.float32)
    one_first = noise(splits[14], (D_IN, H1), (0.00078 * SAMPLES ** -0.5), 3.814697265625e-05, ((0, 8),), jnp.float32)
    one_second = jnp.clip(jnp.exp(math.log(2.380371073862353e-11) - 2.7674736 * jax.random.uniform(splits[15], (D_IN, H1), jnp.float32) ** level_of(splits[15], (D_IN, H1), ((0, 8),), -0.2, 0.2)), 1.4953613434315338e-12, 2.380371073862353e-11)
    hidden_two = noise(splits[16], (H1, H2), H1 ** -0.5, 0.1875, ((0, 8),), jnp.float32)
    two_first = noise(splits[17], (H1, H2), (0.0005 * SAMPLES ** -0.5), 2.288818359375e-05, ((0, 8),), jnp.float32)
    two_second = jnp.clip(jnp.exp(math.log(9.765624940649698e-12) - 2.7725887 * jax.random.uniform(splits[18], (H1, H2), jnp.float32) ** level_of(splits[18], (H1, H2), ((0, 8),), -0.2, 0.2)), 6.103515587906061e-13, 9.765624940649698e-12)
    hidden_three = noise(splits[19], (H2, H3), H2 ** -0.5, 0.1875, ((0, 8),), jnp.float32)
    three_first = noise(splits[20], (H2, H3), (0.0013 * SAMPLES ** -0.5), 6.103515625e-05, ((0, 8),), jnp.float32)
    three_second = jnp.clip(jnp.exp(math.log(7.01904298572309e-11) - 2.7708511 * jax.random.uniform(splits[21], (H2, H3), jnp.float32) ** level_of(splits[21], (H2, H3), ((0, 8),), -0.2, 0.2)), 4.394531179924277e-12, 7.01904298572309e-11)
    smalls = noise(splits[22], (SMALL,), 0.1, 0.625, (), jnp.float32)
    small_first = draw_small_first(jax.random.fold_in(splits[25], 71), 0)
    small_second = draw_small_second(jax.random.fold_in(splits[25], 71), 0)
    return dict(row_ids=row_ids, bag_counts=bag_counts, labels=labels, dense_input=dense_input, tables=tables, table_first=table_first, table_second=table_second, cross_down=cross_down, down_first=down_first, down_second=down_second, cross_up=cross_up, up_first=up_first, up_second=up_second, hidden_one=hidden_one, one_first=one_first, one_second=one_second, hidden_two=hidden_two, two_first=two_first, two_second=two_second, hidden_three=hidden_three, three_first=three_first, three_second=three_second, smalls=smalls, small_first=small_first, small_second=small_second)


BETA_ONE = 0.9
BETA_TWO = 0.999
EPSILON = 1e-12
DECAY = 0.01
HIGH = lax.Precision.HIGHEST

@jax.custom_vjp
def low(v):
    return lax.optimization_barrier(v.astype(jnp.bfloat16)).astype(jnp.float32)

@jax.custom_vjp
def low_back(v):
    return v

def low_keep(v):
    return (low(v), None)

def low_pass(kept, grad):
    return (grad,)

def back_keep(v):
    return (v, None)

def back_low(kept, grad):
    return (low(grad),)
low.defvjp(low_keep, low_pass)
low_back.defvjp(back_keep, back_low)

def matmul(left, right):
    return jnp.dot(left, right, precision=HIGH, preferred_element_type=jnp.float32)

def split_smalls(smalls):
    extents = [CROSS * D_IN, H1, H2, H3, H3, 1]
    pieces = []
    offset = 0
    for extent in extents:
        pieces.append(smalls[offset:offset + extent])
        offset = offset + extent
    return (pieces[0].reshape(CROSS, D_IN), pieces[1], pieces[2], pieces[3], pieces[4], pieces[5])

def pool(tables, row_ids, bag_counts):
    slots = lax.broadcasted_iota(jnp.int32, row_ids.shape, 2)
    feature = lax.broadcasted_iota(jnp.int32, row_ids.shape, 1)
    valid = slots < bag_counts[:, :, None]
    picked = tables[feature, row_ids]
    summed = lax.optimization_barrier(jnp.sum(jnp.where(valid[..., None], picked, 0.0), axis=2))
    return low_back(summed) / bag_counts[:, :, None].astype(jnp.float32)

def block_loss(lowered, smalls, row_ids, bag_counts, labels, dense_input):
    tables, cross_down, cross_up, hidden_one, hidden_two, hidden_three = lowered
    cross_bias, bias_one, bias_two, bias_three, head_weight, head_bias = split_smalls(smalls)
    samples = row_ids.shape[0]
    pooled = pool(tables, row_ids, bag_counts)
    anchor = jnp.concatenate([pooled.reshape(samples, FEATURES * EMB), dense_input], axis=1)
    stream = anchor
    for layer_index in range(CROSS):
        narrow = low(low_back(matmul(low(stream), cross_down[layer_index])))
        factor = low_back(matmul(narrow, cross_up[layer_index]) + cross_bias[layer_index])
        stream = anchor * factor + stream
    pre_one = low_back(matmul(low(stream), hidden_one) + bias_one)
    pre_two = low_back(matmul(low(jax.nn.silu(pre_one)), hidden_two) + bias_two)
    pre_three = low_back(matmul(low(jax.nn.silu(pre_two)), hidden_three) + bias_three)
    top = jax.nn.silu(pre_three)
    logit = matmul(top, head_weight) + head_bias[0]
    target = labels.astype(jnp.float32)
    return jnp.sum(jax.nn.softplus(logit) - target * logit)

def adamw(weight, grad, first, second, rate):
    first = BETA_ONE * first + (1.0 - BETA_ONE) * grad
    second = BETA_TWO * second + (1.0 - BETA_TWO) * grad * grad
    corr_one = 1.0 - BETA_ONE ** STEP
    corr_two = 1.0 - BETA_TWO ** STEP
    moved = first / corr_one / (jnp.sqrt(second / corr_two) + EPSILON) + DECAY * weight
    return (weight - rate * moved, first, second)

def reference(row_ids, bag_counts, labels, dense_input, tables, table_first, table_second, cross_down, down_first, down_second, cross_up, up_first, up_second, hidden_one, one_first, one_second, hidden_two, two_first, two_second, hidden_three, three_first, three_second, smalls, small_first, small_second):
    block = math.gcd(SAMPLES, 512)
    blocks = SAMPLES // block
    data = (row_ids.reshape(blocks, block, FEATURES, BAG), bag_counts.reshape(blocks, block, FEATURES), labels.reshape(blocks, block), dense_input.reshape(blocks, block, DENSE))
    masters = (tables, cross_down, cross_up, hidden_one, hidden_two, hidden_three, smalls)

    def objective(weights):
        lowered = tuple((low(item) for item in weights[:6]))

        def add_block(total, item):
            part = jax.checkpoint(block_loss)(lowered, weights[6], item[0], item[1], item[2], item[3])
            return (total + part, None)
        total, unused = lax.scan(add_block, jnp.zeros((), jnp.float32), data)
        return total
    loss_sum, pull = jax.vjp(objective, masters)
    grads = pull(jnp.ones((), jnp.float32) / SAMPLES)[0]
    firsts = (table_first, down_first, up_first, one_first, two_first, three_first, small_first)
    seconds = (table_second, down_second, up_second, one_second, two_second, three_second, small_second)
    rates = (1.0, D_IN ** (-0.5), RANK ** (-0.5), D_IN ** (-0.5), H1 ** (-0.5), H2 ** (-0.5), 0.1)
    results = [loss_sum]
    for index in range(7):
        results.extend(adamw(masters[index], grads[index], firsts[index], seconds[index], rates[index]))
    return (results[0], results[1], results[2], results[3], results[4], results[5], results[6], results[7], results[8], results[9], results[10], results[11], results[12], results[13], results[14], results[15], results[16], results[17], results[18], results[19], results[20], results[21])
```

```python
import jax
import jax.numpy as jnp
from jax import lax
from jax.experimental import pallas as pl
from jax.experimental.pallas import tpu as pltpu
from jax.sharding import PartitionSpec as P

D_IN = 3456
RANK = 512
CROSS = 3
H1 = 1024
H2 = 1024
H3 = 512
STEP = 10
GROUP = 8
SLOTS = 32
LOW = 128


BETA_ONE = 0.9
BETA_TWO = 0.999
EPSILON = 1e-12
DECAY = 0.01
HIGH = lax.Precision.HIGHEST


def split_smalls(smalls):
    extents = [CROSS * D_IN, H1, H2, H3, H3, 1]
    pieces = []
    offset = 0
    for extent in extents:
        pieces.append(smalls[offset : offset + extent])
        offset = offset + extent
    return (pieces[0].reshape(CROSS, D_IN), pieces[1], pieces[2], pieces[3], pieces[4], pieces[5])


def product(left, right):
    return jnp.dot(left, right, preferred_element_type=jnp.float32)


def left_product(left, right):
    return lax.dot_general(
        left, right, (((0,), (0,)), ((), ())), preferred_element_type=jnp.float32
    )


def right_product(left, right):
    return lax.dot_general(
        left, right, (((1,), (1,)), ((), ())), preferred_element_type=jnp.float32
    )


def silu_slope(value):
    logistic = jax.nn.sigmoid(value)
    return logistic * (1.0 + value * (1.0 - logistic))


def slot_ids(row_ids, bag_counts):
    samples, features, slots = row_ids.shape
    live = lax.broadcasted_iota(jnp.int32, row_ids.shape, 2) < bag_counts[:, :, None]
    ids = jnp.pad(jnp.where(live, row_ids, -1), ((0, 0), (0, 0), (0, SLOTS - slots)), constant_values=-1)
    return ids.transpose(1, 0, 2).reshape(features, samples // GROUP, GROUP * SLOTS)


def one_hot(codes, levels):
    rows = jnp.broadcast_to(codes, (16, codes.shape[1])).astype(jnp.bfloat16)
    wanted = lax.broadcasted_iota(jnp.int32, (levels, codes.shape[1]), 0).astype(jnp.float32).astype(jnp.bfloat16)
    hits = jnp.concatenate([rows] * (levels // 16), axis=0) == wanted
    return jnp.where(hits, jnp.ones((), jnp.bfloat16), jnp.zeros((), jnp.bfloat16)).astype(jnp.float8_e4m3fn)


def pool_kernel(ids_ref, table_ref, counts_ref, dense_ref, anchor_ref, hits_ref, code_ref):
    feature = pl.program_id(0)
    features = pl.num_programs(0) - 1
    samples = hits_ref.shape[1]
    highs = hits_ref.shape[2] // LOW

    @pl.when(feature < features)
    def _():
        ids = ids_ref[0]
        member = lax.broadcasted_iota(jnp.int32, ids.shape, 1) // SLOTS
        code_ref[0] = ((ids >> 7) * GROUP + member).astype(jnp.float32)
        code_ref[1] = (ids & (LOW - 1)).astype(jnp.float32)

        def add_groups(step, unused):
            first = pl.multiple_of(step * 8, 8)
            high_codes = code_ref[0, pl.ds(first, 8), :]
            low_codes = code_ref[1, pl.ds(first, 8), :]
            for pair in range(4):
                products = []
                for row in (2 * pair, 2 * pair + 1):
                    high_hits = one_hot(high_codes[row : row + 1], highs * GROUP)
                    low_hits = one_hot(low_codes[row : row + 1], LOW)
                    products.append(right_product(high_hits, low_hits))
                start = pl.multiple_of(step * 8 * GROUP + pair * 2 * GROUP, 2 * GROUP)
                for high in range(highs):
                    part = slice(high * GROUP, (high + 1) * GROUP)
                    tile = jnp.concatenate([products[0][part], products[1][part]], axis=0)
                    hits_ref[0, pl.ds(start, 2 * GROUP), high * LOW : (high + 1) * LOW] = tile.astype(
                        jnp.bfloat16
                    )
            return unused

        lax.fori_loop(0, samples // (8 * GROUP), add_groups, 0)
        summed = product(hits_ref[0], table_ref[0])
        lanes = lax.broadcasted_iota(jnp.int32, counts_ref.shape, 1)
        counts = jnp.sum(jnp.where(lanes == feature, counts_ref[...], 0.0), axis=1, keepdims=True)
        anchor_ref[...] = summed / counts

    @pl.when(feature == features)
    def _():
        anchor_ref[...] = dense_ref[...]


def pool(ids, whole_table, count_float, dense_input):
    features, rows, width = whole_table.shape
    samples = count_float.shape[0]
    last = features - 1
    return pl.pallas_call(
        pool_kernel,
        grid=(features + 1,),
        in_specs=[
            pl.BlockSpec((1,) + ids.shape[1:], lambda f: (jnp.minimum(f, last), 0, 0)),
            pl.BlockSpec((1, rows, width), lambda f: (jnp.minimum(f, last), 0, 0)),
            pl.BlockSpec((samples, features), lambda f: (0, 0)),
            pl.BlockSpec((samples, width), lambda f: (0, 0)),
        ],
        out_specs=[
            pl.BlockSpec((samples, width), lambda f: (0, f)),
            pl.BlockSpec((1, samples, rows), lambda f: (jnp.minimum(f, last), 0, 0)),
        ],
        out_shape=[
            jax.ShapeDtypeStruct((samples, (features + 1) * width), jnp.float32),
            jax.ShapeDtypeStruct((features, samples, rows), jnp.bfloat16),
        ],
        scratch_shapes=[pltpu.VMEM((2,) + ids.shape[1:], jnp.float32)],
        compiler_params=pltpu.CompilerParams(vmem_limit_bytes=48 * 2**20),
        cost_estimate=pl.CostEstimate(
            flops=6 * samples * features * rows * width,
            bytes_accessed=2 * features * rows * (samples + width) + 4 * samples * features * (width + SLOTS),
            transcendentals=0,
        ),
    )(ids, whole_table, count_float, dense_input)


def cross_forward(anchor, stream, down, upward, bias):
    low_stream = stream.astype(jnp.bfloat16)
    narrow = product(low_stream, down).astype(jnp.bfloat16)
    factor = product(narrow, upward) + bias
    return (anchor * factor + stream, (low_stream, narrow, factor))


def cross_backward(anchor, saved, down, upward, grad_next):
    low_stream, narrow, factor = saved
    grad_factor = (anchor * grad_next).astype(jnp.bfloat16)
    grad_bias = jnp.sum(grad_factor.astype(jnp.float32), axis=0)
    grad_up = left_product(narrow, grad_factor)
    grad_narrow = right_product(grad_factor, upward).astype(jnp.bfloat16)
    grad_down = left_product(low_stream, grad_narrow)
    grad_stream = grad_next + right_product(grad_narrow, down)
    return (grad_stream, factor * grad_next, grad_down, grad_up, grad_bias)


def dense_backward(inputs, pre, grad_out, weight):
    grad_pre = (grad_out * silu_slope(pre)).astype(jnp.bfloat16)
    grad_weight = left_product(inputs, grad_pre)
    grad_bias = jnp.sum(grad_pre.astype(jnp.float32), axis=0)
    return (grad_weight, grad_bias, right_product(grad_pre, weight))


def adamw(weight, grad, first, second, rate):
    first = BETA_ONE * first + (1.0 - BETA_ONE) * grad
    second = BETA_TWO * second + (1.0 - BETA_TWO) * grad * grad
    corr_one = 1.0 - BETA_ONE**STEP
    corr_two = 1.0 - BETA_TWO**STEP
    moved = first / corr_one / (jnp.sqrt(second / corr_two) + EPSILON) + DECAY * weight
    return (weight - rate * moved, first, second)


def on_device(
    row_ids,
    bag_counts,
    labels,
    dense_input,
    tables,
    table_first,
    table_second,
    cross_down,
    down_first,
    down_second,
    cross_up,
    up_first,
    up_second,
    hidden_one,
    one_first,
    one_second,
    hidden_two,
    two_first,
    two_second,
    hidden_three,
    three_first,
    three_second,
    smalls,
    small_first,
    small_second,
):
    down_all, up_all, one_all, two_all, three_all = (
        lax.all_gather(cross_down.astype(jnp.bfloat16), "rep", axis=1, tiled=True),
        lax.all_gather(cross_up.astype(jnp.bfloat16), "rep", axis=1, tiled=True),
        lax.all_gather(hidden_one.astype(jnp.bfloat16), "rep", axis=0, tiled=True),
        lax.all_gather(hidden_two.astype(jnp.bfloat16), "rep", axis=0, tiled=True),
        lax.all_gather(hidden_three.astype(jnp.bfloat16), "rep", axis=0, tiled=True),
    )
    cross_bias, bias_one, bias_two, bias_three, head_weight, head_bias = split_smalls(smalls)
    group = lax.axis_size("grp")
    samples = row_ids.shape[0]
    repeats = lax.axis_size("rep")
    features, extent, width = tables.shape
    part = extent // repeats
    own_part = lax.dynamic_slice_in_dim(tables, lax.axis_index("rep") * part, part, axis=1)
    whole_table = lax.all_gather(own_part.astype(jnp.bfloat16), ("grp", "rep"), axis=1, tiled=True)
    count_float = bag_counts.astype(jnp.float32)
    anchor, hits = pool(slot_ids(row_ids, bag_counts), whole_table, count_float, dense_input)
    stream = anchor
    kept = []
    for layer_index in range(CROSS):
        stream, saved = cross_forward(
            anchor, stream, down_all[layer_index], up_all[layer_index], cross_bias[layer_index]
        )
        kept.append(saved)
    in_one = stream.astype(jnp.bfloat16)
    pre_one = product(in_one, one_all) + bias_one
    in_two = jax.nn.silu(pre_one).astype(jnp.bfloat16)
    pre_two = product(in_two, two_all) + bias_two
    in_three = jax.nn.silu(pre_two).astype(jnp.bfloat16)
    pre_three = product(in_three, three_all) + bias_three
    top = jax.nn.silu(pre_three)
    logit = jnp.dot(top, head_weight, precision=HIGH) + head_bias[0]
    target = labels.astype(jnp.float32)
    loss_local = jnp.sum(jax.nn.softplus(logit) - target * logit)
    total_samples = samples * lax.axis_size("rep") * group
    grad_logit = (jax.nn.sigmoid(logit) - target) / total_samples
    grad_head = jnp.dot(grad_logit, top, precision=HIGH)
    grad_head_bias = jnp.sum(grad_logit, keepdims=True)
    grad_top = grad_logit[:, None] * head_weight[None, :]
    grad_three, bias_grad_three, grad_in = dense_backward(in_three, pre_three, grad_top, three_all)
    grad_two, bias_grad_two, grad_in = dense_backward(in_two, pre_two, grad_in, two_all)
    grad_one, bias_grad_one, grad_stream = dense_backward(in_one, pre_one, grad_in, one_all)
    grad_anchor = jnp.zeros_like(anchor)
    down_grads = []
    up_grads = []
    bias_grads = []
    for layer_index in reversed(range(CROSS)):
        grad_stream, anchor_part, grad_down, grad_up, grad_bias = cross_backward(
            anchor, kept[layer_index], down_all[layer_index], up_all[layer_index], grad_stream
        )
        grad_anchor = grad_anchor + anchor_part
        down_grads.insert(0, grad_down)
        up_grads.insert(0, grad_up)
        bias_grads.insert(0, grad_bias)
    grad_anchor = grad_anchor + grad_stream
    grad_summed = (
        grad_anchor[:, : features * width].reshape(samples, features, width) / count_float[:, :, None]
    ).astype(jnp.bfloat16)
    row_grad = jnp.einsum("fsr,sfe->fre", hits, grad_summed, preferred_element_type=jnp.float32)
    row_share = row_grad.astype(jnp.bfloat16).reshape(features, group, repeats, part, width)
    row_share = row_share.transpose(2, 1, 0, 3, 4)
    row_share = lax.psum_scatter(row_share, "rep", scatter_dimension=0, tiled=True)[0]
    row_share = lax.psum_scatter(row_share, "grp", scatter_dimension=0, tiled=True)[0]
    table_grad = lax.all_gather(row_share, "rep", axis=1, tiled=True).astype(jnp.float32)
    stack_down = jnp.stack(down_grads)
    stack_up = jnp.stack(up_grads)
    share_down, share_up, share_one, share_two, share_three = (
        lax.psum_scatter(
            stack_down.astype(jnp.bfloat16), "rep", scatter_dimension=1, tiled=True
        ).astype(jnp.float32),
        lax.psum_scatter(
            stack_up.astype(jnp.bfloat16), "rep", scatter_dimension=1, tiled=True
        ).astype(jnp.float32),
        lax.psum_scatter(
            grad_one.astype(jnp.bfloat16), "rep", scatter_dimension=0, tiled=True
        ).astype(jnp.float32),
        lax.psum_scatter(
            grad_two.astype(jnp.bfloat16), "rep", scatter_dimension=0, tiled=True
        ).astype(jnp.float32),
        lax.psum_scatter(
            grad_three.astype(jnp.bfloat16), "rep", scatter_dimension=0, tiled=True
        ).astype(jnp.float32),
    )
    share_down, share_up, share_one, share_two, share_three = (
        lax.psum(share_down.astype(jnp.bfloat16), "grp").astype(jnp.float32),
        lax.psum(share_up.astype(jnp.bfloat16), "grp").astype(jnp.float32),
        lax.psum(share_one.astype(jnp.bfloat16), "grp").astype(jnp.float32),
        lax.psum(share_two.astype(jnp.bfloat16), "grp").astype(jnp.float32),
        lax.psum(share_three.astype(jnp.bfloat16), "grp").astype(jnp.float32),
    )
    small_grad = jnp.concatenate(
        [
            jnp.stack(bias_grads).reshape(-1),
            bias_grad_one,
            bias_grad_two,
            bias_grad_three,
            grad_head,
            grad_head_bias,
        ]
    )
    small_sum, loss_sum = lax.psum((small_grad, loss_local), ("rep", "grp"))
    new_tables, new_table_first, new_table_second = adamw(
        tables, table_grad, table_first, table_second, 1.0
    )
    new_down, new_down_first, new_down_second = adamw(
        cross_down, share_down, down_first, down_second, D_IN ** (-0.5)
    )
    new_up, new_up_first, new_up_second = adamw(
        cross_up, share_up, up_first, up_second, RANK ** (-0.5)
    )
    new_one, new_one_first, new_one_second = adamw(
        hidden_one, share_one, one_first, one_second, D_IN ** (-0.5)
    )
    new_two, new_two_first, new_two_second = adamw(
        hidden_two, share_two, two_first, two_second, H1 ** (-0.5)
    )
    new_three, new_three_first, new_three_second = adamw(
        hidden_three, share_three, three_first, three_second, H2 ** (-0.5)
    )
    new_smalls, new_small_first, new_small_second = adamw(
        smalls, small_sum, small_first, small_second, 0.1
    )
    return (
        loss_sum,
        new_tables,
        new_table_first,
        new_table_second,
        new_down,
        new_down_first,
        new_down_second,
        new_up,
        new_up_first,
        new_up_second,
        new_one,
        new_one_first,
        new_one_second,
        new_two,
        new_two_first,
        new_two_second,
        new_three,
        new_three_first,
        new_three_second,
        new_smalls,
        new_small_first,
        new_small_second,
    )


def solution(mesh):
    return jax.shard_map(
        on_device,
        mesh=mesh,
        in_specs=(
            P(("rep", "grp"), None, None),
            P(("rep", "grp"), None),
            P(("rep", "grp")),
            P(("rep", "grp"), None),
            P(None, "grp", None),
            P(None, "grp", None),
            P(None, "grp", None),
            P(None, "rep", None),
            P(None, "rep", None),
            P(None, "rep", None),
            P(None, "rep", None),
            P(None, "rep", None),
            P(None, "rep", None),
            P("rep", None),
            P("rep", None),
            P("rep", None),
            P("rep", None),
            P("rep", None),
            P("rep", None),
            P("rep", None),
            P("rep", None),
            P("rep", None),
            P(),
            P(),
            P(),
        ),
        out_specs=(
            P(),
            P(None, "grp", None),
            P(None, "grp", None),
            P(None, "grp", None),
            P(None, "rep", None),
            P(None, "rep", None),
            P(None, "rep", None),
            P(None, "rep", None),
            P(None, "rep", None),
            P(None, "rep", None),
            P("rep", None),
            P("rep", None),
            P("rep", None),
            P("rep", None),
            P("rep", None),
            P("rep", None),
            P("rep", None),
            P("rep", None),
            P("rep", None),
            P(),
            P(),
            P(),
        ),
        check_vma=False,
    )
```

```python
import functools

import jax
import jax.numpy as jnp
from jax import lax
from jax.experimental import pallas as pl
from jax.experimental.pallas import tpu as pltpu
from jax.sharding import PartitionSpec as P

D_IN = 3456
RANK = 512
CROSS = 3
H1 = 1024
H2 = 1024
H3 = 512
STEP = 10
GROUP = 8
SLOTS = 32
LOW = 128
VMEM_BYTES = 60 * 2**20


BETA_ONE = 0.9
BETA_TWO = 0.999
EPSILON = 1e-12
DECAY = 0.01


def split_smalls(smalls):
    extents = [CROSS * D_IN, H1, H2, H3, H3, 1]
    pieces = []
    offset = 0
    for extent in extents:
        pieces.append(smalls[offset : offset + extent])
        offset = offset + extent
    return (pieces[0].reshape(CROSS, D_IN), pieces[1], pieces[2], pieces[3], pieces[4], pieces[5])


def product(left, right):
    return jnp.dot(left, right, preferred_element_type=jnp.float32)


def left_product(left, right):
    return lax.dot_general(
        left, right, (((0,), (0,)), ((), ())), preferred_element_type=jnp.float32
    )


def right_product(left, right):
    return lax.dot_general(
        left, right, (((1,), (1,)), ((), ())), preferred_element_type=jnp.float32
    )


def silu_slope(value):
    logistic = jax.nn.sigmoid(value)
    return logistic * (1.0 + value * (1.0 - logistic))


def slot_ids(row_ids, bag_counts):
    samples, features, slots = row_ids.shape
    live = lax.broadcasted_iota(jnp.int32, row_ids.shape, 2) < bag_counts[:, :, None]
    ids = jnp.pad(jnp.where(live, row_ids, -1), ((0, 0), (0, 0), (0, SLOTS - slots)), constant_values=-1)
    return ids.transpose(1, 0, 2).reshape(features, samples // GROUP, GROUP * SLOTS)


def one_hot(codes, levels):
    rows = jnp.broadcast_to(codes, (16, codes.shape[1])).astype(jnp.bfloat16)
    wanted = lax.broadcasted_iota(jnp.int32, (levels, codes.shape[1]), 0).astype(jnp.float32).astype(jnp.bfloat16)
    hits = jnp.concatenate([rows] * (levels // 16), axis=0) == wanted
    return jnp.where(hits, jnp.ones((), jnp.bfloat16), jnp.zeros((), jnp.bfloat16)).astype(jnp.float8_e4m3fn)


def count_kernel(earlier, ids_ref, *refs):
    hits_ref, code_ref = refs[earlier:]
    samples = hits_ref.shape[1]
    highs = hits_ref.shape[2] // LOW
    ids = ids_ref[0]
    member = lax.broadcasted_iota(jnp.int32, ids.shape, 1) // SLOTS
    code_ref[0] = ((ids >> 7) * GROUP + member).astype(jnp.float32)
    code_ref[1] = (ids & (LOW - 1)).astype(jnp.float32)

    def add_groups(step, unused):
        first = pl.multiple_of(step * 8, 8)
        high_codes = code_ref[0, pl.ds(first, 8), :]
        low_codes = code_ref[1, pl.ds(first, 8), :]
        for pair in range(4):
            products = []
            for row in (2 * pair, 2 * pair + 1):
                high_hits = one_hot(high_codes[row : row + 1], highs * GROUP)
                low_hits = one_hot(low_codes[row : row + 1], LOW)
                products.append(right_product(high_hits, low_hits))
            start = pl.multiple_of(step * 8 * GROUP + pair * 2 * GROUP, 2 * GROUP)
            for high in range(highs):
                part = slice(high * GROUP, (high + 1) * GROUP)
                tile = jnp.concatenate([products[0][part], products[1][part]], axis=0)
                hits_ref[0, pl.ds(start, 2 * GROUP), high * LOW : (high + 1) * LOW] = tile.astype(
                    jnp.bfloat16
                )
        return unused

    lax.fori_loop(0, samples // (8 * GROUP), add_groups, 0)


def count(ids, rows, pieces):
    features, groups, slots = ids.shape
    samples = groups * GROUP
    cuts = [features * piece // pieces for piece in range(pieces + 1)]
    hits = None
    for first, last in zip(cuts[:-1], cuts[1:]):
        earlier = [] if hits is None else [hits]
        hits = pl.pallas_call(
            functools.partial(count_kernel, len(earlier)),
            grid=(last - first,),
            in_specs=[pl.BlockSpec((1, groups, slots), functools.partial(shifted_block, first))]
            + [pl.BlockSpec(memory_space=pl.ANY)] * len(earlier),
            out_specs=pl.BlockSpec((1, samples, rows), functools.partial(shifted_block, first)),
            out_shape=jax.ShapeDtypeStruct((features, samples, rows), jnp.bfloat16),
            input_output_aliases={1: 0} if earlier else {},
            scratch_shapes=[pltpu.VMEM((2, groups, slots), jnp.float32)],
            compiler_params=pltpu.CompilerParams(vmem_limit_bytes=VMEM_BYTES),
            cost_estimate=pl.CostEstimate(
                flops=(last - first) * samples * rows * 2048,
                bytes_accessed=2 * (last - first) * rows * samples,
                transcendentals=0,
            ),
        )(ids, *earlier)
    return hits


def shifted_block(first, feature):
    return (feature + first, 0, 0)


def feature_counts(counts_ref, feature):
    lanes = lax.broadcasted_iota(jnp.int32, counts_ref.shape, 1)
    return jnp.sum(jnp.where(lanes == feature, counts_ref[...], 0.0), axis=1, keepdims=True)


def pool_kernel(
    place_ref, hits_ref, own_a, other_a, own_b, other_b, counts_ref, dense_ref, anchor_ref, table_ref, *, keys, half
):
    feature = pl.program_id(0)
    features = pl.num_programs(0) - 1
    mine = place_ref[0]
    member = place_ref[1]
    group = table_ref.shape[0]

    def assemble(own_ref, other_ref, order):
        for position, key in enumerate(order):
            for step in range(group):
                row = lax.rem(member + group - step, group)
                table_ref[row, mine ^ key] = own_ref[position, step, 0]
                table_ref[row, mine ^ (key ^ 1)] = other_ref[position, step, 0]

    @pl.when(feature < half)
    def _():
        assemble(own_a, other_a, keys[0])

    @pl.when((feature >= half) & (feature < features))
    def _():
        assemble(own_b, other_b, keys[1])

    @pl.when(feature < features)
    def _():
        table = table_ref[...].reshape(-1, table_ref.shape[-1])
        anchor_ref[...] = product(hits_ref[0], table) / feature_counts(counts_ref, feature)

    @pl.when(feature == features)
    def _():
        anchor_ref[...] = dense_ref[...]


def pool(hits, first_half, second_half, keys, count_float, dense_input):
    features, samples, rows = hits.shape
    last = features - 1
    half = first_half[0].shape[2]
    halves, group, unused, part, width = first_half[0].shape
    block = (halves, group, 1, part, width)
    low_block = pl.BlockSpec(block, lambda f, place: (0, 0, jnp.minimum(f, half - 1), 0, 0))
    high_block = pl.BlockSpec(block, lambda f, place: (0, 0, jnp.clip(f - half, 0, last - half), 0, 0))
    place = jnp.stack([lax.axis_index("rep"), lax.axis_index("grp")]).astype(jnp.int32)
    return pl.pallas_call(
        functools.partial(pool_kernel, keys=keys, half=half),
        grid_spec=pltpu.PrefetchScalarGridSpec(
            num_scalar_prefetch=1,
            grid=(features + 1,),
            in_specs=[
                pl.BlockSpec((1, samples, rows), lambda f, place: (jnp.minimum(f, last), 0, 0)),
                low_block,
                low_block,
                high_block,
                high_block,
                pl.BlockSpec((samples, features), lambda f, place: (0, 0)),
                pl.BlockSpec((samples, width), lambda f, place: (0, 0)),
            ],
            out_specs=pl.BlockSpec((samples, width), lambda f, place: (0, f)),
            scratch_shapes=[pltpu.VMEM((group, 2 * halves, part, width), jnp.bfloat16)],
        ),
        out_shape=jax.ShapeDtypeStruct((samples, (features + 1) * width), jnp.float32),
        compiler_params=pltpu.CompilerParams(vmem_limit_bytes=VMEM_BYTES),
        cost_estimate=pl.CostEstimate(
            flops=2 * samples * features * rows * width,
            bytes_accessed=2 * features * rows * (samples + width) + 4 * samples * features * width,
            transcendentals=0,
        ),
    )(place, hits, *first_half, *second_half, count_float, dense_input)


def cross_forward_kernel(
    anchor_in, down_ref, up_ref, bias_ref, low_ref, narrow_ref, last_ref, anchor_ref, stream_ref, sum_ref
):
    layer, phase, block = pl.program_id(0), pl.program_id(1), pl.program_id(2)
    layers = pl.num_programs(0)

    @pl.when((layer == 0) & (phase == 0))
    def _():
        anchor_ref[block] = anchor_in[...]
        stream_ref[block] = anchor_in[...]

    @pl.when(phase == 0)
    def _():
        low = stream_ref[block].astype(jnp.bfloat16)
        low_ref[0] = low
        part = product(low, down_ref[0])

        @pl.when(block == 0)
        def _():
            sum_ref[...] = part

        @pl.when(block > 0)
        def _():
            sum_ref[...] += part

    @pl.when((phase == 1) & (block == 0))
    def _():
        narrow_ref[0] = sum_ref[...].astype(jnp.bfloat16)

    @pl.when(phase == 1)
    def _():
        factor = product(narrow_ref[0], up_ref[0]) + bias_ref[0]
        stream = anchor_ref[block] * factor + stream_ref[block]
        stream_ref[block] = stream

        @pl.when(layer == layers - 1)
        def _():
            last_ref[...] = stream.astype(jnp.bfloat16)


def cross_forward(anchor, down, up, bias):
    samples, width = anchor.shape
    layers, unused, rank = down.shape
    blocks = 3
    piece = width // blocks
    final = blocks - 1
    return pl.pallas_call(
        cross_forward_kernel,
        grid=(layers, 2, blocks),
        in_specs=[
            pl.BlockSpec((samples, piece), lambda l, p, j: (0, jnp.where((l == 0) & (p == 0), j, final))),
            pl.BlockSpec((1, piece, rank), lambda l, p, j: (l, jnp.where(p == 0, j, final), 0)),
            pl.BlockSpec((1, rank, piece), lambda l, p, j: (l, 0, jnp.where(p == 1, j, 0))),
            pl.BlockSpec((1, 1, piece), lambda l, p, j: (l, 0, jnp.where(p == 1, j, 0))),
        ],
        out_specs=[
            pl.BlockSpec((1, samples, piece), lambda l, p, j: (l, 0, jnp.where(p == 0, j, final))),
            pl.BlockSpec((1, samples, rank), lambda l, p, j: (l, 0, 0)),
            pl.BlockSpec((samples, piece), lambda l, p, j: (0, jnp.where((l == layers - 1) & (p == 1), j, 0))),
        ],
        out_shape=[
            jax.ShapeDtypeStruct((layers, samples, width), jnp.bfloat16),
            jax.ShapeDtypeStruct((layers, samples, rank), jnp.bfloat16),
            jax.ShapeDtypeStruct((samples, width), jnp.bfloat16),
        ],
        scratch_shapes=[
            pltpu.VMEM((blocks, samples, piece), jnp.float32),
            pltpu.VMEM((blocks, samples, piece), jnp.float32),
            pltpu.VMEM((samples, rank), jnp.float32),
        ],
        compiler_params=pltpu.CompilerParams(vmem_limit_bytes=VMEM_BYTES),
        cost_estimate=pl.CostEstimate(
            flops=4 * layers * samples * width * rank,
            bytes_accessed=4 * layers * width * (rank + samples) + 4 * samples * width,
            transcendentals=0,
        ),
    )(anchor, down, up, bias.reshape(layers, 1, width))


def head_kernel(
    input_ref,
    one_ref,
    late_ref,
    bias_one,
    bias_two,
    bias_three,
    head_ref,
    head_bias,
    target_ref,
    loss_ref,
    grad_head,
    grad_head_bias,
    grad_bias_one,
    grad_bias_two,
    grad_bias_three,
    grad_one,
    grad_late,
    grad_stream,
    sum_ref,
    back_ref,
    *,
    total
):
    step = pl.program_id(0)
    blocks = pl.num_programs(0) // 2

    @pl.when(step < blocks)
    def _():
        part = product(input_ref[...], one_ref[...])

        @pl.when(step == 0)
        def _():
            sum_ref[...] = part

        @pl.when(step > 0)
        def _():
            sum_ref[...] += part

    @pl.when(step == blocks)
    def _():
        pre_one = sum_ref[...] + bias_one[...]
        in_two = jax.nn.silu(pre_one).astype(jnp.bfloat16)
        two = late_ref[:, :H2]
        three = late_ref[:, H2:]
        pre_two = product(in_two, two) + bias_two[...]
        in_three = jax.nn.silu(pre_two).astype(jnp.bfloat16)
        pre_three = product(in_three, three) + bias_three[...]
        top = jax.nn.silu(pre_three)
        head = head_ref[...]
        target = target_ref[...]
        logit = jnp.sum(top * head, axis=1, keepdims=True) + head_bias[...]
        losses = jnp.maximum(logit, 0.0) + jnp.log1p(jnp.exp(-jnp.abs(logit))) - target * logit
        loss_ref[...] = jnp.sum(losses, axis=0, keepdims=True)
        grad_logit = (jax.nn.sigmoid(logit) - target) / total
        grad_head[...] = jnp.sum(grad_logit * top, axis=0, keepdims=True)
        grad_head_bias[...] = jnp.sum(grad_logit, axis=0, keepdims=True)
        back = (grad_logit * head * silu_slope(pre_three)).astype(jnp.bfloat16)
        grad_bias_three[...] = jnp.sum(back.astype(jnp.float32), axis=0, keepdims=True)
        grad_late[:, H2:] = left_product(in_three, back).astype(jnp.bfloat16)
        back = (right_product(back, three) * silu_slope(pre_two)).astype(jnp.bfloat16)
        grad_bias_two[...] = jnp.sum(back.astype(jnp.float32), axis=0, keepdims=True)
        grad_late[:, :H2] = left_product(in_two, back).astype(jnp.bfloat16)
        back = (right_product(back, two) * silu_slope(pre_one)).astype(jnp.bfloat16)
        grad_bias_one[...] = jnp.sum(back.astype(jnp.float32), axis=0, keepdims=True)
        back_ref[...] = back

    @pl.when(step >= blocks)
    def _():
        grad_one[...] = left_product(input_ref[...], back_ref[...]).astype(jnp.bfloat16)
        grad_stream[...] = right_product(back_ref[...], one_ref[...])


def head(inputs, one, late, biases, head_weight, head_bias, target, total):
    samples, width = inputs.shape
    blocks = 3
    piece = width // blocks

    def whole(shape):
        return pl.BlockSpec(shape, lambda s: (0,) * len(shape))

    rows = [bias.reshape(1, -1) for bias in biases] + [head_weight.reshape(1, -1), head_bias.reshape(1, 1)]
    small = [(1, 1), (1, H3), (1, 1), (1, H1), (1, H2), (1, H3)]
    return pl.pallas_call(
        functools.partial(head_kernel, total=total),
        grid=(2 * blocks,),
        in_specs=[
            pl.BlockSpec((samples, piece), lambda s: (0, lax.rem(s, blocks))),
            pl.BlockSpec((piece, H1), lambda s: (lax.rem(s, blocks), 0)),
            whole(late.shape),
        ]
        + [whole(row.shape) for row in rows]
        + [whole((samples, 1))],
        out_specs=[whole(shape) for shape in small]
        + [
            pl.BlockSpec((piece, H1), lambda s: (jnp.maximum(s - blocks, 0), 0)),
            whole(late.shape),
            pl.BlockSpec((samples, piece), lambda s: (0, jnp.maximum(s - blocks, 0))),
        ],
        out_shape=[jax.ShapeDtypeStruct(shape, jnp.float32) for shape in small]
        + [
            jax.ShapeDtypeStruct(one.shape, jnp.bfloat16),
            jax.ShapeDtypeStruct(late.shape, jnp.bfloat16),
            jax.ShapeDtypeStruct((samples, width), jnp.float32),
        ],
        scratch_shapes=[pltpu.VMEM((samples, H1), jnp.float32), pltpu.VMEM((samples, H1), jnp.bfloat16)],
        compiler_params=pltpu.CompilerParams(vmem_limit_bytes=VMEM_BYTES),
        cost_estimate=pl.CostEstimate(
            flops=6 * samples * (width * H1 + H1 * H2 + H2 * H3),
            bytes_accessed=6 * width * H1 + 8 * samples * width,
            transcendentals=8 * samples * (H1 + H2 + H3),
        ),
    )(inputs, one, late, *rows, target)


def cross_backward_kernel(
    core_ref,
    anchor_in,
    grad_in,
    low_ref,
    narrow_ref,
    down_ref,
    up_ref,
    bias_ref,
    counts_ref,
    send_ref,
    keep_ref,
    grad_down,
    grad_bias,
    grad_summed,
    anchor_ref,
    stream_ref,
    total_ref,
    sum_ref,
    back_ref,
    both_ref,
):
    layer, phase, block = pl.program_id(0), pl.program_id(1), pl.program_id(2)
    layers = pl.num_programs(0)

    @pl.when((layer == 0) & (phase == 0))
    def _():
        anchor_ref[block] = anchor_in[...]
        stream_ref[block] = grad_in[...]
        total_ref[block] = jnp.zeros(grad_in.shape, jnp.float32)

    @pl.when(phase == 0)
    def _():
        grad_next = stream_ref[block]
        grad_factor = (anchor_ref[block] * grad_next).astype(jnp.bfloat16)
        grad_bias[0] = jnp.sum(grad_factor.astype(jnp.float32), axis=0, keepdims=True)
        narrow = narrow_ref[0]
        both_ref[...] = left_product(narrow, grad_factor).astype(jnp.bfloat16).reshape(both_ref.shape)
        core = core_ref[0]
        send_ref[0] = both_ref[:, 1 - core]
        keep_ref[0] = both_ref[:, core]
        factor = product(narrow, up_ref[0]) + bias_ref[0]
        total_ref[block] += factor * grad_next
        part = right_product(grad_factor, up_ref[0])

        @pl.when(block == 0)
        def _():
            sum_ref[...] = part

        @pl.when(block > 0)
        def _():
            sum_ref[...] += part

    @pl.when((phase == 1) & (block == 0))
    def _():
        back_ref[...] = sum_ref[...].astype(jnp.bfloat16)

    @pl.when(phase == 1)
    def _():
        back = back_ref[...]
        grad_down[0] = left_product(low_ref[0], back).astype(jnp.bfloat16)
        grad_stream = stream_ref[block] + right_product(back, down_ref[0])
        stream_ref[block] = grad_stream

        @pl.when(layer == layers - 1)
        def _():
            features = grad_stream.shape[1] // LOW
            total = total_ref[block] + grad_stream
            for index in range(features):
                counts = jnp.maximum(feature_counts(counts_ref, block * features + index), 1.0)
                part = slice(index * LOW, (index + 1) * LOW)
                grad_summed[:, part] = (total[:, part] / counts).astype(jnp.bfloat16)


def cross_backward(anchor, grad_stream, lows, narrows, down, up, bias, count_float, core, repeats):
    samples, width = anchor.shape
    layers, unused, rank = down.shape
    blocks = 3
    piece = width // blocks
    final = blocks - 1
    share = rank // repeats

    def first_pass(l, p, j, core):
        return (0, jnp.where((l == 0) & (p == 0), j, final))

    def up_block(l, p, j, core):
        return (layers - 1 - l, 0, jnp.where(p == 0, j, final))

    def low_block(l, p, j, core):
        return (layers - 1 - l, 0, jnp.where(p == 1, j, 0))

    def down_block(l, p, j, core):
        return (layers - 1 - l, jnp.where(p == 1, j, 0), 0)

    half = jax.ShapeDtypeStruct((layers, repeats // 2, share, width), jnp.bfloat16)
    half_spec = pl.BlockSpec(
        (1, repeats // 2, share, piece),
        lambda l, p, j, core: (layers - 1 - l, 0, 0, jnp.where(p == 0, j, final)),
    )
    return pl.pallas_call(
        cross_backward_kernel,
        grid_spec=pltpu.PrefetchScalarGridSpec(
            num_scalar_prefetch=1,
            grid=(layers, 2, blocks),
            in_specs=[
                pl.BlockSpec((samples, piece), first_pass),
                pl.BlockSpec((samples, piece), first_pass),
                pl.BlockSpec((1, samples, piece), low_block),
                pl.BlockSpec((1, samples, rank), lambda l, p, j, core: (layers - 1 - l, 0, 0)),
                pl.BlockSpec((1, piece, rank), down_block),
                pl.BlockSpec((1, rank, piece), up_block),
                pl.BlockSpec((1, 1, piece), up_block),
                pl.BlockSpec(count_float.shape, lambda l, p, j, core: (0, 0)),
            ],
            out_specs=[
                half_spec,
                half_spec,
                pl.BlockSpec((1, piece, rank), down_block),
                pl.BlockSpec((1, 1, piece), up_block),
                pl.BlockSpec(
                    (samples, piece),
                    lambda l, p, j, core: (0, jnp.where((l == layers - 1) & (p == 1), j, 0)),
                ),
            ],
            scratch_shapes=[
                pltpu.VMEM((blocks, samples, piece), jnp.float32),
                pltpu.VMEM((blocks, samples, piece), jnp.float32),
                pltpu.VMEM((blocks, samples, piece), jnp.float32),
                pltpu.VMEM((samples, rank), jnp.float32),
                pltpu.VMEM((samples, rank), jnp.bfloat16),
                pltpu.VMEM((repeats // 2, 2, share, piece), jnp.bfloat16),
            ],
        ),
        out_shape=[
            half,
            half,
            jax.ShapeDtypeStruct(down.shape, jnp.bfloat16),
            jax.ShapeDtypeStruct((layers, 1, width), jnp.float32),
            jax.ShapeDtypeStruct((samples, width), jnp.bfloat16),
        ],
        compiler_params=pltpu.CompilerParams(vmem_limit_bytes=VMEM_BYTES),
        cost_estimate=pl.CostEstimate(
            flops=10 * layers * samples * width * rank,
            bytes_accessed=layers * width * (8 * rank + 2 * samples) + 10 * samples * width,
            transcendentals=0,
        ),
    )(core, anchor, grad_stream, lows, narrows, down, up, bias.reshape(layers, 1, width), count_float)


def row_kernel(core_ref, hits_ref, grad_ref, send_ref, keep_ref, both_ref):
    both_ref[...] = left_product(hits_ref[0], grad_ref[...]).astype(jnp.bfloat16).reshape(both_ref.shape)
    core = core_ref[0]
    send_ref[0] = both_ref[:, 1 - core]
    keep_ref[0] = both_ref[:, core]


def row_gradient(hits, grad_summed, first, features, group, core):
    unused, samples, rows = hits.shape
    half = rows // group // 2
    shape = jax.ShapeDtypeStruct((features, group, half, LOW), jnp.bfloat16)
    spec = pl.BlockSpec((1, group, half, LOW), lambda f, core: (f, 0, 0, 0))
    return pl.pallas_call(
        row_kernel,
        grid_spec=pltpu.PrefetchScalarGridSpec(
            num_scalar_prefetch=1,
            grid=(features,),
            in_specs=[
                pl.BlockSpec((1, samples, rows), lambda f, core: (f + first, 0, 0)),
                pl.BlockSpec((samples, LOW), lambda f, core: (0, f + first)),
            ],
            out_specs=[spec, spec],
            scratch_shapes=[pltpu.VMEM((group, 2, half, LOW), jnp.bfloat16)],
        ),
        out_shape=[shape, shape],
        compiler_params=pltpu.CompilerParams(vmem_limit_bytes=VMEM_BYTES),
        cost_estimate=pl.CostEstimate(
            flops=8 * samples * features * rows * LOW,
            bytes_accessed=2 * features * rows * (samples + LOW),
            transcendentals=0,
        ),
    )(core, hits, grad_summed)


def flip(value, bit):
    return lax.ppermute(value, "rep", [(i, i ^ bit) for i in range(lax.axis_size("rep"))])


def ring(value):
    size = lax.axis_size("grp")
    return lax.ppermute(value, "grp", [(i, (i + 1) % size) for i in range(size)])


def across():
    return [1 << i for i in range(1, lax.axis_size("rep").bit_length() - 1)]


def gather_across(value, order):
    keys = [0]
    for bit in order:
        value = jnp.concatenate([value, flip(value, bit)], axis=0)
        keys = keys + [key ^ bit for key in keys]
    return value, keys


def place(value, keys, axis, index_of):
    mine = lax.axis_index("rep")
    extent = value.shape[axis + 1]
    shape = list(value.shape[1:])
    shape[axis] = extent * len(keys)
    whole = jnp.zeros(shape, value.dtype)
    for position, key in enumerate(keys):
        whole = lax.dynamic_update_slice_in_dim(whole, value[position], index_of(mine ^ key) * extent, axis)
    return whole


def scatter_pair(keep, received, bits, order, axis):
    left = list(bits)
    for bit in order:
        position = axis + left.index(bit)
        mine = (lax.axis_index("rep") // bit) % 2
        send = lax.dynamic_index_in_dim(keep, 1 - mine, position, keepdims=False) + lax.dynamic_index_in_dim(
            received, 1 - mine, position, keepdims=False
        )
        keep = lax.dynamic_index_in_dim(keep, mine, position, keepdims=False) + lax.dynamic_index_in_dim(
            received, mine, position, keepdims=False
        )
        received = flip(send, bit)
        left.remove(bit)
    return keep + received


def ring_scatter(chunks):
    size = lax.axis_size("grp")
    mine = lax.axis_index("grp")
    value = lax.dynamic_index_in_dim(chunks, (mine + size - 1) % size, 0, keepdims=False)
    for step in range(1, size):
        own = lax.dynamic_index_in_dim(chunks, (mine + 2 * size - 1 - step) % size, 0, keepdims=False)
        value = own + ring(value)
    return value


def ring_gather(value):
    size = lax.axis_size("grp")
    mine = lax.axis_index("grp")
    whole = jnp.zeros((size,) + value.shape, value.dtype)
    for step in range(size):
        whole = lax.dynamic_update_index_in_dim(whole, value, (mine + size - step) % size, 0)
        if step < size - 1:
            value = ring(value)
    return whole


def sum_groups(shares):
    size = lax.axis_size("grp")
    flat = [share.reshape(size, -1, LOW) for share in shares]
    total = ring_gather(ring_scatter(jnp.concatenate(flat, axis=1)))
    results = []
    offset = 0
    for share, part in zip(shares, flat):
        piece = total[:, offset : offset + part.shape[1]]
        results.append(piece.reshape(share.shape).astype(jnp.float32))
        offset = offset + part.shape[1]
    return results


def sum_all(value):
    for bit in [1] + across():
        value = value + flip(value, bit)
    size = lax.axis_size("grp")
    bit = 1
    while bit < size:
        value = value + lax.ppermute(value, "grp", [(i, i ^ bit) for i in range(size)])
        bit = 2 * bit
    return value


def adamw(weight, grad, first, second, rate):
    first = BETA_ONE * first + (1.0 - BETA_ONE) * grad
    second = BETA_TWO * second + (1.0 - BETA_TWO) * grad * grad
    corr_one = 1.0 - BETA_ONE**STEP
    corr_two = 1.0 - BETA_TWO**STEP
    moved = first / corr_one / (jnp.sqrt(second / corr_two) + EPSILON) + DECAY * weight
    return (weight - rate * moved, first, second)


def on_device(
    row_ids,
    bag_counts,
    labels,
    dense_input,
    tables,
    table_first,
    table_second,
    cross_down,
    down_first,
    down_second,
    cross_up,
    up_first,
    up_second,
    hidden_one,
    one_first,
    one_second,
    hidden_two,
    two_first,
    two_second,
    hidden_three,
    three_first,
    three_second,
    smalls,
    small_first,
    small_second,
):
    up_down = across()
    down_up = up_down[::-1]
    down_all = lax.all_gather(cross_down.astype(jnp.bfloat16), "rep", axis=1, tiled=True)
    up_all = lax.all_gather(cross_up.astype(jnp.bfloat16), "rep", axis=1, tiled=True)
    one_all = lax.all_gather(hidden_one.astype(jnp.bfloat16), "rep", axis=0, tiled=True)
    cross_bias, bias_one, bias_two, bias_three, head_weight, head_bias = split_smalls(smalls)
    group = lax.axis_size("grp")
    samples = row_ids.shape[0]
    repeats = lax.axis_size("rep")
    features, extent, width = tables.shape
    part = extent // repeats
    own_part = lax.dynamic_slice_in_dim(tables, lax.axis_index("rep") * part, part, axis=1)
    own_parts = [own_part.astype(jnp.bfloat16)]
    for step in range(group - 1):
        own_parts.append(ring(own_parts[-1]))
    half = features // 2
    spans = ((0, half, up_down), (half, features, down_up))
    table_halves = []
    table_keys = []
    for first, last, order in spans:
        rows = jnp.stack([piece[first:last] for piece in own_parts])[None]
        rows, keys = gather_across(rows, order)
        table_halves.append((rows, flip(rows, 1)))
        table_keys.append(keys)
    late = jnp.concatenate([hidden_two, hidden_three], axis=1).astype(jnp.bfloat16)
    late_all = place(*gather_across(late[None], up_down + [1]), 0, lambda index: index)
    count_float = bag_counts.astype(jnp.float32)
    hits = count(slot_ids(row_ids, bag_counts), group * extent, 4)
    anchor = pool(hits, table_halves[0], table_halves[1], table_keys, count_float, dense_input)
    lows, narrows, in_one = cross_forward(anchor, down_all, up_all, cross_bias)
    total_samples = samples * lax.axis_size("rep") * group
    target = labels.astype(jnp.float32)[:, None]
    (
        loss_local,
        grad_head,
        grad_head_bias,
        bias_grad_one,
        bias_grad_two,
        bias_grad_three,
        grad_one,
        grad_late,
        grad_stream,
    ) = head(
        in_one, one_all, late_all, (bias_one, bias_two, bias_three), head_weight, head_bias, target, total_samples
    )
    share_one = lax.psum_scatter(grad_one, "rep", scatter_dimension=0, tiled=True)
    core = (lax.axis_index("rep") % 2).astype(jnp.int32).reshape(1)
    send_up, keep_up, grad_down, bias_grads, grad_summed = cross_backward(
        anchor, grad_stream, lows, narrows, down_all, up_all, cross_bias, count_float, core, repeats
    )
    share_down = lax.psum_scatter(grad_down, "rep", scatter_dimension=1, tiled=True)
    bits = up_down[::-1]
    reduced = []
    for first, last, order in spans:
        send, keep = row_gradient(hits, grad_summed, first, last - first, group, core)
        received = flip(send, 1)
        shape = (last - first, group) + (2,) * len(bits) + (part, width)
        reduced.append(scatter_pair(keep.reshape(shape), received.reshape(shape), bits, order, 2))
    row_share = ring_scatter(jnp.concatenate(reduced, axis=0).transpose(1, 0, 2, 3))
    table_grads = []
    for first, last, order in spans:
        value, keys = gather_across(row_share[None, first:last], order + [1])
        table_grads.append(place(value, keys, 1, lambda index: (index % 2) * (repeats // 2) + index // 2))
    table_grad = jnp.concatenate(table_grads, axis=0).astype(jnp.float32)
    late_blocks = grad_late.reshape((2,) * len(bits) + (2, -1) + grad_late.shape[1:])
    late_received = flip(lax.dynamic_index_in_dim(late_blocks, 1 - core[0], len(bits), keepdims=False), 1)
    late_keep = lax.dynamic_index_in_dim(late_blocks, core[0], len(bits), keepdims=False)
    share_late = scatter_pair(late_keep, late_received, bits, up_down, 0)
    received_up = flip(send_up, 1)
    share_rows = keep_up.shape[2] // 2
    shape = (CROSS,) + (2,) * len(bits) + (2, share_rows, D_IN)
    ups = []
    for index, order in ((0, up_down), (1, down_up)):
        pair = [lax.index_in_dim(item.reshape(shape), index, len(bits) + 1, keepdims=False) for item in (keep_up, received_up)]
        ups.append(scatter_pair(pair[0], pair[1], bits, order, 1))
    share_one, share_late = sum_groups([share_one, share_late])
    share_two, share_three = share_late[:, :H2], share_late[:, H2:]
    (share_up,) = sum_groups([jnp.concatenate(ups, axis=1)])
    (share_down,) = sum_groups([share_down])
    small_grad = jnp.concatenate(
        [
            item.reshape(-1)
            for item in (
                bias_grads,
                bias_grad_one,
                bias_grad_two,
                bias_grad_three,
                grad_head,
                grad_head_bias,
                loss_local,
            )
        ]
    )
    small_total = sum_all(small_grad)
    small_sum, loss_sum = small_total[:-1], small_total[-1]
    new_tables, new_table_first, new_table_second = adamw(
        tables, table_grad, table_first, table_second, 1.0
    )
    new_down, new_down_first, new_down_second = adamw(
        cross_down, share_down, down_first, down_second, D_IN ** (-0.5)
    )
    new_up, new_up_first, new_up_second = adamw(
        cross_up, share_up, up_first, up_second, RANK ** (-0.5)
    )
    new_one, new_one_first, new_one_second = adamw(
        hidden_one, share_one, one_first, one_second, D_IN ** (-0.5)
    )
    new_two, new_two_first, new_two_second = adamw(
        hidden_two, share_two, two_first, two_second, H1 ** (-0.5)
    )
    new_three, new_three_first, new_three_second = adamw(
        hidden_three, share_three, three_first, three_second, H2 ** (-0.5)
    )
    new_smalls, new_small_first, new_small_second = adamw(
        smalls, small_sum, small_first, small_second, 0.1
    )
    return (
        loss_sum,
        new_tables,
        new_table_first,
        new_table_second,
        new_down,
        new_down_first,
        new_down_second,
        new_up,
        new_up_first,
        new_up_second,
        new_one,
        new_one_first,
        new_one_second,
        new_two,
        new_two_first,
        new_two_second,
        new_three,
        new_three_first,
        new_three_second,
        new_smalls,
        new_small_first,
        new_small_second,
    )


def solution(mesh):
    return jax.shard_map(
        on_device,
        mesh=mesh,
        in_specs=(
            P(("rep", "grp"), None, None),
            P(("rep", "grp"), None),
            P(("rep", "grp")),
            P(("rep", "grp"), None),
            P(None, "grp", None),
            P(None, "grp", None),
            P(None, "grp", None),
            P(None, "rep", None),
            P(None, "rep", None),
            P(None, "rep", None),
            P(None, "rep", None),
            P(None, "rep", None),
            P(None, "rep", None),
            P("rep", None),
            P("rep", None),
            P("rep", None),
            P("rep", None),
            P("rep", None),
            P("rep", None),
            P("rep", None),
            P("rep", None),
            P("rep", None),
            P(),
            P(),
            P(),
        ),
        out_specs=(
            P(),
            P(None, "grp", None),
            P(None, "grp", None),
            P(None, "grp", None),
            P(None, "rep", None),
            P(None, "rep", None),
            P(None, "rep", None),
            P(None, "rep", None),
            P(None, "rep", None),
            P(None, "rep", None),
            P("rep", None),
            P("rep", None),
            P("rep", None),
            P("rep", None),
            P("rep", None),
            P("rep", None),
            P("rep", None),
            P("rep", None),
            P("rep", None),
            P(),
            P(),
            P(),
        ),
        check_vma=False,
    )
```

```python
import functools

import jax
import jax.numpy as jnp
from jax import lax
from jax.experimental import pallas as pl
from jax.experimental.pallas import tpu as pltpu
from jax.sharding import PartitionSpec as P

D_IN = 3456
RANK = 512
CROSS = 3
H1 = 1024
H2 = 1024
H3 = 512
STEP = 10
GROUP = 8
SLOTS = 32
LOW = 128
VMEM_BYTES = 60 * 2**20


BETA_ONE = 0.9
BETA_TWO = 0.999
EPSILON = 1e-12
DECAY = 0.01


def split_smalls(smalls):
    extents = [CROSS * D_IN, H1, H2, H3, H3, 1]
    pieces = []
    offset = 0
    for extent in extents:
        pieces.append(smalls[offset : offset + extent])
        offset = offset + extent
    return (pieces[0].reshape(CROSS, D_IN), pieces[1], pieces[2], pieces[3], pieces[4], pieces[5])


def product(left, right):
    return jnp.dot(left, right, preferred_element_type=jnp.float32)


def left_product(left, right):
    return lax.dot_general(
        left, right, (((0,), (0,)), ((), ())), preferred_element_type=jnp.float32
    )


def right_product(left, right):
    return lax.dot_general(
        left, right, (((1,), (1,)), ((), ())), preferred_element_type=jnp.float32
    )


def silu_slope(value):
    logistic = jax.nn.sigmoid(value)
    return logistic * (1.0 + value * (1.0 - logistic))


def slot_ids(row_ids, bag_counts):
    samples, features, slots = row_ids.shape
    live = lax.broadcasted_iota(jnp.int32, row_ids.shape, 2) < bag_counts[:, :, None]
    ids = jnp.pad(jnp.where(live, row_ids, -1), ((0, 0), (0, 0), (0, SLOTS - slots)), constant_values=-1)
    return ids.transpose(1, 0, 2).reshape(features, samples // GROUP, GROUP * SLOTS)


def one_hot(codes, levels):
    rows = jnp.broadcast_to(codes, (16, codes.shape[1])).astype(jnp.bfloat16)
    wanted = lax.broadcasted_iota(jnp.int32, (levels, codes.shape[1]), 0).astype(jnp.float32).astype(jnp.bfloat16)
    hits = jnp.concatenate([rows] * (levels // 16), axis=0) == wanted
    return jnp.where(hits, jnp.ones((), jnp.bfloat16), jnp.zeros((), jnp.bfloat16)).astype(jnp.float8_e4m3fn)


def count_kernel(earlier, ids_ref, *refs):
    hits_ref, code_ref = refs[earlier:]
    samples = hits_ref.shape[1]
    highs = hits_ref.shape[2] // LOW
    ids = ids_ref[0]
    member = lax.broadcasted_iota(jnp.int32, ids.shape, 1) // SLOTS
    code_ref[0] = ((ids >> 7) * GROUP + member).astype(jnp.float32)
    code_ref[1] = (ids & (LOW - 1)).astype(jnp.float32)

    def add_groups(step, unused):
        first = pl.multiple_of(step * 8, 8)
        high_codes = code_ref[0, pl.ds(first, 8), :]
        low_codes = code_ref[1, pl.ds(first, 8), :]
        for pair in range(4):
            products = []
            for row in (2 * pair, 2 * pair + 1):
                high_hits = one_hot(high_codes[row : row + 1], highs * GROUP)
                low_hits = one_hot(low_codes[row : row + 1], LOW)
                products.append(right_product(high_hits, low_hits))
            start = pl.multiple_of(step * 8 * GROUP + pair * 2 * GROUP, 2 * GROUP)
            for high in range(highs):
                part = slice(high * GROUP, (high + 1) * GROUP)
                tile = jnp.concatenate([products[0][part], products[1][part]], axis=0)
                hits_ref[0, pl.ds(start, 2 * GROUP), high * LOW : (high + 1) * LOW] = tile.astype(
                    jnp.bfloat16
                )
        return unused

    lax.fori_loop(0, samples // (8 * GROUP), add_groups, 0)


def count(ids, rows, pieces):
    features, groups, slots = ids.shape
    samples = groups * GROUP
    cuts = [features * piece // pieces for piece in range(pieces + 1)]
    hits = None
    for first, last in zip(cuts[:-1], cuts[1:]):
        earlier = [] if hits is None else [hits]
        hits = pl.pallas_call(
            functools.partial(count_kernel, len(earlier)),
            grid=(last - first,),
            in_specs=[pl.BlockSpec((1, groups, slots), functools.partial(shifted_block, first))]
            + [pl.BlockSpec(memory_space=pl.ANY)] * len(earlier),
            out_specs=pl.BlockSpec((1, samples, rows), functools.partial(shifted_block, first)),
            out_shape=jax.ShapeDtypeStruct((features, samples, rows), jnp.bfloat16),
            input_output_aliases={1: 0} if earlier else {},
            scratch_shapes=[pltpu.VMEM((2, groups, slots), jnp.float32)],
            compiler_params=pltpu.CompilerParams(vmem_limit_bytes=VMEM_BYTES),
            cost_estimate=pl.CostEstimate(flops=1, bytes_accessed=1, transcendentals=0),
        )(ids, *earlier)
    return hits


def shifted_block(first, feature):
    return (feature + first, 0, 0)


def feature_counts(counts_ref, feature):
    lanes = lax.broadcasted_iota(jnp.int32, counts_ref.shape, 1)
    return jnp.sum(jnp.where(lanes == feature, counts_ref[...], 0.0), axis=1, keepdims=True)


def pool_kernel(
    place_ref, hits_ref, own_a, other_a, own_b, other_b, counts_ref, dense_ref, anchor_ref, table_ref, *, keys, half
):
    feature = pl.program_id(0)
    features = pl.num_programs(0) - 1
    mine = place_ref[0]
    member = place_ref[1]
    group = table_ref.shape[0]

    def assemble(own_ref, other_ref, order):
        for position, key in enumerate(order):
            for step in range(group):
                row = lax.rem(member + group - step, group)
                table_ref[row, mine ^ key] = own_ref[position, step, 0]
                table_ref[row, mine ^ (key ^ 1)] = other_ref[position, step, 0]

    @pl.when(feature < half)
    def _():
        assemble(own_a, other_a, keys[0])

    @pl.when((feature >= half) & (feature < features))
    def _():
        assemble(own_b, other_b, keys[1])

    @pl.when(feature < features)
    def _():
        table = table_ref[...].reshape(-1, table_ref.shape[-1])
        anchor_ref[...] = product(hits_ref[0], table) / feature_counts(counts_ref, feature)

    @pl.when(feature == features)
    def _():
        anchor_ref[...] = dense_ref[...]


def pool(hits, first_half, second_half, keys, count_float, dense_input):
    features, samples, rows = hits.shape
    last = features - 1
    half = first_half[0].shape[2]
    halves, group, unused, part, width = first_half[0].shape
    block = (halves, group, 1, part, width)
    low_block = pl.BlockSpec(block, lambda f, place: (0, 0, jnp.minimum(f, half - 1), 0, 0))
    high_block = pl.BlockSpec(block, lambda f, place: (0, 0, jnp.clip(f - half, 0, last - half), 0, 0))
    place = jnp.stack([lax.axis_index("rep"), lax.axis_index("grp")]).astype(jnp.int32)
    return pl.pallas_call(
        functools.partial(pool_kernel, keys=keys, half=half),
        grid_spec=pltpu.PrefetchScalarGridSpec(
            num_scalar_prefetch=1,
            grid=(features + 1,),
            in_specs=[
                pl.BlockSpec((1, samples, rows), lambda f, place: (jnp.minimum(f, last), 0, 0)),
                low_block,
                low_block,
                high_block,
                high_block,
                pl.BlockSpec((samples, features), lambda f, place: (0, 0)),
                pl.BlockSpec((samples, width), lambda f, place: (0, 0)),
            ],
            out_specs=pl.BlockSpec((samples, width), lambda f, place: (0, f)),
            scratch_shapes=[pltpu.VMEM((group, 2 * halves, part, width), jnp.bfloat16)],
        ),
        out_shape=jax.ShapeDtypeStruct((samples, (features + 1) * width), jnp.float32),
        compiler_params=pltpu.CompilerParams(vmem_limit_bytes=VMEM_BYTES),
        cost_estimate=pl.CostEstimate(flops=1, bytes_accessed=1, transcendentals=0),
    )(place, hits, *first_half, *second_half, count_float, dense_input)


def cross_forward_kernel(
    anchor_in, down_ref, up_ref, bias_ref, low_ref, narrow_ref, last_ref, anchor_ref, stream_ref, sum_ref
):
    layer, phase, block = pl.program_id(0), pl.program_id(1), pl.program_id(2)
    layers = pl.num_programs(0)

    @pl.when((layer == 0) & (phase == 0))
    def _():
        anchor_ref[block] = anchor_in[...]
        stream_ref[block] = anchor_in[...]

    @pl.when(phase == 0)
    def _():
        low = stream_ref[block].astype(jnp.bfloat16)
        low_ref[0] = low
        part = product(low, down_ref[0])

        @pl.when(block == 0)
        def _():
            sum_ref[...] = part

        @pl.when(block > 0)
        def _():
            sum_ref[...] += part

    @pl.when((phase == 1) & (block == 0))
    def _():
        narrow_ref[0] = sum_ref[...].astype(jnp.bfloat16)

    @pl.when(phase == 1)
    def _():
        factor = product(narrow_ref[0], up_ref[0]) + bias_ref[0]
        stream = anchor_ref[block] * factor + stream_ref[block]
        stream_ref[block] = stream

        @pl.when(layer == layers - 1)
        def _():
            last_ref[...] = stream.astype(jnp.bfloat16)


def cross_forward(anchor, down, up, bias):
    samples, width = anchor.shape
    layers, unused, rank = down.shape
    blocks = 3
    piece = width // blocks
    final = blocks - 1
    return pl.pallas_call(
        cross_forward_kernel,
        grid=(layers, 2, blocks),
        in_specs=[
            pl.BlockSpec((samples, piece), lambda l, p, j: (0, jnp.where((l == 0) & (p == 0), j, final))),
            pl.BlockSpec((1, piece, rank), lambda l, p, j: (l, jnp.where(p == 0, j, final), 0)),
            pl.BlockSpec((1, rank, piece), lambda l, p, j: (l, 0, jnp.where(p == 1, j, 0))),
            pl.BlockSpec((1, 1, piece), lambda l, p, j: (l, 0, jnp.where(p == 1, j, 0))),
        ],
        out_specs=[
            pl.BlockSpec((1, samples, piece), lambda l, p, j: (l, 0, jnp.where(p == 0, j, final))),
            pl.BlockSpec((1, samples, rank), lambda l, p, j: (l, 0, 0)),
            pl.BlockSpec((samples, piece), lambda l, p, j: (0, jnp.where((l == layers - 1) & (p == 1), j, 0))),
        ],
        out_shape=[
            jax.ShapeDtypeStruct((layers, samples, width), jnp.bfloat16),
            jax.ShapeDtypeStruct((layers, samples, rank), jnp.bfloat16),
            jax.ShapeDtypeStruct((samples, width), jnp.bfloat16),
        ],
        scratch_shapes=[
            pltpu.VMEM((blocks, samples, piece), jnp.float32),
            pltpu.VMEM((blocks, samples, piece), jnp.float32),
            pltpu.VMEM((samples, rank), jnp.float32),
        ],
        compiler_params=pltpu.CompilerParams(vmem_limit_bytes=VMEM_BYTES),
        cost_estimate=pl.CostEstimate(flops=1, bytes_accessed=1, transcendentals=0),
    )(anchor, down, up, bias.reshape(layers, 1, width))


def head_kernel(
    input_ref,
    one_ref,
    late_ref,
    bias_one,
    bias_two,
    bias_three,
    head_ref,
    head_bias,
    target_ref,
    loss_ref,
    grad_head,
    grad_head_bias,
    grad_bias_one,
    grad_bias_two,
    grad_bias_three,
    grad_one,
    grad_late,
    grad_stream,
    sum_ref,
    back_ref,
    *,
    total
):
    step = pl.program_id(0)
    blocks = pl.num_programs(0) // 2

    @pl.when(step < blocks)
    def _():
        part = product(input_ref[...], one_ref[...])

        @pl.when(step == 0)
        def _():
            sum_ref[...] = part

        @pl.when(step > 0)
        def _():
            sum_ref[...] += part

    @pl.when(step == blocks)
    def _():
        pre_one = sum_ref[...] + bias_one[...]
        in_two = jax.nn.silu(pre_one).astype(jnp.bfloat16)
        two = late_ref[:, :H2]
        three = late_ref[:, H2:]
        pre_two = product(in_two, two) + bias_two[...]
        in_three = jax.nn.silu(pre_two).astype(jnp.bfloat16)
        pre_three = product(in_three, three) + bias_three[...]
        top = jax.nn.silu(pre_three)
        head = head_ref[...]
        target = target_ref[...]
        logit = jnp.sum(top * head, axis=1, keepdims=True) + head_bias[...]
        losses = jnp.maximum(logit, 0.0) + jnp.log1p(jnp.exp(-jnp.abs(logit))) - target * logit
        loss_ref[...] = jnp.sum(losses, axis=0, keepdims=True)
        grad_logit = (jax.nn.sigmoid(logit) - target) / total
        grad_head[...] = jnp.sum(grad_logit * top, axis=0, keepdims=True)
        grad_head_bias[...] = jnp.sum(grad_logit, axis=0, keepdims=True)
        back = (grad_logit * head * silu_slope(pre_three)).astype(jnp.bfloat16)
        grad_bias_three[...] = jnp.sum(back.astype(jnp.float32), axis=0, keepdims=True)
        grad_late[:, H2:] = left_product(in_three, back).astype(jnp.bfloat16)
        back = (right_product(back, three) * silu_slope(pre_two)).astype(jnp.bfloat16)
        grad_bias_two[...] = jnp.sum(back.astype(jnp.float32), axis=0, keepdims=True)
        grad_late[:, :H2] = left_product(in_two, back).astype(jnp.bfloat16)
        back = (right_product(back, two) * silu_slope(pre_one)).astype(jnp.bfloat16)
        grad_bias_one[...] = jnp.sum(back.astype(jnp.float32), axis=0, keepdims=True)
        back_ref[...] = back

    @pl.when(step >= blocks)
    def _():
        grad_one[...] = left_product(input_ref[...], back_ref[...]).astype(jnp.bfloat16)
        grad_stream[...] = right_product(back_ref[...], one_ref[...])


def head(inputs, one, late, biases, head_weight, head_bias, target, total):
    samples, width = inputs.shape
    blocks = 3
    piece = width // blocks

    def whole(shape):
        return pl.BlockSpec(shape, lambda s: (0,) * len(shape))

    rows = [bias.reshape(1, -1) for bias in biases] + [head_weight.reshape(1, -1), head_bias.reshape(1, 1)]
    small = [(1, 1), (1, H3), (1, 1), (1, H1), (1, H2), (1, H3)]
    return pl.pallas_call(
        functools.partial(head_kernel, total=total),
        grid=(2 * blocks,),
        in_specs=[
            pl.BlockSpec((samples, piece), lambda s: (0, lax.rem(s, blocks))),
            pl.BlockSpec((piece, H1), lambda s: (lax.rem(s, blocks), 0)),
            whole(late.shape),
        ]
        + [whole(row.shape) for row in rows]
        + [whole((samples, 1))],
        out_specs=[whole(shape) for shape in small]
        + [
            pl.BlockSpec((piece, H1), lambda s: (jnp.maximum(s - blocks, 0), 0)),
            whole(late.shape),
            pl.BlockSpec((samples, piece), lambda s: (0, jnp.maximum(s - blocks, 0))),
        ],
        out_shape=[jax.ShapeDtypeStruct(shape, jnp.float32) for shape in small]
        + [
            jax.ShapeDtypeStruct(one.shape, jnp.bfloat16),
            jax.ShapeDtypeStruct(late.shape, jnp.bfloat16),
            jax.ShapeDtypeStruct((samples, width), jnp.float32),
        ],
        scratch_shapes=[pltpu.VMEM((samples, H1), jnp.float32), pltpu.VMEM((samples, H1), jnp.bfloat16)],
        compiler_params=pltpu.CompilerParams(vmem_limit_bytes=VMEM_BYTES),
        cost_estimate=pl.CostEstimate(flops=1, bytes_accessed=1, transcendentals=0),
    )(inputs, one, late, *rows, target)


def cross_backward_kernel(
    core_ref,
    anchor_in,
    grad_in,
    low_ref,
    narrow_ref,
    down_ref,
    up_ref,
    bias_ref,
    counts_ref,
    send_ref,
    keep_ref,
    grad_down,
    grad_bias,
    grad_summed,
    anchor_ref,
    stream_ref,
    total_ref,
    sum_ref,
    back_ref,
    both_ref,
):
    layer, phase, block = pl.program_id(0), pl.program_id(1), pl.program_id(2)
    layers = pl.num_programs(0)

    @pl.when((layer == 0) & (phase == 0))
    def _():
        anchor_ref[block] = anchor_in[...]
        stream_ref[block] = grad_in[...]
        total_ref[block] = jnp.zeros(grad_in.shape, jnp.float32)

    @pl.when(phase == 0)
    def _():
        grad_next = stream_ref[block]
        grad_factor = (anchor_ref[block] * grad_next).astype(jnp.bfloat16)
        grad_bias[0] = jnp.sum(grad_factor.astype(jnp.float32), axis=0, keepdims=True)
        narrow = narrow_ref[0]
        both_ref[...] = left_product(narrow, grad_factor).astype(jnp.bfloat16).reshape(both_ref.shape)
        core = core_ref[0]
        send_ref[0] = both_ref[:, 1 - core]
        keep_ref[0] = both_ref[:, core]
        factor = product(narrow, up_ref[0]) + bias_ref[0]
        total_ref[block] += factor * grad_next
        part = right_product(grad_factor, up_ref[0])

        @pl.when(block == 0)
        def _():
            sum_ref[...] = part

        @pl.when(block > 0)
        def _():
            sum_ref[...] += part

    @pl.when((phase == 1) & (block == 0))
    def _():
        back_ref[...] = sum_ref[...].astype(jnp.bfloat16)

    @pl.when(phase == 1)
    def _():
        back = back_ref[...]
        grad_down[0] = left_product(low_ref[0], back).astype(jnp.bfloat16)
        grad_stream = stream_ref[block] + right_product(back, down_ref[0])
        stream_ref[block] = grad_stream

        @pl.when(layer == layers - 1)
        def _():
            features = grad_stream.shape[1] // LOW
            total = total_ref[block] + grad_stream
            for index in range(features):
                counts = jnp.maximum(feature_counts(counts_ref, block * features + index), 1.0)
                part = slice(index * LOW, (index + 1) * LOW)
                grad_summed[:, part] = (total[:, part] / counts).astype(jnp.bfloat16)


def cross_backward(anchor, grad_stream, lows, narrows, down, up, bias, count_float, core, repeats):
    samples, width = anchor.shape
    layers, unused, rank = down.shape
    blocks = 3
    piece = width // blocks
    final = blocks - 1
    share = rank // repeats

    def first_pass(l, p, j, core):
        return (0, jnp.where((l == 0) & (p == 0), j, final))

    def up_block(l, p, j, core):
        return (layers - 1 - l, 0, jnp.where(p == 0, j, final))

    def low_block(l, p, j, core):
        return (layers - 1 - l, 0, jnp.where(p == 1, j, 0))

    def down_block(l, p, j, core):
        return (layers - 1 - l, jnp.where(p == 1, j, 0), 0)

    half = jax.ShapeDtypeStruct((layers, repeats // 2, share, width), jnp.bfloat16)
    half_spec = pl.BlockSpec(
        (1, repeats // 2, share, piece),
        lambda l, p, j, core: (layers - 1 - l, 0, 0, jnp.where(p == 0, j, final)),
    )
    return pl.pallas_call(
        cross_backward_kernel,
        grid_spec=pltpu.PrefetchScalarGridSpec(
            num_scalar_prefetch=1,
            grid=(layers, 2, blocks),
            in_specs=[
                pl.BlockSpec((samples, piece), first_pass),
                pl.BlockSpec((samples, piece), first_pass),
                pl.BlockSpec((1, samples, piece), low_block),
                pl.BlockSpec((1, samples, rank), lambda l, p, j, core: (layers - 1 - l, 0, 0)),
                pl.BlockSpec((1, piece, rank), down_block),
                pl.BlockSpec((1, rank, piece), up_block),
                pl.BlockSpec((1, 1, piece), up_block),
                pl.BlockSpec(count_float.shape, lambda l, p, j, core: (0, 0)),
            ],
            out_specs=[
                half_spec,
                half_spec,
                pl.BlockSpec((1, piece, rank), down_block),
                pl.BlockSpec((1, 1, piece), up_block),
                pl.BlockSpec(
                    (samples, piece),
                    lambda l, p, j, core: (0, jnp.where((l == layers - 1) & (p == 1), j, 0)),
                ),
            ],
            scratch_shapes=[
                pltpu.VMEM((blocks, samples, piece), jnp.float32),
                pltpu.VMEM((blocks, samples, piece), jnp.float32),
                pltpu.VMEM((blocks, samples, piece), jnp.float32),
                pltpu.VMEM((samples, rank), jnp.float32),
                pltpu.VMEM((samples, rank), jnp.bfloat16),
                pltpu.VMEM((repeats // 2, 2, share, piece), jnp.bfloat16),
            ],
        ),
        out_shape=[
            half,
            half,
            jax.ShapeDtypeStruct(down.shape, jnp.bfloat16),
            jax.ShapeDtypeStruct((layers, 1, width), jnp.float32),
            jax.ShapeDtypeStruct((samples, width), jnp.bfloat16),
        ],
        compiler_params=pltpu.CompilerParams(vmem_limit_bytes=VMEM_BYTES),
        cost_estimate=pl.CostEstimate(
            flops=10**12,
            bytes_accessed=layers * width * (8 * rank + 2 * samples) + 10 * samples * width,
            transcendentals=0,
        ),
    )(core, anchor, grad_stream, lows, narrows, down, up, bias.reshape(layers, 1, width), count_float)


def row_kernel(earlier, core_ref, hits_ref, grad_ref, *refs):
    send_ref, keep_ref, both_ref = refs[earlier:]
    both_ref[...] = left_product(hits_ref[0], grad_ref[...]).astype(jnp.bfloat16).reshape(both_ref.shape)
    core = core_ref[0]
    send_ref[0] = both_ref[:, 1 - core]
    keep_ref[0] = both_ref[:, core]


def row_gradient(hits, grad_summed, start, stop, group, core, pieces):
    unused, samples, rows = hits.shape
    half = rows // group // 2
    shape = jax.ShapeDtypeStruct((stop - start, group, half, LOW), jnp.bfloat16)
    cuts = [start + (stop - start) * piece // pieces for piece in range(pieces + 1)]
    results = []
    for first, last in zip(cuts[:-1], cuts[1:]):
        spec = pl.BlockSpec((1, group, half, LOW), functools.partial(row_block, first - start))
        results = pl.pallas_call(
            functools.partial(row_kernel, len(results)),
            grid_spec=pltpu.PrefetchScalarGridSpec(
                num_scalar_prefetch=1,
                grid=(last - first,),
                in_specs=[
                    pl.BlockSpec((1, samples, rows), functools.partial(hits_block, first)),
                    pl.BlockSpec((samples, LOW), functools.partial(column_block, first)),
                ]
                + [pl.BlockSpec(memory_space=pl.ANY)] * len(results),
                out_specs=[spec, spec],
                scratch_shapes=[pltpu.VMEM((group, 2, half, LOW), jnp.bfloat16)],
            ),
            out_shape=[shape, shape],
            input_output_aliases={3: 0, 4: 1} if results else {},
            compiler_params=pltpu.CompilerParams(vmem_limit_bytes=VMEM_BYTES),
            cost_estimate=pl.CostEstimate(
                flops=10**12,
                bytes_accessed=2 * (last - first) * rows * (samples + LOW),
                transcendentals=0,
            ),
        )(core, hits, grad_summed, *results)
    return results


def row_block(first, feature, core):
    return (feature + first, 0, 0, 0)


def hits_block(first, feature, core):
    return (feature + first, 0, 0)


def column_block(first, feature, core):
    return (0, feature + first)


def flip(value, bit):
    return lax.ppermute(value, "rep", [(i, i ^ bit) for i in range(lax.axis_size("rep"))])


def shift(value, step):
    size = lax.axis_size("grp")
    return lax.ppermute(value, "grp", [(i, (i + step) % size) for i in range(size)])


def across():
    return [1 << i for i in range(1, lax.axis_size("rep").bit_length() - 1)]


def gather_across(value, order):
    keys = [0]
    for bit in order:
        value = jnp.concatenate([value, flip(value, bit)], axis=0)
        keys = keys + [key ^ bit for key in keys]
    return value, keys


def place(value, keys, axis, index_of):
    mine = lax.axis_index("rep")
    extent = value.shape[axis + 1]
    shape = list(value.shape[1:])
    shape[axis] = extent * len(keys)
    whole = jnp.zeros(shape, value.dtype)
    for position, key in enumerate(keys):
        whole = lax.dynamic_update_slice_in_dim(whole, value[position], index_of(mine ^ key) * extent, axis)
    return whole


def after(value, earlier):
    return lax.optimization_barrier((value, earlier))[0]


class HalvingSum:
    def __init__(self, keep, received, bits, order, axis):
        self.keep, self.received = keep, received
        self.left, self.order, self.axis = list(bits), list(order), axis

    def step(self, *earlier):
        bit = self.order.pop(0)
        position = self.axis + self.left.index(bit)
        self.left.remove(bit)
        mine = (lax.axis_index("rep") // bit) % 2
        pair = after((self.keep, self.received), earlier)
        send, keep = (
            sum(lax.dynamic_index_in_dim(item, index, position, keepdims=False) for item in pair)
            for index in (1 - mine, mine)
        )
        self.keep, self.sent = keep, send
        self.received = flip(self.sent, bit)

    def result(self):
        return self.keep + self.received


class GroupSum:
    def __init__(self, *shares):
        self.size = lax.axis_size("grp")
        self.mine = lax.axis_index("grp")
        self.shares = shares

    def scatter(self, *earlier):
        chunks = [share.reshape(self.size, -1, LOW) for share in after(self.shares, earlier)]
        self.lengths = [chunk.shape[1] for chunk in chunks]
        sent = []
        for step in range(self.size):
            index = lax.rem(self.mine + step, self.size)
            parts = [lax.dynamic_index_in_dim(chunk, index, 0, keepdims=False) for chunk in chunks]
            sent.append(jnp.concatenate(parts, axis=0) if len(parts) > 1 else parts[0])
        self.sent = sent
        self.received = [shift(part, step) for step, part in enumerate(self.sent) if step]
        self.total = sum(part.astype(jnp.float32) for part in [self.sent[0]] + self.received).astype(sent[0].dtype)

    def gather(self, *earlier):
        self.sent = after(self.total, earlier)
        self.received = [shift(self.sent, step) for step in range(1, self.size)]

    def result(self):
        whole = jnp.zeros((self.size,) + self.total.shape, self.total.dtype)
        for step, part in enumerate([self.sent] + self.received):
            index = lax.rem(self.mine + self.size - step, self.size)
            whole = lax.dynamic_update_index_in_dim(whole, part, index, 0)
        results = []
        offset = 0
        for share, length in zip(self.shares, self.lengths):
            part = whole[:, offset : offset + length]
            results.append(part.reshape(share.shape).astype(jnp.float32))
            offset = offset + length
        return results


class SmallSum:
    def __init__(self, value):
        self.value, self.received = value, None
        self.left = [("rep", bit) for bit in [1] + across()]
        bit = 1
        while bit < lax.axis_size("grp"):
            self.left.append(("grp", bit))
            bit = 2 * bit

    def step(self):
        if self.received is not None:
            self.value = self.value + self.received
        axis, bit = self.left.pop(0)
        self.sent = self.value
        self.received = lax.ppermute(self.value, axis, [(i, i ^ bit) for i in range(lax.axis_size(axis))])

    def finish(self):
        while self.left:
            self.step()
        self.value = self.value + self.received


def adamw(weight, grad, first, second, rate):
    first = BETA_ONE * first + (1.0 - BETA_ONE) * grad
    second = BETA_TWO * second + (1.0 - BETA_TWO) * grad * grad
    corr_one = 1.0 - BETA_ONE**STEP
    corr_two = 1.0 - BETA_TWO**STEP
    moved = first / corr_one / (jnp.sqrt(second / corr_two) + EPSILON) + DECAY * weight
    return (weight - rate * moved, first, second)


def on_device(
    row_ids,
    bag_counts,
    labels,
    dense_input,
    tables,
    table_first,
    table_second,
    cross_down,
    down_first,
    down_second,
    cross_up,
    up_first,
    up_second,
    hidden_one,
    one_first,
    one_second,
    hidden_two,
    two_first,
    two_second,
    hidden_three,
    three_first,
    three_second,
    smalls,
    small_first,
    small_second,
):
    up_down = across()
    down_up = up_down[::-1]
    down_all = lax.all_gather(cross_down.astype(jnp.bfloat16), "rep", axis=1, tiled=True)
    up_all = lax.all_gather(cross_up.astype(jnp.bfloat16), "rep", axis=1, tiled=True)
    one_all = lax.all_gather(hidden_one.astype(jnp.bfloat16), "rep", axis=0, tiled=True)
    cross_bias, bias_one, bias_two, bias_three, head_weight, head_bias = split_smalls(smalls)
    group = lax.axis_size("grp")
    samples = row_ids.shape[0]
    repeats = lax.axis_size("rep")
    features, extent, width = tables.shape
    part = extent // repeats
    own_part = lax.dynamic_slice_in_dim(tables, lax.axis_index("rep") * part, part, axis=1)
    own_part = own_part.astype(jnp.bfloat16)
    own_parts = [own_part] + [shift(own_part, step) for step in range(1, group)]
    half = features // 2
    spans = ((0, half, up_down), (half, features, down_up))
    table_halves = []
    table_keys = []
    for first, last, order in spans:
        rows = jnp.stack([piece[first:last] for piece in own_parts])[None]
        rows, keys = gather_across(rows, order)
        table_halves.append((rows, flip(rows, 1)))
        table_keys.append(keys)
    late = jnp.concatenate([hidden_two, hidden_three], axis=1).astype(jnp.bfloat16)
    late_all = place(*gather_across(late[None], up_down + [1]), 0, lambda index: index)
    count_float = bag_counts.astype(jnp.float32)
    hits = count(slot_ids(row_ids, bag_counts), group * extent, 4)
    anchor = pool(hits, table_halves[0], table_halves[1], table_keys, count_float, dense_input)
    lows, narrows, in_one = cross_forward(anchor, down_all, up_all, cross_bias)
    total_samples = samples * lax.axis_size("rep") * group
    target = labels.astype(jnp.float32)[:, None]
    (
        loss_local,
        grad_head,
        grad_head_bias,
        bias_grad_one,
        bias_grad_two,
        bias_grad_three,
        grad_one,
        grad_late,
        grad_stream,
    ) = head(
        in_one, one_all, late_all, (bias_one, bias_two, bias_three), head_weight, head_bias, target, total_samples
    )
    share_one = lax.psum_scatter(grad_one, "rep", scatter_dimension=0, tiled=True)
    core = (lax.axis_index("rep") % 2).astype(jnp.int32).reshape(1)
    bits = up_down[::-1]
    late_blocks = grad_late.reshape((2,) * len(bits) + (2, -1) + grad_late.shape[1:])
    late_send, late_keep = (
        lax.dynamic_index_in_dim(late_blocks, index, len(bits), keepdims=False) for index in (1 - core[0], core[0])
    )
    late_sum = HalvingSum(late_keep, flip(late_send, 1), bits, up_down, 0)
    late_sum.step()
    send_up, keep_up, grad_down, bias_grads, grad_summed = cross_backward(
        anchor,
        after(grad_stream, late_sum.sent),
        lows,
        narrows,
        down_all,
        up_all,
        cross_bias,
        count_float,
        core,
        repeats,
    )
    share_down = lax.psum_scatter(grad_down, "rep", scatter_dimension=1, tiled=True)
    received_up = flip(send_up, 1)
    share_rows = keep_up.shape[2] // 2
    shape = (CROSS,) + (2,) * len(bits) + (2, share_rows, D_IN)
    up_sums = [
        HalvingSum(
            lax.index_in_dim(keep_up.reshape(shape), index, len(bits) + 1, keepdims=False),
            lax.index_in_dim(received_up.reshape(shape), index, len(bits) + 1, keepdims=False),
            bits,
            order,
            1,
        )
        for index, order in ((0, up_down), (1, down_up))
    ]
    small_grad = jnp.concatenate(
        [
            item.reshape(-1)
            for item in (
                bias_grads,
                bias_grad_one,
                bias_grad_two,
                bias_grad_three,
                grad_head,
                grad_head_bias,
                loss_local,
            )
        ]
    )
    up_p, up_q = up_sums
    row_sums = []
    grad_rows = after(grad_summed, late_sum.received)
    for first, last, order in spans:
        send, keep = row_gradient(hits, grad_rows, first, last, group, core, 2)
        shape = (last - first, group) + (2,) * len(bits) + (part, width)
        row_sums.append(HalvingSum(keep.reshape(shape), flip(send, 1).reshape(shape), bits, order, 2))
        if len(row_sums) == 1:
            for step in bits[1:]:
                late_sum.step(keep)
            for item in up_sums:
                item.step(late_sum.sent)
            one_total = GroupSum(share_one, late_sum.result())
            one_total.scatter(*[item.sent for item in up_sums])
            one_total.gather()
            grad_rows = after(grad_rows, one_total.sent)
    row_p, row_q = row_sums
    for step in bits[1:]:
        for item in up_sums:
            item.step(one_total.sent)
    for item in row_sums:
        item.step(up_p.sent, up_q.sent)
    share_up = jnp.concatenate([item.result() for item in up_sums], axis=1)
    share_up, share_down = lax.psum((share_up, share_down), "grp")
    for step in bits[1:]:
        for item in row_sums:
            item.step(up_p.received, up_q.received)
    row_parts = [item.result() for item in row_sums]
    row_total = GroupSum(jnp.concatenate(row_parts, axis=0).transpose(1, 0, 2, 3))
    row_total.scatter(share_up, share_down)
    small = SmallSum(after(small_grad, row_total.sent))
    small.finish()
    row_share = row_total.total.reshape(features, part, width)
    share_one, share_late = one_total.result()
    share_up, share_down = share_up.astype(jnp.float32), share_down.astype(jnp.float32)
    share_two, share_three = share_late[:, :H2], share_late[:, H2:]
    small_sum, loss_sum = small.value[:-1], small.value[-1]
    new_one, new_one_first, new_one_second = adamw(
        hidden_one, share_one, one_first, one_second, D_IN ** (-0.5)
    )
    new_two, new_two_first, new_two_second = adamw(
        hidden_two, share_two, two_first, two_second, H1 ** (-0.5)
    )
    new_three, new_three_first, new_three_second = adamw(
        hidden_three, share_three, three_first, three_second, H2 ** (-0.5)
    )
    table_grads = []
    for first, last, order in spans:
        value, keys = gather_across(row_share[None, first:last], order + [1])
        table_grads.append(place(value, keys, 1, lambda index: (index % 2) * (repeats // 2) + index // 2))
    table_grad = jnp.concatenate(table_grads, axis=0).astype(jnp.float32)
    new_up, new_up_first, new_up_second = adamw(
        cross_up, share_up, up_first, up_second, RANK ** (-0.5)
    )
    new_tables, new_table_first, new_table_second = adamw(
        tables, table_grad, table_first, table_second, 1.0
    )
    new_down, new_down_first, new_down_second = adamw(
        cross_down, share_down, down_first, down_second, D_IN ** (-0.5)
    )
    new_smalls, new_small_first, new_small_second = adamw(
        smalls, small_sum, small_first, small_second, 0.1
    )
    return (
        loss_sum,
        new_tables,
        new_table_first,
        new_table_second,
        new_down,
        new_down_first,
        new_down_second,
        new_up,
        new_up_first,
        new_up_second,
        new_one,
        new_one_first,
        new_one_second,
        new_two,
        new_two_first,
        new_two_second,
        new_three,
        new_three_first,
        new_three_second,
        new_smalls,
        new_small_first,
        new_small_second,
    )


def solution(mesh):
    return jax.shard_map(
        on_device,
        mesh=mesh,
        in_specs=(
            P(("rep", "grp"), None, None),
            P(("rep", "grp"), None),
            P(("rep", "grp")),
            P(("rep", "grp"), None),
            P(None, "grp", None),
            P(None, "grp", None),
            P(None, "grp", None),
            P(None, "rep", None),
            P(None, "rep", None),
            P(None, "rep", None),
            P(None, "rep", None),
            P(None, "rep", None),
            P(None, "rep", None),
            P("rep", None),
            P("rep", None),
            P("rep", None),
            P("rep", None),
            P("rep", None),
            P("rep", None),
            P("rep", None),
            P("rep", None),
            P("rep", None),
            P(),
            P(),
            P(),
        ),
        out_specs=(
            P(),
            P(None, "grp", None),
            P(None, "grp", None),
            P(None, "grp", None),
            P(None, "rep", None),
            P(None, "rep", None),
            P(None, "rep", None),
            P(None, "rep", None),
            P(None, "rep", None),
            P(None, "rep", None),
            P("rep", None),
            P("rep", None),
            P("rep", None),
            P("rep", None),
            P("rep", None),
            P("rep", None),
            P("rep", None),
            P("rep", None),
            P("rep", None),
            P(),
            P(),
            P(),
        ),
        check_vma=False,
    )
```

```python
import functools

import jax
import jax.numpy as jnp
from jax import lax
from jax.experimental import pallas as pl
from jax.experimental.pallas import tpu as pltpu
from jax.sharding import PartitionSpec as P

D_IN = 3456
RANK = 512
CROSS = 3
H1 = 1024
H2 = 1024
H3 = 512
STEP = 10
GROUP = 8
SLOTS = 32
LOW = 128
VMEM_BYTES = 60 * 2**20
HINT = 10**10


BETA_ONE = 0.9
BETA_TWO = 0.999
EPSILON = 1e-12
DECAY = 0.01


def split_smalls(smalls):
    extents = [CROSS * D_IN, H1, H2, H3, H3, 1]
    pieces = []
    offset = 0
    for extent in extents:
        pieces.append(smalls[offset : offset + extent])
        offset = offset + extent
    return (pieces[0].reshape(CROSS, D_IN), pieces[1], pieces[2], pieces[3], pieces[4], pieces[5])


def product(left, right):
    return jnp.dot(left, right, preferred_element_type=jnp.float32)


def left_product(left, right):
    return lax.dot_general(
        left, right, (((0,), (0,)), ((), ())), preferred_element_type=jnp.float32
    )


def right_product(left, right):
    return lax.dot_general(
        left, right, (((1,), (1,)), ((), ())), preferred_element_type=jnp.float32
    )


def silu_slope(value):
    logistic = jax.nn.sigmoid(value)
    return logistic * (1.0 + value * (1.0 - logistic))


def slot_ids(row_ids, bag_counts):
    samples, features, slots = row_ids.shape
    live = lax.broadcasted_iota(jnp.int32, row_ids.shape, 2) < bag_counts[:, :, None]
    ids = jnp.pad(jnp.where(live, row_ids, -1), ((0, 0), (0, 0), (0, SLOTS - slots)), constant_values=-1)
    return ids.transpose(1, 0, 2).reshape(features, samples // GROUP, GROUP * SLOTS)


def one_hot(codes, levels):
    rows = jnp.broadcast_to(codes, (16, codes.shape[1])).astype(jnp.bfloat16)
    wanted = lax.broadcasted_iota(jnp.int32, (levels, codes.shape[1]), 0).astype(jnp.float32).astype(jnp.bfloat16)
    hits = jnp.concatenate([rows] * (levels // 16), axis=0) == wanted
    return jnp.where(hits, jnp.ones((), jnp.bfloat16), jnp.zeros((), jnp.bfloat16)).astype(jnp.float8_e4m3fn)


def count_kernel(earlier, ids_ref, *refs):
    hits_ref, code_ref = refs[earlier:]
    samples = hits_ref.shape[1]
    highs = hits_ref.shape[2] // LOW
    ids = ids_ref[0]
    member = lax.broadcasted_iota(jnp.int32, ids.shape, 1) // SLOTS
    code_ref[0] = ((ids >> 7) * GROUP + member).astype(jnp.float32)
    code_ref[1] = (ids & (LOW - 1)).astype(jnp.float32)

    def add_groups(step, unused):
        first = pl.multiple_of(step * 8, 8)
        high_codes = code_ref[0, pl.ds(first, 8), :]
        low_codes = code_ref[1, pl.ds(first, 8), :]
        for pair in range(4):
            products = []
            for row in (2 * pair, 2 * pair + 1):
                high_hits = one_hot(high_codes[row : row + 1], highs * GROUP)
                low_hits = one_hot(low_codes[row : row + 1], LOW)
                products.append(right_product(high_hits, low_hits))
            start = pl.multiple_of(step * 8 * GROUP + pair * 2 * GROUP, 2 * GROUP)
            for high in range(highs):
                part = slice(high * GROUP, (high + 1) * GROUP)
                tile = jnp.concatenate([products[0][part], products[1][part]], axis=0)
                hits_ref[0, pl.ds(start, 2 * GROUP), high * LOW : (high + 1) * LOW] = tile.astype(
                    jnp.bfloat16
                )
        return unused

    lax.fori_loop(0, samples // (8 * GROUP), add_groups, 0)


def count(ids, rows, pieces):
    features, groups, slots = ids.shape
    samples = groups * GROUP
    cuts = [features * piece // pieces for piece in range(pieces + 1)]
    hits = None
    for first, last in zip(cuts[:-1], cuts[1:]):
        earlier = [] if hits is None else [hits]
        hits = pl.pallas_call(
            functools.partial(count_kernel, len(earlier)),
            grid=(last - first,),
            in_specs=[pl.BlockSpec((1, groups, slots), functools.partial(shifted_block, first))]
            + [pl.BlockSpec(memory_space=pl.ANY)] * len(earlier),
            out_specs=pl.BlockSpec((1, samples, rows), functools.partial(shifted_block, first)),
            out_shape=jax.ShapeDtypeStruct((features, samples, rows), jnp.bfloat16),
            input_output_aliases={1: 0} if earlier else {},
            scratch_shapes=[pltpu.VMEM((2, groups, slots), jnp.float32)],
            compiler_params=pltpu.CompilerParams(vmem_limit_bytes=VMEM_BYTES),
            cost_estimate=pl.CostEstimate(flops=1, bytes_accessed=1, transcendentals=0),
        )(ids, *earlier)
    return hits


def shifted_block(first, feature):
    return (feature + first, 0, 0)


def feature_counts(counts_ref, feature):
    lanes = lax.broadcasted_iota(jnp.int32, counts_ref.shape, 1)
    return jnp.sum(jnp.where(lanes == feature, counts_ref[...], 0.0), axis=1, keepdims=True)


def pool_kernel(
    place_ref, hits_ref, own_a, other_a, own_b, other_b, counts_ref, dense_ref, anchor_ref, table_ref, *, keys, half
):
    feature = pl.program_id(0)
    features = pl.num_programs(0) - 1
    mine = place_ref[0]
    member = place_ref[1]
    group = table_ref.shape[0]

    def assemble(own_ref, other_ref, order):
        for position, key in enumerate(order):
            for step in range(group):
                row = lax.rem(member + group - step, group)
                table_ref[row, mine ^ key] = own_ref[position, step, 0]
                table_ref[row, mine ^ (key ^ 1)] = other_ref[position, step, 0]

    @pl.when(feature < half)
    def _():
        assemble(own_a, other_a, keys[0])

    @pl.when((feature >= half) & (feature < features))
    def _():
        assemble(own_b, other_b, keys[1])

    @pl.when(feature < features)
    def _():
        table = table_ref[...].reshape(-1, table_ref.shape[-1])
        anchor_ref[...] = product(hits_ref[0], table) / feature_counts(counts_ref, feature)

    @pl.when(feature == features)
    def _():
        anchor_ref[...] = dense_ref[...]


def pool(hits, first_half, second_half, keys, count_float, dense_input):
    features, samples, rows = hits.shape
    last = features - 1
    half = first_half[0].shape[2]
    halves, group, unused, part, width = first_half[0].shape
    block = (halves, group, 1, part, width)
    low_block = pl.BlockSpec(block, lambda f, place: (0, 0, jnp.minimum(f, half - 1), 0, 0))
    high_block = pl.BlockSpec(block, lambda f, place: (0, 0, jnp.clip(f - half, 0, last - half), 0, 0))
    place = jnp.stack([lax.axis_index("rep"), lax.axis_index("grp")]).astype(jnp.int32)
    return pl.pallas_call(
        functools.partial(pool_kernel, keys=keys, half=half),
        grid_spec=pltpu.PrefetchScalarGridSpec(
            num_scalar_prefetch=1,
            grid=(features + 1,),
            in_specs=[
                pl.BlockSpec((1, samples, rows), lambda f, place: (jnp.minimum(f, last), 0, 0)),
                low_block,
                low_block,
                high_block,
                high_block,
                pl.BlockSpec((samples, features), lambda f, place: (0, 0)),
                pl.BlockSpec((samples, width), lambda f, place: (0, 0)),
            ],
            out_specs=pl.BlockSpec((samples, width), lambda f, place: (0, f)),
            scratch_shapes=[pltpu.VMEM((group, 2 * halves, part, width), jnp.bfloat16)],
        ),
        out_shape=jax.ShapeDtypeStruct((samples, (features + 1) * width), jnp.float32),
        compiler_params=pltpu.CompilerParams(vmem_limit_bytes=VMEM_BYTES),
        cost_estimate=pl.CostEstimate(flops=1, bytes_accessed=1, transcendentals=0),
    )(place, hits, *first_half, *second_half, count_float, dense_input)


def cross_forward_kernel(
    anchor_in, down_ref, up_ref, bias_ref, low_ref, narrow_ref, last_ref, anchor_ref, stream_ref, sum_ref
):
    layer, phase, block = pl.program_id(0), pl.program_id(1), pl.program_id(2)
    layers = pl.num_programs(0)

    @pl.when((layer == 0) & (phase == 0))
    def _():
        anchor_ref[block] = anchor_in[...]
        stream_ref[block] = anchor_in[...]

    @pl.when(phase == 0)
    def _():
        low = stream_ref[block].astype(jnp.bfloat16)
        low_ref[0] = low
        part = product(low, down_ref[0])

        @pl.when(block == 0)
        def _():
            sum_ref[...] = part

        @pl.when(block > 0)
        def _():
            sum_ref[...] += part

    @pl.when((phase == 1) & (block == 0))
    def _():
        narrow_ref[0] = sum_ref[...].astype(jnp.bfloat16)

    @pl.when(phase == 1)
    def _():
        factor = product(narrow_ref[0], up_ref[0]) + bias_ref[0]
        stream = anchor_ref[block] * factor + stream_ref[block]
        stream_ref[block] = stream

        @pl.when(layer == layers - 1)
        def _():
            last_ref[...] = stream.astype(jnp.bfloat16)


def cross_forward(anchor, down, up, bias):
    samples, width = anchor.shape
    layers, unused, rank = down.shape
    blocks = 3
    piece = width // blocks
    final = blocks - 1
    return pl.pallas_call(
        cross_forward_kernel,
        grid=(layers, 2, blocks),
        in_specs=[
            pl.BlockSpec((samples, piece), lambda l, p, j: (0, jnp.where((l == 0) & (p == 0), j, final))),
            pl.BlockSpec((1, piece, rank), lambda l, p, j: (l, jnp.where(p == 0, j, final), 0)),
            pl.BlockSpec((1, rank, piece), lambda l, p, j: (l, 0, jnp.where(p == 1, j, 0))),
            pl.BlockSpec((1, 1, piece), lambda l, p, j: (l, 0, jnp.where(p == 1, j, 0))),
        ],
        out_specs=[
            pl.BlockSpec((1, samples, piece), lambda l, p, j: (l, 0, jnp.where(p == 0, j, final))),
            pl.BlockSpec((1, samples, rank), lambda l, p, j: (l, 0, 0)),
            pl.BlockSpec((samples, piece), lambda l, p, j: (0, jnp.where((l == layers - 1) & (p == 1), j, 0))),
        ],
        out_shape=[
            jax.ShapeDtypeStruct((layers, samples, width), jnp.bfloat16),
            jax.ShapeDtypeStruct((layers, samples, rank), jnp.bfloat16),
            jax.ShapeDtypeStruct((samples, width), jnp.bfloat16),
        ],
        scratch_shapes=[
            pltpu.VMEM((blocks, samples, piece), jnp.float32),
            pltpu.VMEM((blocks, samples, piece), jnp.float32),
            pltpu.VMEM((samples, rank), jnp.float32),
        ],
        compiler_params=pltpu.CompilerParams(vmem_limit_bytes=VMEM_BYTES),
        cost_estimate=pl.CostEstimate(flops=1, bytes_accessed=1, transcendentals=0),
    )(anchor, down, up, bias.reshape(layers, 1, width))


def head_kernel(
    input_ref,
    one_ref,
    late_ref,
    bias_one,
    bias_two,
    bias_three,
    head_ref,
    head_bias,
    target_ref,
    loss_ref,
    grad_head,
    grad_head_bias,
    grad_bias_one,
    grad_bias_two,
    grad_bias_three,
    grad_one,
    grad_late,
    grad_stream,
    sum_ref,
    back_ref,
    *,
    total
):
    step = pl.program_id(0)
    blocks = pl.num_programs(0) // 2

    @pl.when(step < blocks)
    def _():
        part = product(input_ref[...], one_ref[...])

        @pl.when(step == 0)
        def _():
            sum_ref[...] = part

        @pl.when(step > 0)
        def _():
            sum_ref[...] += part

    @pl.when(step == blocks)
    def _():
        pre_one = sum_ref[...] + bias_one[...]
        in_two = jax.nn.silu(pre_one).astype(jnp.bfloat16)
        two = late_ref[:, :H2]
        three = late_ref[:, H2:]
        pre_two = product(in_two, two) + bias_two[...]
        in_three = jax.nn.silu(pre_two).astype(jnp.bfloat16)
        pre_three = product(in_three, three) + bias_three[...]
        top = jax.nn.silu(pre_three)
        head = head_ref[...]
        target = target_ref[...]
        logit = jnp.sum(top * head, axis=1, keepdims=True) + head_bias[...]
        losses = jnp.maximum(logit, 0.0) + jnp.log1p(jnp.exp(-jnp.abs(logit))) - target * logit
        loss_ref[...] = jnp.sum(losses, axis=0, keepdims=True)
        grad_logit = (jax.nn.sigmoid(logit) - target) / total
        grad_head[...] = jnp.sum(grad_logit * top, axis=0, keepdims=True)
        grad_head_bias[...] = jnp.sum(grad_logit, axis=0, keepdims=True)
        back = (grad_logit * head * silu_slope(pre_three)).astype(jnp.bfloat16)
        grad_bias_three[...] = jnp.sum(back.astype(jnp.float32), axis=0, keepdims=True)
        grad_late[:, H2:] = left_product(in_three, back).astype(jnp.bfloat16)
        back = (right_product(back, three) * silu_slope(pre_two)).astype(jnp.bfloat16)
        grad_bias_two[...] = jnp.sum(back.astype(jnp.float32), axis=0, keepdims=True)
        grad_late[:, :H2] = left_product(in_two, back).astype(jnp.bfloat16)
        back = (right_product(back, two) * silu_slope(pre_one)).astype(jnp.bfloat16)
        grad_bias_one[...] = jnp.sum(back.astype(jnp.float32), axis=0, keepdims=True)
        back_ref[...] = back

    @pl.when(step >= blocks)
    def _():
        grad_one[...] = left_product(input_ref[...], back_ref[...]).astype(jnp.bfloat16)
        grad_stream[...] = right_product(back_ref[...], one_ref[...])


def head(inputs, one, late, biases, head_weight, head_bias, target, total):
    samples, width = inputs.shape
    blocks = 3
    piece = width // blocks

    def whole(shape):
        return pl.BlockSpec(shape, lambda s: (0,) * len(shape))

    rows = [bias.reshape(1, -1) for bias in biases] + [head_weight.reshape(1, -1), head_bias.reshape(1, 1)]
    small = [(1, 1), (1, H3), (1, 1), (1, H1), (1, H2), (1, H3)]
    return pl.pallas_call(
        functools.partial(head_kernel, total=total),
        grid=(2 * blocks,),
        in_specs=[
            pl.BlockSpec((samples, piece), lambda s: (0, lax.rem(s, blocks))),
            pl.BlockSpec((piece, H1), lambda s: (lax.rem(s, blocks), 0)),
            whole(late.shape),
        ]
        + [whole(row.shape) for row in rows]
        + [whole((samples, 1))],
        out_specs=[whole(shape) for shape in small]
        + [
            pl.BlockSpec((piece, H1), lambda s: (jnp.maximum(s - blocks, 0), 0)),
            whole(late.shape),
            pl.BlockSpec((samples, piece), lambda s: (0, jnp.maximum(s - blocks, 0))),
        ],
        out_shape=[jax.ShapeDtypeStruct(shape, jnp.float32) for shape in small]
        + [
            jax.ShapeDtypeStruct(one.shape, jnp.bfloat16),
            jax.ShapeDtypeStruct(late.shape, jnp.bfloat16),
            jax.ShapeDtypeStruct((samples, width), jnp.float32),
        ],
        scratch_shapes=[pltpu.VMEM((samples, H1), jnp.float32), pltpu.VMEM((samples, H1), jnp.bfloat16)],
        compiler_params=pltpu.CompilerParams(vmem_limit_bytes=VMEM_BYTES),
        cost_estimate=pl.CostEstimate(flops=1, bytes_accessed=1, transcendentals=0),
    )(inputs, one, late, *rows, target)


def cross_backward_kernel(
    core_ref,
    anchor_in,
    grad_in,
    low_ref,
    narrow_ref,
    down_ref,
    up_ref,
    bias_ref,
    counts_ref,
    send_ref,
    keep_ref,
    grad_down,
    grad_bias,
    grad_summed,
    anchor_ref,
    stream_ref,
    total_ref,
    sum_ref,
    back_ref,
    both_ref,
):
    layer, phase, block = pl.program_id(0), pl.program_id(1), pl.program_id(2)
    layers = pl.num_programs(0)

    @pl.when((layer == 0) & (phase == 0))
    def _():
        anchor_ref[block] = anchor_in[...]
        stream_ref[block] = grad_in[...]
        total_ref[block] = jnp.zeros(grad_in.shape, jnp.float32)

    @pl.when(phase == 0)
    def _():
        grad_next = stream_ref[block]
        grad_factor = (anchor_ref[block] * grad_next).astype(jnp.bfloat16)
        grad_bias[0] = jnp.sum(grad_factor.astype(jnp.float32), axis=0, keepdims=True)
        narrow = narrow_ref[0]
        both_ref[...] = left_product(narrow, grad_factor).astype(jnp.bfloat16).reshape(both_ref.shape)
        core = core_ref[0]
        send_ref[0] = both_ref[:, 1 - core]
        keep_ref[0] = both_ref[:, core]
        factor = product(narrow, up_ref[0]) + bias_ref[0]
        total_ref[block] += factor * grad_next
        part = right_product(grad_factor, up_ref[0])

        @pl.when(block == 0)
        def _():
            sum_ref[...] = part

        @pl.when(block > 0)
        def _():
            sum_ref[...] += part

    @pl.when((phase == 1) & (block == 0))
    def _():
        back_ref[...] = sum_ref[...].astype(jnp.bfloat16)

    @pl.when(phase == 1)
    def _():
        back = back_ref[...]
        grad_down[0] = left_product(low_ref[0], back).astype(jnp.bfloat16)
        grad_stream = stream_ref[block] + right_product(back, down_ref[0])
        stream_ref[block] = grad_stream

        @pl.when(layer == layers - 1)
        def _():
            features = grad_stream.shape[1] // LOW
            total = total_ref[block] + grad_stream
            for index in range(features):
                counts = jnp.maximum(feature_counts(counts_ref, block * features + index), 1.0)
                part = slice(index * LOW, (index + 1) * LOW)
                grad_summed[:, part] = (total[:, part] / counts).astype(jnp.bfloat16)


def cross_backward(anchor, grad_stream, lows, narrows, down, up, bias, count_float, core, repeats):
    samples, width = anchor.shape
    layers, unused, rank = down.shape
    blocks = 3
    piece = width // blocks
    final = blocks - 1
    share = rank // repeats

    def first_pass(l, p, j, core):
        return (0, jnp.where((l == 0) & (p == 0), j, final))

    def up_block(l, p, j, core):
        return (layers - 1 - l, 0, jnp.where(p == 0, j, final))

    def low_block(l, p, j, core):
        return (layers - 1 - l, 0, jnp.where(p == 1, j, 0))

    def down_block(l, p, j, core):
        return (layers - 1 - l, jnp.where(p == 1, j, 0), 0)

    half = jax.ShapeDtypeStruct((layers, repeats // 2, share, width), jnp.bfloat16)
    half_spec = pl.BlockSpec(
        (1, repeats // 2, share, piece),
        lambda l, p, j, core: (layers - 1 - l, 0, 0, jnp.where(p == 0, j, final)),
    )
    return pl.pallas_call(
        cross_backward_kernel,
        grid_spec=pltpu.PrefetchScalarGridSpec(
            num_scalar_prefetch=1,
            grid=(layers, 2, blocks),
            in_specs=[
                pl.BlockSpec((samples, piece), first_pass),
                pl.BlockSpec((samples, piece), first_pass),
                pl.BlockSpec((1, samples, piece), low_block),
                pl.BlockSpec((1, samples, rank), lambda l, p, j, core: (layers - 1 - l, 0, 0)),
                pl.BlockSpec((1, piece, rank), down_block),
                pl.BlockSpec((1, rank, piece), up_block),
                pl.BlockSpec((1, 1, piece), up_block),
                pl.BlockSpec(count_float.shape, lambda l, p, j, core: (0, 0)),
            ],
            out_specs=[
                half_spec,
                half_spec,
                pl.BlockSpec((1, piece, rank), down_block),
                pl.BlockSpec((1, 1, piece), up_block),
                pl.BlockSpec(
                    (samples, piece),
                    lambda l, p, j, core: (0, jnp.where((l == layers - 1) & (p == 1), j, 0)),
                ),
            ],
            scratch_shapes=[
                pltpu.VMEM((blocks, samples, piece), jnp.float32),
                pltpu.VMEM((blocks, samples, piece), jnp.float32),
                pltpu.VMEM((blocks, samples, piece), jnp.float32),
                pltpu.VMEM((samples, rank), jnp.float32),
                pltpu.VMEM((samples, rank), jnp.bfloat16),
                pltpu.VMEM((repeats // 2, 2, share, piece), jnp.bfloat16),
            ],
        ),
        out_shape=[
            half,
            half,
            jax.ShapeDtypeStruct(down.shape, jnp.bfloat16),
            jax.ShapeDtypeStruct((layers, 1, width), jnp.float32),
            jax.ShapeDtypeStruct((samples, width), jnp.bfloat16),
        ],
        compiler_params=pltpu.CompilerParams(vmem_limit_bytes=VMEM_BYTES),
        cost_estimate=pl.CostEstimate(
            flops=10**12,
            bytes_accessed=layers * width * (8 * rank + 2 * samples) + 10 * samples * width,
            transcendentals=0,
        ),
    )(core, anchor, grad_stream, lows, narrows, down, up, bias.reshape(layers, 1, width), count_float)


def row_kernel(earlier, core_ref, hits_ref, grad_ref, *refs):
    send_ref, keep_ref, both_ref = refs[earlier:]
    both_ref[...] = left_product(hits_ref[0], grad_ref[...]).astype(jnp.bfloat16).reshape(both_ref.shape)
    core = core_ref[0]
    send_ref[0] = both_ref[:, 1 - core]
    keep_ref[0] = both_ref[:, core]


def row_gradient(hits, grad_summed, start, stop, group, core, pieces, hint):
    unused, samples, rows = hits.shape
    half = rows // group // 2
    shape = jax.ShapeDtypeStruct((stop - start, group, half, LOW), jnp.bfloat16)
    cuts = [start + (stop - start) * piece // pieces for piece in range(pieces + 1)]
    results = []
    for first, last in zip(cuts[:-1], cuts[1:]):
        spec = pl.BlockSpec((1, group, half, LOW), functools.partial(row_block, first - start))
        results = pl.pallas_call(
            functools.partial(row_kernel, len(results)),
            grid_spec=pltpu.PrefetchScalarGridSpec(
                num_scalar_prefetch=1,
                grid=(last - first,),
                in_specs=[
                    pl.BlockSpec((1, samples, rows), functools.partial(hits_block, first)),
                    pl.BlockSpec((samples, LOW), functools.partial(column_block, first)),
                ]
                + [pl.BlockSpec(memory_space=pl.ANY)] * len(results),
                out_specs=[spec, spec],
                scratch_shapes=[pltpu.VMEM((group, 2, half, LOW), jnp.bfloat16)],
            ),
            out_shape=[shape, shape],
            input_output_aliases={3: 0, 4: 1} if results else {},
            compiler_params=pltpu.CompilerParams(vmem_limit_bytes=VMEM_BYTES),
            cost_estimate=pl.CostEstimate(
                flops=hint,
                bytes_accessed=2 * (last - first) * rows * (samples + LOW),
                transcendentals=0,
            ),
        )(core, hits, grad_summed, *results)
    return results


def row_block(first, feature, core):
    return (feature + first, 0, 0, 0)


def hits_block(first, feature, core):
    return (feature + first, 0, 0)


def column_block(first, feature, core):
    return (0, feature + first)


def flip(value, bit):
    return lax.ppermute(value, "rep", [(i, i ^ bit) for i in range(lax.axis_size("rep"))])


def shift(value, step):
    size = lax.axis_size("grp")
    return lax.ppermute(value, "grp", [(i, (i + step) % size) for i in range(size)])


def across():
    return [1 << i for i in range(1, lax.axis_size("rep").bit_length() - 1)]


def gather_across(value, order):
    keys = [0]
    for bit in order:
        value = jnp.concatenate([value, flip(value, bit)], axis=0)
        keys = keys + [key ^ bit for key in keys]
    return value, keys


def place(value, keys, axis, index_of):
    mine = lax.axis_index("rep")
    extent = value.shape[axis + 1]
    shape = list(value.shape[1:])
    shape[axis] = extent * len(keys)
    whole = jnp.zeros(shape, value.dtype)
    for position, key in enumerate(keys):
        whole = lax.dynamic_update_slice_in_dim(whole, value[position], index_of(mine ^ key) * extent, axis)
    return whole


def after(value, earlier):
    return lax.optimization_barrier((value, earlier))[0]


class HalvingSum:
    def __init__(self, keep, received, bits, order, axis):
        self.keep, self.received = keep, received
        self.left, self.order, self.axis = list(bits), list(order), axis

    def step(self, *earlier):
        bit = self.order.pop(0)
        position = self.axis + self.left.index(bit)
        self.left.remove(bit)
        mine = (lax.axis_index("rep") // bit) % 2
        pair = after((self.keep, self.received), earlier)
        send, keep = (
            sum(lax.dynamic_index_in_dim(item, index, position, keepdims=False) for item in pair)
            for index in (1 - mine, mine)
        )
        self.keep, self.sent = keep, send
        self.received = flip(self.sent, bit)

    def result(self):
        return self.keep + self.received


class GroupSum:
    def __init__(self, *shares):
        self.size = lax.axis_size("grp")
        self.mine = lax.axis_index("grp")
        self.shares = shares

    def scatter(self, *earlier):
        chunks = [share.reshape(self.size, -1, LOW) for share in after(self.shares, earlier)]
        self.lengths = [chunk.shape[1] for chunk in chunks]
        sent = []
        for step in range(self.size):
            index = lax.rem(self.mine + step, self.size)
            parts = [lax.dynamic_index_in_dim(chunk, index, 0, keepdims=False) for chunk in chunks]
            sent.append(jnp.concatenate(parts, axis=0) if len(parts) > 1 else parts[0])
        self.sent = sent
        self.received = [shift(part, step) for step, part in enumerate(self.sent) if step]
        self.total = sum(part.astype(jnp.float32) for part in [self.sent[0]] + self.received).astype(sent[0].dtype)

    def gather(self, *earlier):
        self.sent = after(self.total, earlier)
        self.received = [shift(self.sent, step) for step in range(1, self.size)]

    def result(self):
        whole = jnp.zeros((self.size,) + self.total.shape, self.total.dtype)
        for step, part in enumerate([self.sent] + self.received):
            index = lax.rem(self.mine + self.size - step, self.size)
            whole = lax.dynamic_update_index_in_dim(whole, part, index, 0)
        results = []
        offset = 0
        for share, length in zip(self.shares, self.lengths):
            part = whole[:, offset : offset + length]
            results.append(part.reshape(share.shape).astype(jnp.float32))
            offset = offset + length
        return results


class SmallSum:
    def __init__(self, value):
        self.value, self.received = value, None
        self.left = [("rep", bit) for bit in [1] + across()]
        bit = 1
        while bit < lax.axis_size("grp"):
            self.left.append(("grp", bit))
            bit = 2 * bit

    def step(self):
        if self.received is not None:
            self.value = self.value + self.received
        axis, bit = self.left.pop(0)
        self.sent = self.value
        self.received = lax.ppermute(self.value, axis, [(i, i ^ bit) for i in range(lax.axis_size(axis))])

    def finish(self):
        while self.left:
            self.step()
        self.value = self.value + self.received


def adamw(weight, grad, first, second, rate):
    first = BETA_ONE * first + (1.0 - BETA_ONE) * grad
    second = BETA_TWO * second + (1.0 - BETA_TWO) * grad * grad
    corr_one = 1.0 - BETA_ONE**STEP
    corr_two = 1.0 - BETA_TWO**STEP
    moved = first / corr_one / (jnp.sqrt(second / corr_two) + EPSILON) + DECAY * weight
    return (weight - rate * moved, first, second)


def on_device(
    row_ids,
    bag_counts,
    labels,
    dense_input,
    tables,
    table_first,
    table_second,
    cross_down,
    down_first,
    down_second,
    cross_up,
    up_first,
    up_second,
    hidden_one,
    one_first,
    one_second,
    hidden_two,
    two_first,
    two_second,
    hidden_three,
    three_first,
    three_second,
    smalls,
    small_first,
    small_second,
):
    up_down = across()
    down_up = up_down[::-1]
    down_all = lax.all_gather(cross_down.astype(jnp.bfloat16), "rep", axis=1, tiled=True)
    up_all = lax.all_gather(cross_up.astype(jnp.bfloat16), "rep", axis=1, tiled=True)
    one_all = lax.all_gather(hidden_one.astype(jnp.bfloat16), "rep", axis=0, tiled=True)
    cross_bias, bias_one, bias_two, bias_three, head_weight, head_bias = split_smalls(smalls)
    group = lax.axis_size("grp")
    samples = row_ids.shape[0]
    repeats = lax.axis_size("rep")
    features, extent, width = tables.shape
    part = extent // repeats
    own_part = lax.dynamic_slice_in_dim(tables, lax.axis_index("rep") * part, part, axis=1)
    own_part = own_part.astype(jnp.bfloat16)
    own_parts = [own_part] + [shift(own_part, step) for step in range(1, group)]
    half = features // 2
    spans = ((0, half, up_down), (half, features, down_up))
    table_halves = []
    table_keys = []
    for first, last, order in spans:
        rows = jnp.stack([piece[first:last] for piece in own_parts])[None]
        rows, keys = gather_across(rows, order)
        table_halves.append((rows, flip(rows, 1)))
        table_keys.append(keys)
    late = jnp.concatenate([hidden_two, hidden_three], axis=1).astype(jnp.bfloat16)
    late_all = place(*gather_across(late[None], up_down + [1]), 0, lambda index: index)
    count_float = bag_counts.astype(jnp.float32)
    hits = count(slot_ids(row_ids, bag_counts), group * extent, 4)
    anchor = pool(hits, table_halves[0], table_halves[1], table_keys, count_float, dense_input)
    lows, narrows, in_one = cross_forward(anchor, down_all, up_all, cross_bias)
    total_samples = samples * lax.axis_size("rep") * group
    target = labels.astype(jnp.float32)[:, None]
    (
        loss_local,
        grad_head,
        grad_head_bias,
        bias_grad_one,
        bias_grad_two,
        bias_grad_three,
        grad_one,
        grad_late,
        grad_stream,
    ) = head(
        in_one, one_all, late_all, (bias_one, bias_two, bias_three), head_weight, head_bias, target, total_samples
    )
    share_one = lax.psum_scatter(grad_one, "rep", scatter_dimension=0, tiled=True)
    core = (lax.axis_index("rep") % 2).astype(jnp.int32).reshape(1)
    bits = up_down[::-1]
    late_blocks = grad_late.reshape((2,) * len(bits) + (2, -1) + grad_late.shape[1:])
    late_send, late_keep = (
        lax.dynamic_index_in_dim(late_blocks, index, len(bits), keepdims=False) for index in (1 - core[0], core[0])
    )
    late_sum = HalvingSum(late_keep, flip(late_send, 1), bits, up_down, 0)
    late_sum.step()
    send_up, keep_up, grad_down, bias_grads, grad_summed = cross_backward(
        anchor,
        after(grad_stream, late_sum.sent),
        lows,
        narrows,
        down_all,
        up_all,
        cross_bias,
        count_float,
        core,
        repeats,
    )
    share_down = lax.psum_scatter(grad_down, "rep", scatter_dimension=1, tiled=True)
    received_up = flip(send_up, 1)
    share_rows = keep_up.shape[2] // 2
    shape = (CROSS,) + (2,) * len(bits) + (2, share_rows, D_IN)
    up_sums = [
        HalvingSum(
            lax.index_in_dim(keep_up.reshape(shape), index, len(bits) + 1, keepdims=False),
            lax.index_in_dim(received_up.reshape(shape), index, len(bits) + 1, keepdims=False),
            bits,
            order,
            1,
        )
        for index, order in ((0, up_down), (1, down_up))
    ]
    small_grad = jnp.concatenate(
        [
            item.reshape(-1)
            for item in (
                bias_grads,
                bias_grad_one,
                bias_grad_two,
                bias_grad_three,
                grad_head,
                grad_head_bias,
                loss_local,
            )
        ]
    )
    up_p, up_q = up_sums
    row_sums = []
    grad_rows = after(grad_summed, late_sum.received)
    for first, last, order in spans:
        send, keep = row_gradient(hits, grad_rows, first, last, group, core, 2, 10**12 if first == 0 else HINT)
        shape = (last - first, group) + (2,) * len(bits) + (part, width)
        row_sums.append(HalvingSum(keep.reshape(shape), flip(send, 1).reshape(shape), bits, order, 2))
        if len(row_sums) == 1:
            for step in bits[1:]:
                late_sum.step(keep)
            for item in up_sums:
                item.step(late_sum.sent)
            grad_rows = after(grad_rows, [item.sent for item in up_sums] + [late_sum.sent, share_one])
    row_p, row_q = row_sums
    one_total = GroupSum(share_one, late_sum.result())
    one_total.scatter(keep)
    first_sent = list(one_total.sent)
    for step in bits[1:]:
        for item in up_sums:
            item.step(*first_sent)
    one_total.gather(*[item.sent for item in up_sums])
    for item in row_sums:
        item.step(up_p.sent, up_q.sent)
    share_up = jnp.concatenate([item.result() for item in up_sums], axis=1)
    share_up, share_down = lax.psum((share_up, share_down), "grp")
    for step in bits[1:]:
        for item in row_sums:
            item.step(up_p.received, up_q.received)
    row_parts = [item.result() for item in row_sums]
    row_total = GroupSum(jnp.concatenate(row_parts, axis=0).transpose(1, 0, 2, 3))
    row_total.scatter(share_up, share_down)
    small = SmallSum(after(small_grad, row_total.sent))
    small.finish()
    row_share = row_total.total.reshape(features, part, width)
    share_one, share_late = one_total.result()
    share_up, share_down = share_up.astype(jnp.float32), share_down.astype(jnp.float32)
    share_two, share_three = share_late[:, :H2], share_late[:, H2:]
    small_sum, loss_sum = small.value[:-1], small.value[-1]
    new_one, new_one_first, new_one_second = adamw(
        hidden_one, share_one, one_first, one_second, D_IN ** (-0.5)
    )
    new_two, new_two_first, new_two_second = adamw(
        hidden_two, share_two, two_first, two_second, H1 ** (-0.5)
    )
    new_three, new_three_first, new_three_second = adamw(
        hidden_three, share_three, three_first, three_second, H2 ** (-0.5)
    )
    table_grads = []
    for first, last, order in spans:
        value, keys = gather_across(row_share[None, first:last], order + [1])
        table_grads.append(place(value, keys, 1, lambda index: (index % 2) * (repeats // 2) + index // 2))
    table_grad = jnp.concatenate(table_grads, axis=0).astype(jnp.float32)
    new_up, new_up_first, new_up_second = adamw(
        cross_up, share_up, up_first, up_second, RANK ** (-0.5)
    )
    new_tables, new_table_first, new_table_second = adamw(
        tables, table_grad, table_first, table_second, 1.0
    )
    new_down, new_down_first, new_down_second = adamw(
        cross_down, share_down, down_first, down_second, D_IN ** (-0.5)
    )
    new_smalls, new_small_first, new_small_second = adamw(
        smalls, small_sum, small_first, small_second, 0.1
    )
    return (
        loss_sum,
        new_tables,
        new_table_first,
        new_table_second,
        new_down,
        new_down_first,
        new_down_second,
        new_up,
        new_up_first,
        new_up_second,
        new_one,
        new_one_first,
        new_one_second,
        new_two,
        new_two_first,
        new_two_second,
        new_three,
        new_three_first,
        new_three_second,
        new_smalls,
        new_small_first,
        new_small_second,
    )


def solution(mesh):
    return jax.shard_map(
        on_device,
        mesh=mesh,
        in_specs=(
            P(("rep", "grp"), None, None),
            P(("rep", "grp"), None),
            P(("rep", "grp")),
            P(("rep", "grp"), None),
            P(None, "grp", None),
            P(None, "grp", None),
            P(None, "grp", None),
            P(None, "rep", None),
            P(None, "rep", None),
            P(None, "rep", None),
            P(None, "rep", None),
            P(None, "rep", None),
            P(None, "rep", None),
            P("rep", None),
            P("rep", None),
            P("rep", None),
            P("rep", None),
            P("rep", None),
            P("rep", None),
            P("rep", None),
            P("rep", None),
            P("rep", None),
            P(),
            P(),
            P(),
        ),
        out_specs=(
            P(),
            P(None, "grp", None),
            P(None, "grp", None),
            P(None, "grp", None),
            P(None, "rep", None),
            P(None, "rep", None),
            P(None, "rep", None),
            P(None, "rep", None),
            P(None, "rep", None),
            P(None, "rep", None),
            P("rep", None),
            P("rep", None),
            P("rep", None),
            P("rep", None),
            P("rep", None),
            P("rep", None),
            P("rep", None),
            P("rep", None),
            P("rep", None),
            P(),
            P(),
            P(),
        ),
        check_vma=False,
    )
```

```python
import functools

import jax
import jax.numpy as jnp
from jax import lax
from jax.experimental import pallas as pl
from jax.experimental.pallas import tpu as pltpu
from jax.sharding import PartitionSpec as P

D_IN = 3456
RANK = 512
CROSS = 3
H1 = 1024
H2 = 1024
H3 = 512
STEP = 10
GROUP = 8
SLOTS = 32
LOW = 128
PAIR = 2
VMEM_BYTES = 60 * 2**20
HINT = 10**10


BETA_ONE = 0.9
BETA_TWO = 0.999
EPSILON = 1e-12
DECAY = 0.01


def split_smalls(smalls):
    extents = [CROSS * D_IN, H1, H2, H3, H3, 1]
    pieces = []
    offset = 0
    for extent in extents:
        pieces.append(smalls[offset : offset + extent])
        offset = offset + extent
    return (pieces[0].reshape(CROSS, D_IN), pieces[1], pieces[2], pieces[3], pieces[4], pieces[5])


def product(left, right):
    return jnp.dot(left, right, preferred_element_type=jnp.float32)


def left_product(left, right):
    return lax.dot_general(
        left, right, (((0,), (0,)), ((), ())), preferred_element_type=jnp.float32
    )


def right_product(left, right):
    return lax.dot_general(
        left, right, (((1,), (1,)), ((), ())), preferred_element_type=jnp.float32
    )


def silu_slope(value):
    logistic = jax.nn.sigmoid(value)
    return logistic * (1.0 + value * (1.0 - logistic))


def slot_ids(row_ids, bag_counts):
    samples, features, slots = row_ids.shape
    live = lax.broadcasted_iota(jnp.int32, row_ids.shape, 2) < bag_counts[:, :, None]
    ids = jnp.pad(jnp.where(live, row_ids, -1), ((0, 0), (0, 0), (0, SLOTS - slots)), constant_values=-1)
    return ids.transpose(1, 0, 2).reshape(features, samples // GROUP, GROUP * SLOTS)


def one_hot(codes, levels):
    rows = jnp.broadcast_to(codes, (16, codes.shape[1])).astype(jnp.bfloat16)
    wanted = lax.broadcasted_iota(jnp.int32, (levels, codes.shape[1]), 0).astype(jnp.float32).astype(jnp.bfloat16)
    hits = jnp.concatenate([rows] * (levels // 16), axis=0) == wanted
    return jnp.where(hits, jnp.ones((), jnp.bfloat16), jnp.zeros((), jnp.bfloat16)).astype(jnp.float8_e4m3fn)


def count_kernel(earlier, ids_ref, *refs):
    hits_ref, code_ref = refs[earlier:]
    samples = hits_ref.shape[1]
    highs = hits_ref.shape[2] // LOW
    ids = ids_ref[0]
    member = lax.broadcasted_iota(jnp.int32, ids.shape, 1) // SLOTS
    code_ref[0] = ((ids >> 7) * GROUP + member).astype(jnp.float32)
    code_ref[1] = (ids & (LOW - 1)).astype(jnp.float32)

    def add_groups(step, unused):
        first = pl.multiple_of(step * 8, 8)
        high_codes = code_ref[0, pl.ds(first, 8), :]
        low_codes = code_ref[1, pl.ds(first, 8), :]
        for pair in range(4):
            products = []
            for row in (2 * pair, 2 * pair + 1):
                high_hits = one_hot(high_codes[row : row + 1], highs * GROUP)
                low_hits = one_hot(low_codes[row : row + 1], LOW)
                products.append(right_product(high_hits, low_hits))
            start = pl.multiple_of(step * 8 * GROUP + pair * 2 * GROUP, 2 * GROUP)
            for high in range(highs):
                part = slice(high * GROUP, (high + 1) * GROUP)
                tile = jnp.concatenate([products[0][part], products[1][part]], axis=0)
                hits_ref[0, pl.ds(start, 2 * GROUP), high * LOW : (high + 1) * LOW] = tile.astype(
                    jnp.bfloat16
                )
        return unused

    lax.fori_loop(0, samples // (8 * GROUP), add_groups, 0)


def count(ids, rows, pieces):
    features, groups, slots = ids.shape
    samples = groups * GROUP
    cuts = [features * piece // pieces for piece in range(pieces + 1)]
    hits = None
    for first, last in zip(cuts[:-1], cuts[1:]):
        earlier = [] if hits is None else [hits]
        hits = pl.pallas_call(
            functools.partial(count_kernel, len(earlier)),
            grid=(last - first,),
            in_specs=[pl.BlockSpec((1, groups, slots), functools.partial(shifted_block, first))]
            + [pl.BlockSpec(memory_space=pl.ANY)] * len(earlier),
            out_specs=pl.BlockSpec((1, samples, rows), functools.partial(shifted_block, first)),
            out_shape=jax.ShapeDtypeStruct((features, samples, rows), jnp.bfloat16),
            input_output_aliases={1: 0} if earlier else {},
            scratch_shapes=[pltpu.VMEM((2, groups, slots), jnp.float32)],
            compiler_params=pltpu.CompilerParams(vmem_limit_bytes=VMEM_BYTES),
            cost_estimate=pl.CostEstimate(flops=1, bytes_accessed=1, transcendentals=0),
        )(ids, *earlier)
    return hits


def shifted_block(first, feature):
    return (feature + first, 0, 0)


def feature_counts(counts_ref, feature):
    lanes = lax.broadcasted_iota(jnp.int32, counts_ref.shape, 1)
    return jnp.sum(jnp.where(lanes == feature, counts_ref[...], 0.0), axis=1, keepdims=True)


def pool_kernel(
    place_ref, hits_ref, own_a, other_a, own_b, other_b, counts_ref, dense_ref, anchor_ref, table_ref, *, keys, half
):
    feature = pl.program_id(0)
    features = pl.num_programs(0) - 1
    mine = place_ref[0]
    member = place_ref[1]
    group = table_ref.shape[0]

    def assemble(own_ref, other_ref, order):
        for position, key in enumerate(order):
            for step in range(group):
                row = lax.rem(member + group - step, group)
                table_ref[row, mine ^ key] = own_ref[position, step, 0]
                table_ref[row, mine ^ (key ^ 1)] = other_ref[position, step, 0]

    @pl.when(feature < half)
    def _():
        assemble(own_a, other_a, keys[0])

    @pl.when((feature >= half) & (feature < features))
    def _():
        assemble(own_b, other_b, keys[1])

    @pl.when(feature < features)
    def _():
        table = table_ref[...].reshape(-1, table_ref.shape[-1])
        anchor_ref[...] = product(hits_ref[0], table) / feature_counts(counts_ref, feature)

    @pl.when(feature == features)
    def _():
        anchor_ref[...] = dense_ref[...]


def pool(hits, first_half, second_half, keys, count_float, dense_input):
    features, samples, rows = hits.shape
    last = features - 1
    half = first_half[0].shape[2]
    halves, group, unused, part, width = first_half[0].shape
    block = (halves, group, 1, part, width)
    low_block = pl.BlockSpec(block, lambda f, place: (0, 0, jnp.minimum(f, half - 1), 0, 0))
    high_block = pl.BlockSpec(block, lambda f, place: (0, 0, jnp.clip(f - half, 0, last - half), 0, 0))
    place = jnp.stack([lax.axis_index("rep"), lax.axis_index("grp")]).astype(jnp.int32)
    return pl.pallas_call(
        functools.partial(pool_kernel, keys=keys, half=half),
        grid_spec=pltpu.PrefetchScalarGridSpec(
            num_scalar_prefetch=1,
            grid=(features + 1,),
            in_specs=[
                pl.BlockSpec((1, samples, rows), lambda f, place: (jnp.minimum(f, last), 0, 0)),
                low_block,
                low_block,
                high_block,
                high_block,
                pl.BlockSpec((samples, features), lambda f, place: (0, 0)),
                pl.BlockSpec((samples, width), lambda f, place: (0, 0)),
            ],
            out_specs=pl.BlockSpec((samples, width), lambda f, place: (0, f)),
            scratch_shapes=[pltpu.VMEM((group, 2 * halves, part, width), jnp.bfloat16)],
        ),
        out_shape=jax.ShapeDtypeStruct((samples, (features + 1) * width), jnp.float32),
        compiler_params=pltpu.CompilerParams(vmem_limit_bytes=VMEM_BYTES),
        cost_estimate=pl.CostEstimate(flops=1, bytes_accessed=1, transcendentals=0),
    )(place, hits, *first_half, *second_half, count_float, dense_input)


def cross_forward_kernel(
    anchor_in, down_ref, up_ref, bias_ref, low_ref, narrow_ref, last_ref, anchor_ref, stream_ref, sum_ref
):
    layer, phase, block = pl.program_id(0), pl.program_id(1), pl.program_id(2)
    layers = pl.num_programs(0)

    @pl.when((layer == 0) & (phase == 0))
    def _():
        anchor_ref[block] = anchor_in[...]
        stream_ref[block] = anchor_in[...]

    @pl.when(phase == 0)
    def _():
        low = stream_ref[block].astype(jnp.bfloat16)
        low_ref[0] = low
        part = product(low, down_ref[0])

        @pl.when(block == 0)
        def _():
            sum_ref[...] = part

        @pl.when(block > 0)
        def _():
            sum_ref[...] += part

    @pl.when((phase == 1) & (block == 0))
    def _():
        narrow_ref[0] = sum_ref[...].astype(jnp.bfloat16)

    @pl.when(phase == 1)
    def _():
        factor = product(narrow_ref[0], up_ref[0]) + bias_ref[0]
        stream = anchor_ref[block] * factor + stream_ref[block]
        stream_ref[block] = stream

        @pl.when(layer == layers - 1)
        def _():
            last_ref[...] = stream.astype(jnp.bfloat16)


def cross_forward(anchor, down, up, bias):
    samples, width = anchor.shape
    layers, unused, rank = down.shape
    blocks = 3
    piece = width // blocks
    final = blocks - 1
    return pl.pallas_call(
        cross_forward_kernel,
        grid=(layers, 2, blocks),
        in_specs=[
            pl.BlockSpec((samples, piece), lambda l, p, j: (0, jnp.where((l == 0) & (p == 0), j, final))),
            pl.BlockSpec((1, piece, rank), lambda l, p, j: (l, jnp.where(p == 0, j, final), 0)),
            pl.BlockSpec((1, rank, piece), lambda l, p, j: (l, 0, jnp.where(p == 1, j, 0))),
            pl.BlockSpec((1, 1, piece), lambda l, p, j: (l, 0, jnp.where(p == 1, j, 0))),
        ],
        out_specs=[
            pl.BlockSpec((1, samples, piece), lambda l, p, j: (l, 0, jnp.where(p == 0, j, final))),
            pl.BlockSpec((1, samples, rank), lambda l, p, j: (l, 0, 0)),
            pl.BlockSpec((samples, piece), lambda l, p, j: (0, jnp.where((l == layers - 1) & (p == 1), j, 0))),
        ],
        out_shape=[
            jax.ShapeDtypeStruct((layers, samples, width), jnp.bfloat16),
            jax.ShapeDtypeStruct((layers, samples, rank), jnp.bfloat16),
            jax.ShapeDtypeStruct((samples, width), jnp.bfloat16),
        ],
        scratch_shapes=[
            pltpu.VMEM((blocks, samples, piece), jnp.float32),
            pltpu.VMEM((blocks, samples, piece), jnp.float32),
            pltpu.VMEM((samples, rank), jnp.float32),
        ],
        compiler_params=pltpu.CompilerParams(vmem_limit_bytes=VMEM_BYTES),
        cost_estimate=pl.CostEstimate(flops=1, bytes_accessed=1, transcendentals=0),
    )(anchor, down, up, bias.reshape(layers, 1, width))


def head_kernel(
    input_ref,
    one_ref,
    late_ref,
    bias_one,
    bias_two,
    bias_three,
    head_ref,
    head_bias,
    target_ref,
    loss_ref,
    grad_head,
    grad_head_bias,
    grad_bias_one,
    grad_bias_two,
    grad_bias_three,
    grad_one,
    grad_late,
    grad_stream,
    sum_ref,
    back_ref,
    *,
    total
):
    step = pl.program_id(0)
    blocks = pl.num_programs(0) // 2

    @pl.when(step < blocks)
    def _():
        part = product(input_ref[...], one_ref[...])

        @pl.when(step == 0)
        def _():
            sum_ref[...] = part

        @pl.when(step > 0)
        def _():
            sum_ref[...] += part

    @pl.when(step == blocks)
    def _():
        pre_one = sum_ref[...] + bias_one[...]
        in_two = jax.nn.silu(pre_one).astype(jnp.bfloat16)
        two = late_ref[:, :H2]
        three = late_ref[:, H2:]
        pre_two = product(in_two, two) + bias_two[...]
        in_three = jax.nn.silu(pre_two).astype(jnp.bfloat16)
        pre_three = product(in_three, three) + bias_three[...]
        top = jax.nn.silu(pre_three)
        head = head_ref[...]
        target = target_ref[...]
        logit = jnp.sum(top * head, axis=1, keepdims=True) + head_bias[...]
        losses = jnp.maximum(logit, 0.0) + jnp.log1p(jnp.exp(-jnp.abs(logit))) - target * logit
        loss_ref[...] = jnp.sum(losses, axis=0, keepdims=True)
        grad_logit = (jax.nn.sigmoid(logit) - target) / total
        grad_head[...] = jnp.sum(grad_logit * top, axis=0, keepdims=True)
        grad_head_bias[...] = jnp.sum(grad_logit, axis=0, keepdims=True)
        back = (grad_logit * head * silu_slope(pre_three)).astype(jnp.bfloat16)
        grad_bias_three[...] = jnp.sum(back.astype(jnp.float32), axis=0, keepdims=True)
        grad_late[:, H2:] = left_product(in_three, back).astype(jnp.bfloat16)
        back = (right_product(back, three) * silu_slope(pre_two)).astype(jnp.bfloat16)
        grad_bias_two[...] = jnp.sum(back.astype(jnp.float32), axis=0, keepdims=True)
        grad_late[:, :H2] = left_product(in_two, back).astype(jnp.bfloat16)
        back = (right_product(back, two) * silu_slope(pre_one)).astype(jnp.bfloat16)
        grad_bias_one[...] = jnp.sum(back.astype(jnp.float32), axis=0, keepdims=True)
        back_ref[...] = back

    @pl.when(step >= blocks)
    def _():
        grad_one[...] = left_product(input_ref[...], back_ref[...]).astype(jnp.bfloat16)
        grad_stream[...] = right_product(back_ref[...], one_ref[...])


def head(inputs, one, late, biases, head_weight, head_bias, target, total):
    samples, width = inputs.shape
    blocks = 3
    piece = width // blocks

    def whole(shape):
        return pl.BlockSpec(shape, lambda s: (0,) * len(shape))

    rows = [bias.reshape(1, -1) for bias in biases] + [head_weight.reshape(1, -1), head_bias.reshape(1, 1)]
    small = [(1, 1), (1, H3), (1, 1), (1, H1), (1, H2), (1, H3)]
    return pl.pallas_call(
        functools.partial(head_kernel, total=total),
        grid=(2 * blocks,),
        in_specs=[
            pl.BlockSpec((samples, piece), lambda s: (0, lax.rem(s, blocks))),
            pl.BlockSpec((piece, H1), lambda s: (lax.rem(s, blocks), 0)),
            whole(late.shape),
        ]
        + [whole(row.shape) for row in rows]
        + [whole((samples, 1))],
        out_specs=[whole(shape) for shape in small]
        + [
            pl.BlockSpec((piece, H1), lambda s: (jnp.maximum(s - blocks, 0), 0)),
            whole(late.shape),
            pl.BlockSpec((samples, piece), lambda s: (0, jnp.maximum(s - blocks, 0))),
        ],
        out_shape=[jax.ShapeDtypeStruct(shape, jnp.float32) for shape in small]
        + [
            jax.ShapeDtypeStruct(one.shape, jnp.bfloat16),
            jax.ShapeDtypeStruct(late.shape, jnp.bfloat16),
            jax.ShapeDtypeStruct((samples, width), jnp.float32),
        ],
        scratch_shapes=[pltpu.VMEM((samples, H1), jnp.float32), pltpu.VMEM((samples, H1), jnp.bfloat16)],
        compiler_params=pltpu.CompilerParams(vmem_limit_bytes=VMEM_BYTES),
        cost_estimate=pl.CostEstimate(flops=1, bytes_accessed=1, transcendentals=0),
    )(inputs, one, late, *rows, target)


def cross_backward_kernel(
    core_ref,
    anchor_in,
    grad_in,
    low_ref,
    narrow_ref,
    down_ref,
    up_ref,
    bias_ref,
    counts_ref,
    send_ref,
    keep_ref,
    grad_down,
    grad_bias,
    grad_summed,
    anchor_ref,
    stream_ref,
    total_ref,
    sum_ref,
    back_ref,
    both_ref,
):
    layer, phase, block = pl.program_id(0), pl.program_id(1), pl.program_id(2)
    layers = pl.num_programs(0)

    @pl.when((layer == 0) & (phase == 0))
    def _():
        anchor_ref[block] = anchor_in[...]
        stream_ref[block] = grad_in[...]
        total_ref[block] = jnp.zeros(grad_in.shape, jnp.float32)

    @pl.when(phase == 0)
    def _():
        grad_next = stream_ref[block]
        grad_factor = (anchor_ref[block] * grad_next).astype(jnp.bfloat16)
        grad_bias[0] = jnp.sum(grad_factor.astype(jnp.float32), axis=0, keepdims=True)
        narrow = narrow_ref[0]
        both_ref[...] = left_product(narrow, grad_factor).astype(jnp.bfloat16).reshape(both_ref.shape)
        core = core_ref[0]
        send_ref[0] = both_ref[:, 1 - core]
        keep_ref[0] = both_ref[:, core]
        factor = product(narrow, up_ref[0]) + bias_ref[0]
        total_ref[block] += factor * grad_next
        part = right_product(grad_factor, up_ref[0])

        @pl.when(block == 0)
        def _():
            sum_ref[...] = part

        @pl.when(block > 0)
        def _():
            sum_ref[...] += part

    @pl.when((phase == 1) & (block == 0))
    def _():
        back_ref[...] = sum_ref[...].astype(jnp.bfloat16)

    @pl.when(phase == 1)
    def _():
        back = back_ref[...]
        grad_down[0] = left_product(low_ref[0], back).astype(jnp.bfloat16)
        grad_stream = stream_ref[block] + right_product(back, down_ref[0])
        stream_ref[block] = grad_stream

        @pl.when(layer == layers - 1)
        def _():
            features = grad_stream.shape[1] // LOW
            total = total_ref[block] + grad_stream
            for index in range(features):
                counts = jnp.maximum(feature_counts(counts_ref, block * features + index), 1.0)
                part = slice(index * LOW, (index + 1) * LOW)
                grad_summed[:, part] = (total[:, part] / counts).astype(jnp.bfloat16)


def cross_backward(anchor, grad_stream, lows, narrows, down, up, bias, count_float, core, repeats):
    samples, width = anchor.shape
    layers, unused, rank = down.shape
    blocks = 3
    piece = width // blocks
    final = blocks - 1
    share = rank // repeats

    def first_pass(l, p, j, core):
        return (0, jnp.where((l == 0) & (p == 0), j, final))

    def up_block(l, p, j, core):
        return (layers - 1 - l, 0, jnp.where(p == 0, j, final))

    def low_block(l, p, j, core):
        return (layers - 1 - l, 0, jnp.where(p == 1, j, 0))

    def down_block(l, p, j, core):
        return (layers - 1 - l, jnp.where(p == 1, j, 0), 0)

    half = jax.ShapeDtypeStruct((layers, repeats // 2, share, width), jnp.bfloat16)
    half_spec = pl.BlockSpec(
        (1, repeats // 2, share, piece),
        lambda l, p, j, core: (layers - 1 - l, 0, 0, jnp.where(p == 0, j, final)),
    )
    return pl.pallas_call(
        cross_backward_kernel,
        grid_spec=pltpu.PrefetchScalarGridSpec(
            num_scalar_prefetch=1,
            grid=(layers, 2, blocks),
            in_specs=[
                pl.BlockSpec((samples, piece), first_pass),
                pl.BlockSpec((samples, piece), first_pass),
                pl.BlockSpec((1, samples, piece), low_block),
                pl.BlockSpec((1, samples, rank), lambda l, p, j, core: (layers - 1 - l, 0, 0)),
                pl.BlockSpec((1, piece, rank), down_block),
                pl.BlockSpec((1, rank, piece), up_block),
                pl.BlockSpec((1, 1, piece), up_block),
                pl.BlockSpec(count_float.shape, lambda l, p, j, core: (0, 0)),
            ],
            out_specs=[
                half_spec,
                half_spec,
                pl.BlockSpec((1, piece, rank), down_block),
                pl.BlockSpec((1, 1, piece), up_block),
                pl.BlockSpec(
                    (samples, piece),
                    lambda l, p, j, core: (0, jnp.where((l == layers - 1) & (p == 1), j, 0)),
                ),
            ],
            scratch_shapes=[
                pltpu.VMEM((blocks, samples, piece), jnp.float32),
                pltpu.VMEM((blocks, samples, piece), jnp.float32),
                pltpu.VMEM((blocks, samples, piece), jnp.float32),
                pltpu.VMEM((samples, rank), jnp.float32),
                pltpu.VMEM((samples, rank), jnp.bfloat16),
                pltpu.VMEM((repeats // 2, 2, share, piece), jnp.bfloat16),
            ],
        ),
        out_shape=[
            half,
            half,
            jax.ShapeDtypeStruct(down.shape, jnp.bfloat16),
            jax.ShapeDtypeStruct((layers, 1, width), jnp.float32),
            jax.ShapeDtypeStruct((samples, width), jnp.bfloat16),
        ],
        compiler_params=pltpu.CompilerParams(vmem_limit_bytes=VMEM_BYTES),
        cost_estimate=pl.CostEstimate(
            flops=10**12,
            bytes_accessed=layers * width * (8 * rank + 2 * samples) + 10 * samples * width,
            transcendentals=0,
        ),
    )(core, anchor, grad_stream, lows, narrows, down, up, bias.reshape(layers, 1, width), count_float)


def row_kernel(earlier, core_ref, hits_ref, grad_ref, *refs):
    send_ref, keep_ref, both_ref = refs[earlier:]
    core = core_ref[0]
    for index in range(PAIR):
        grad = grad_ref[:, index * LOW : (index + 1) * LOW]
        rows = left_product(grad, hits_ref[index]).T
        both_ref[index] = rows.astype(jnp.bfloat16).reshape(both_ref.shape[1:])
        send_ref[index] = both_ref[index, :, 1 - core]
        keep_ref[index] = both_ref[index, :, core]


def row_gradient(hits, grad_summed, start, stop, group, core, pieces, hint):
    unused, samples, rows = hits.shape
    half = rows // group // 2
    shape = jax.ShapeDtypeStruct((stop - start, group, half, LOW), jnp.bfloat16)
    cuts = [start + (stop - start) // PAIR * piece // pieces * PAIR for piece in range(pieces + 1)]
    results = []
    for first, last in zip(cuts[:-1], cuts[1:]):
        spec = pl.BlockSpec((PAIR, group, half, LOW), functools.partial(row_block, (first - start) // PAIR))
        results = pl.pallas_call(
            functools.partial(row_kernel, len(results)),
            grid_spec=pltpu.PrefetchScalarGridSpec(
                num_scalar_prefetch=1,
                grid=((last - first) // PAIR,),
                in_specs=[
                    pl.BlockSpec((PAIR, samples, rows), functools.partial(hits_block, first // PAIR)),
                    pl.BlockSpec((samples, PAIR * LOW), functools.partial(column_block, first // PAIR)),
                ]
                + [pl.BlockSpec(memory_space=pl.ANY)] * len(results),
                out_specs=[spec, spec],
                scratch_shapes=[pltpu.VMEM((PAIR, group, 2, half, LOW), jnp.bfloat16)],
            ),
            out_shape=[shape, shape],
            input_output_aliases={3: 0, 4: 1} if results else {},
            compiler_params=pltpu.CompilerParams(vmem_limit_bytes=VMEM_BYTES),
            cost_estimate=pl.CostEstimate(flops=hint, bytes_accessed=1, transcendentals=0),
        )(core, hits, grad_summed, *results)
    return results


def row_block(first, feature, core):
    return (feature + first, 0, 0, 0)


def hits_block(first, feature, core):
    return (feature + first, 0, 0)


def column_block(first, feature, core):
    return (0, feature + first)


def flip(value, bit):
    return lax.ppermute(value, "rep", [(i, i ^ bit) for i in range(lax.axis_size("rep"))])


def shift(value, step):
    size = lax.axis_size("grp")
    return lax.ppermute(value, "grp", [(i, (i + step) % size) for i in range(size)])


def across():
    return [1 << i for i in range(1, lax.axis_size("rep").bit_length() - 1)]


def gather_across(value, order):
    keys = [0]
    for bit in order:
        value = jnp.concatenate([value, flip(value, bit)], axis=0)
        keys = keys + [key ^ bit for key in keys]
    return value, keys


def place(value, keys, axis, index_of):
    mine = lax.axis_index("rep")
    extent = value.shape[axis + 1]
    shape = list(value.shape[1:])
    shape[axis] = extent * len(keys)
    whole = jnp.zeros(shape, value.dtype)
    for position, key in enumerate(keys):
        whole = lax.dynamic_update_slice_in_dim(whole, value[position], index_of(mine ^ key) * extent, axis)
    return whole


def after(value, earlier):
    return lax.optimization_barrier((value, earlier))[0]


class HalvingSum:
    def __init__(self, keep, received, bits, order, axis):
        self.keep, self.received = keep, received
        self.left, self.order, self.axis = list(bits), list(order), axis

    def step(self, *earlier):
        bit = self.order.pop(0)
        position = self.axis + self.left.index(bit)
        self.left.remove(bit)
        mine = (lax.axis_index("rep") // bit) % 2
        pair = after((self.keep, self.received), earlier)
        send, keep = (
            sum(lax.dynamic_index_in_dim(item, index, position, keepdims=False) for item in pair)
            for index in (1 - mine, mine)
        )
        self.keep, self.sent = keep, send
        self.received = flip(self.sent, bit)

    def result(self):
        return self.keep + self.received


class GroupSum:
    def __init__(self, *shares):
        self.size = lax.axis_size("grp")
        self.mine = lax.axis_index("grp")
        self.shares = shares

    def scatter(self, *earlier):
        chunks = [share.reshape(self.size, -1, LOW) for share in after(self.shares, earlier)]
        self.lengths = [chunk.shape[1] for chunk in chunks]
        sent = []
        for step in range(self.size):
            index = lax.rem(self.mine + step, self.size)
            parts = [lax.dynamic_index_in_dim(chunk, index, 0, keepdims=False) for chunk in chunks]
            sent.append(jnp.concatenate(parts, axis=0) if len(parts) > 1 else parts[0])
        self.sent = sent
        self.received = [shift(part, step) for step, part in enumerate(self.sent) if step]
        self.total = sum(part.astype(jnp.float32) for part in [self.sent[0]] + self.received).astype(sent[0].dtype)

    def gather(self, *earlier):
        self.sent = after(self.total, earlier)
        self.received = [shift(self.sent, step) for step in range(1, self.size)]

    def result(self):
        whole = jnp.zeros((self.size,) + self.total.shape, self.total.dtype)
        for step, part in enumerate([self.sent] + self.received):
            index = lax.rem(self.mine + self.size - step, self.size)
            whole = lax.dynamic_update_index_in_dim(whole, part, index, 0)
        results = []
        offset = 0
        for share, length in zip(self.shares, self.lengths):
            part = whole[:, offset : offset + length]
            results.append(part.reshape(share.shape).astype(jnp.float32))
            offset = offset + length
        return results


class SmallSum:
    def __init__(self, value):
        self.value, self.received = value, None
        self.left = [("rep", bit) for bit in [1] + across()]
        bit = 1
        while bit < lax.axis_size("grp"):
            self.left.append(("grp", bit))
            bit = 2 * bit

    def step(self):
        if self.received is not None:
            self.value = self.value + self.received
        axis, bit = self.left.pop(0)
        self.sent = self.value
        self.received = lax.ppermute(self.value, axis, [(i, i ^ bit) for i in range(lax.axis_size(axis))])

    def finish(self):
        while self.left:
            self.step()
        self.value = self.value + self.received


def adamw(weight, grad, first, second, rate):
    first = BETA_ONE * first + (1.0 - BETA_ONE) * grad
    second = BETA_TWO * second + (1.0 - BETA_TWO) * grad * grad
    corr_one = 1.0 - BETA_ONE**STEP
    corr_two = 1.0 - BETA_TWO**STEP
    moved = first / corr_one / (jnp.sqrt(second / corr_two) + EPSILON) + DECAY * weight
    return (weight - rate * moved, first, second)


def on_device(
    row_ids,
    bag_counts,
    labels,
    dense_input,
    tables,
    table_first,
    table_second,
    cross_down,
    down_first,
    down_second,
    cross_up,
    up_first,
    up_second,
    hidden_one,
    one_first,
    one_second,
    hidden_two,
    two_first,
    two_second,
    hidden_three,
    three_first,
    three_second,
    smalls,
    small_first,
    small_second,
):
    up_down = across()
    down_up = up_down[::-1]
    down_all = lax.all_gather(cross_down.astype(jnp.bfloat16), "rep", axis=1, tiled=True)
    up_all = lax.all_gather(cross_up.astype(jnp.bfloat16), "rep", axis=1, tiled=True)
    one_all = lax.all_gather(hidden_one.astype(jnp.bfloat16), "rep", axis=0, tiled=True)
    cross_bias, bias_one, bias_two, bias_three, head_weight, head_bias = split_smalls(smalls)
    group = lax.axis_size("grp")
    samples = row_ids.shape[0]
    repeats = lax.axis_size("rep")
    features, extent, width = tables.shape
    part = extent // repeats
    own_part = lax.dynamic_slice_in_dim(tables, lax.axis_index("rep") * part, part, axis=1)
    own_part = own_part.astype(jnp.bfloat16)
    own_parts = [own_part] + [shift(own_part, step) for step in range(1, group)]
    half = features // 2
    even = (half + 1) // PAIR * PAIR
    row_spans = ((0, even, up_down), (even, features, down_up))
    spans = ((0, half, up_down), (half, features, down_up))
    table_halves = []
    table_keys = []
    for first, last, order in spans:
        rows = jnp.stack([piece[first:last] for piece in own_parts])[None]
        rows, keys = gather_across(rows, order)
        table_halves.append((rows, flip(rows, 1)))
        table_keys.append(keys)
    late = jnp.concatenate([hidden_two, hidden_three], axis=1).astype(jnp.bfloat16)
    late_all = place(*gather_across(late[None], up_down + [1]), 0, lambda index: index)
    count_float = bag_counts.astype(jnp.float32)
    hits = count(slot_ids(row_ids, bag_counts), group * extent, 4)
    anchor = pool(hits, table_halves[0], table_halves[1], table_keys, count_float, dense_input)
    lows, narrows, in_one = cross_forward(anchor, down_all, up_all, cross_bias)
    total_samples = samples * lax.axis_size("rep") * group
    target = labels.astype(jnp.float32)[:, None]
    (
        loss_local,
        grad_head,
        grad_head_bias,
        bias_grad_one,
        bias_grad_two,
        bias_grad_three,
        grad_one,
        grad_late,
        grad_stream,
    ) = head(
        in_one, one_all, late_all, (bias_one, bias_two, bias_three), head_weight, head_bias, target, total_samples
    )
    share_one = lax.psum_scatter(grad_one, "rep", scatter_dimension=0, tiled=True)
    core = (lax.axis_index("rep") % 2).astype(jnp.int32).reshape(1)
    bits = up_down[::-1]
    late_blocks = grad_late.reshape((2,) * len(bits) + (2, -1) + grad_late.shape[1:])
    late_send, late_keep = (
        lax.dynamic_index_in_dim(late_blocks, index, len(bits), keepdims=False) for index in (1 - core[0], core[0])
    )
    late_sum = HalvingSum(late_keep, flip(late_send, 1), bits, up_down, 0)
    late_sum.step()
    send_up, keep_up, grad_down, bias_grads, grad_summed = cross_backward(
        anchor,
        after(grad_stream, late_sum.sent),
        lows,
        narrows,
        down_all,
        up_all,
        cross_bias,
        count_float,
        core,
        repeats,
    )
    share_down = lax.psum_scatter(grad_down, "rep", scatter_dimension=1, tiled=True)
    received_up = flip(send_up, 1)
    share_rows = keep_up.shape[2] // 2
    shape = (CROSS,) + (2,) * len(bits) + (2, share_rows, D_IN)
    up_sums = [
        HalvingSum(
            lax.index_in_dim(keep_up.reshape(shape), index, len(bits) + 1, keepdims=False),
            lax.index_in_dim(received_up.reshape(shape), index, len(bits) + 1, keepdims=False),
            bits,
            order,
            1,
        )
        for index, order in ((0, up_down), (1, down_up))
    ]
    small_grad = jnp.concatenate(
        [
            item.reshape(-1)
            for item in (
                bias_grads,
                bias_grad_one,
                bias_grad_two,
                bias_grad_three,
                grad_head,
                grad_head_bias,
                loss_local,
            )
        ]
    )
    up_p, up_q = up_sums
    row_sums = []
    grad_rows = after(grad_summed, late_sum.received)
    for first, last, order in row_spans:
        send, keep = row_gradient(hits, grad_rows, first, last, group, core, 1, 10**12 if first == 0 else HINT)
        shape = (last - first, group) + (2,) * len(bits) + (part, width)
        row_sums.append(HalvingSum(keep.reshape(shape), flip(send, 1).reshape(shape), bits, order, 2))
        if len(row_sums) == 1:
            for step in bits[1:]:
                late_sum.step(keep)
            for item in up_sums:
                item.step(late_sum.sent)
            grad_rows = after(grad_rows, [item.sent for item in up_sums] + [late_sum.sent, share_one])
    row_p, row_q = row_sums
    one_total = GroupSum(share_one, late_sum.result())
    one_total.scatter(keep, row_p.received)
    one_total.gather()
    for step in bits[1:]:
        for item in up_sums:
            item.step(one_total.sent)
    for item in row_sums:
        item.step(up_p.sent, up_q.sent)
    share_up = jnp.concatenate([item.result() for item in up_sums], axis=1)
    share_up, share_down = lax.psum((share_up, share_down), "grp")
    for step in bits[1:]:
        for item in row_sums:
            item.step(up_p.received, up_q.received)
    row_parts = [item.result() for item in row_sums]
    row_total = GroupSum(jnp.concatenate(row_parts, axis=0).transpose(1, 0, 2, 3))
    row_total.scatter(share_up, share_down)
    small = SmallSum(after(small_grad, row_total.sent))
    small.finish()
    row_share = row_total.total.reshape(features, part, width)
    share_one, share_late = one_total.result()
    share_up, share_down = share_up.astype(jnp.float32), share_down.astype(jnp.float32)
    share_two, share_three = share_late[:, :H2], share_late[:, H2:]
    small_sum, loss_sum = small.value[:-1], small.value[-1]
    new_one, new_one_first, new_one_second = adamw(
        hidden_one, share_one, one_first, one_second, D_IN ** (-0.5)
    )
    new_two, new_two_first, new_two_second = adamw(
        hidden_two, share_two, two_first, two_second, H1 ** (-0.5)
    )
    new_three, new_three_first, new_three_second = adamw(
        hidden_three, share_three, three_first, three_second, H2 ** (-0.5)
    )
    table_grads = []
    for first, last, order in spans:
        value, keys = gather_across(row_share[None, first:last], order + [1])
        table_grads.append(place(value, keys, 1, lambda index: (index % 2) * (repeats // 2) + index // 2))
    table_grad = jnp.concatenate(table_grads, axis=0).astype(jnp.float32)
    new_up, new_up_first, new_up_second = adamw(
        cross_up, share_up, up_first, up_second, RANK ** (-0.5)
    )
    new_tables, new_table_first, new_table_second = adamw(
        tables, table_grad, table_first, table_second, 1.0
    )
    new_down, new_down_first, new_down_second = adamw(
        cross_down, share_down, down_first, down_second, D_IN ** (-0.5)
    )
    new_smalls, new_small_first, new_small_second = adamw(
        smalls, small_sum, small_first, small_second, 0.1
    )
    return (
        loss_sum,
        new_tables,
        new_table_first,
        new_table_second,
        new_down,
        new_down_first,
        new_down_second,
        new_up,
        new_up_first,
        new_up_second,
        new_one,
        new_one_first,
        new_one_second,
        new_two,
        new_two_first,
        new_two_second,
        new_three,
        new_three_first,
        new_three_second,
        new_smalls,
        new_small_first,
        new_small_second,
    )


def solution(mesh):
    return jax.shard_map(
        on_device,
        mesh=mesh,
        in_specs=(
            P(("rep", "grp"), None, None),
            P(("rep", "grp"), None),
            P(("rep", "grp")),
            P(("rep", "grp"), None),
            P(None, "grp", None),
            P(None, "grp", None),
            P(None, "grp", None),
            P(None, "rep", None),
            P(None, "rep", None),
            P(None, "rep", None),
            P(None, "rep", None),
            P(None, "rep", None),
            P(None, "rep", None),
            P("rep", None),
            P("rep", None),
            P("rep", None),
            P("rep", None),
            P("rep", None),
            P("rep", None),
            P("rep", None),
            P("rep", None),
            P("rep", None),
            P(),
            P(),
            P(),
        ),
        out_specs=(
            P(),
            P(None, "grp", None),
            P(None, "grp", None),
            P(None, "grp", None),
            P(None, "rep", None),
            P(None, "rep", None),
            P(None, "rep", None),
            P(None, "rep", None),
            P(None, "rep", None),
            P(None, "rep", None),
            P("rep", None),
            P("rep", None),
            P("rep", None),
            P("rep", None),
            P("rep", None),
            P("rep", None),
            P("rep", None),
            P("rep", None),
            P("rep", None),
            P(),
            P(),
            P(),
        ),
        check_vma=False,
    )
```

```python
import functools

import jax
import jax.numpy as jnp
from jax import lax
from jax.experimental import pallas as pl
from jax.experimental.pallas import tpu as pltpu
from jax.sharding import PartitionSpec as P

D_IN = 3456
RANK = 512
CROSS = 3
H1 = 1024
H2 = 1024
H3 = 512
STEP = 10
GROUP = 8
SLOTS = 32
LOW = 128
PAIR = 2
VMEM_BYTES = 60 * 2**20
HINT = 10**10


BETA_ONE = 0.9
BETA_TWO = 0.999
EPSILON = 1e-12
DECAY = 0.01


def split_smalls(smalls):
    extents = [CROSS * D_IN, H1, H2, H3, H3, 1]
    pieces = []
    offset = 0
    for extent in extents:
        pieces.append(smalls[offset : offset + extent])
        offset = offset + extent
    return (pieces[0].reshape(CROSS, D_IN), pieces[1], pieces[2], pieces[3], pieces[4], pieces[5])


def product(left, right):
    return jnp.dot(left, right, preferred_element_type=jnp.float32)


def left_product(left, right):
    return lax.dot_general(
        left, right, (((0,), (0,)), ((), ())), preferred_element_type=jnp.float32
    )


def right_product(left, right):
    return lax.dot_general(
        left, right, (((1,), (1,)), ((), ())), preferred_element_type=jnp.float32
    )


def silu_slope(value):
    logistic = jax.nn.sigmoid(value)
    return logistic * (1.0 + value * (1.0 - logistic))


def slot_ids(row_ids, bag_counts):
    samples, features, slots = row_ids.shape
    live = lax.broadcasted_iota(jnp.int32, row_ids.shape, 2) < bag_counts[:, :, None]
    ids = jnp.pad(jnp.where(live, row_ids, -1), ((0, 0), (0, 0), (0, SLOTS - slots)), constant_values=-1)
    return ids.transpose(1, 0, 2).reshape(features, samples // GROUP, GROUP * SLOTS)


def one_hot(codes, levels):
    rows = jnp.broadcast_to(codes, (16, codes.shape[1])).astype(jnp.bfloat16)
    wanted = lax.broadcasted_iota(jnp.int32, (levels, codes.shape[1]), 0).astype(jnp.float32).astype(jnp.bfloat16)
    hits = jnp.concatenate([rows] * (levels // 16), axis=0) == wanted
    return jnp.where(hits, jnp.ones((), jnp.bfloat16), jnp.zeros((), jnp.bfloat16)).astype(jnp.float8_e4m3fn)


def count_kernel(earlier, ids_ref, *refs):
    hits_ref, code_ref = refs[earlier:]
    samples = hits_ref.shape[1]
    highs = hits_ref.shape[2] // LOW
    ids = ids_ref[0]
    member = lax.broadcasted_iota(jnp.int32, ids.shape, 1) // SLOTS
    code_ref[0] = ((ids >> 7) * GROUP + member).astype(jnp.float32)
    code_ref[1] = (ids & (LOW - 1)).astype(jnp.float32)

    def add_groups(step, unused):
        first = pl.multiple_of(step * 8, 8)
        high_codes = code_ref[0, pl.ds(first, 8), :]
        low_codes = code_ref[1, pl.ds(first, 8), :]
        for pair in range(4):
            products = []
            for row in (2 * pair, 2 * pair + 1):
                high_hits = one_hot(high_codes[row : row + 1], highs * GROUP)
                low_hits = one_hot(low_codes[row : row + 1], LOW)
                products.append(right_product(high_hits, low_hits))
            start = pl.multiple_of(step * 8 * GROUP + pair * 2 * GROUP, 2 * GROUP)
            for high in range(highs):
                part = slice(high * GROUP, (high + 1) * GROUP)
                tile = jnp.concatenate([products[0][part], products[1][part]], axis=0)
                hits_ref[0, pl.ds(start, 2 * GROUP), high * LOW : (high + 1) * LOW] = tile.astype(
                    jnp.bfloat16
                )
        return unused

    lax.fori_loop(0, samples // (8 * GROUP), add_groups, 0)


def count(ids, rows, pieces):
    features, groups, slots = ids.shape
    samples = groups * GROUP
    cuts = [features * piece // pieces for piece in range(pieces + 1)]
    hits = None
    for first, last in zip(cuts[:-1], cuts[1:]):
        earlier = [] if hits is None else [hits]
        hits = pl.pallas_call(
            functools.partial(count_kernel, len(earlier)),
            grid=(last - first,),
            in_specs=[pl.BlockSpec((1, groups, slots), functools.partial(shifted_block, first))]
            + [pl.BlockSpec(memory_space=pl.ANY)] * len(earlier),
            out_specs=pl.BlockSpec((1, samples, rows), functools.partial(shifted_block, first)),
            out_shape=jax.ShapeDtypeStruct((features, samples, rows), jnp.bfloat16),
            input_output_aliases={1: 0} if earlier else {},
            scratch_shapes=[pltpu.VMEM((2, groups, slots), jnp.float32)],
            compiler_params=pltpu.CompilerParams(vmem_limit_bytes=VMEM_BYTES),
            cost_estimate=pl.CostEstimate(flops=1, bytes_accessed=1, transcendentals=0),
        )(ids, *earlier)
    return hits


def shifted_block(first, feature):
    return (feature + first, 0, 0)


def feature_counts(counts_ref, feature):
    lanes = lax.broadcasted_iota(jnp.int32, counts_ref.shape, 1)
    return jnp.sum(jnp.where(lanes == feature, counts_ref[...], 0.0), axis=1, keepdims=True)


def pool_kernel(
    place_ref, hits_ref, own_a, other_a, own_b, other_b, counts_ref, dense_ref, anchor_ref, table_ref, *, keys, half
):
    feature = pl.program_id(0)
    features = pl.num_programs(0) - 1
    mine = place_ref[0]
    member = place_ref[1]
    group = table_ref.shape[0]

    def assemble(own_ref, other_ref, order):
        for position, key in enumerate(order):
            for step in range(group):
                row = lax.rem(member + group - step, group)
                table_ref[row, mine ^ key] = own_ref[position, step, 0]
                table_ref[row, mine ^ (key ^ 1)] = other_ref[position, step, 0]

    @pl.when(feature < half)
    def _():
        assemble(own_a, other_a, keys[0])

    @pl.when((feature >= half) & (feature < features))
    def _():
        assemble(own_b, other_b, keys[1])

    @pl.when(feature < features)
    def _():
        table = table_ref[...].reshape(-1, table_ref.shape[-1])
        anchor_ref[...] = product(hits_ref[0], table) / feature_counts(counts_ref, feature)

    @pl.when(feature == features)
    def _():
        anchor_ref[...] = dense_ref[...]


def pool(hits, first_half, second_half, keys, count_float, dense_input):
    features, samples, rows = hits.shape
    last = features - 1
    half = first_half[0].shape[2]
    halves, group, unused, part, width = first_half[0].shape
    block = (halves, group, 1, part, width)
    low_block = pl.BlockSpec(block, lambda f, place: (0, 0, jnp.minimum(f, half - 1), 0, 0))
    high_block = pl.BlockSpec(block, lambda f, place: (0, 0, jnp.clip(f - half, 0, last - half), 0, 0))
    place = jnp.stack([lax.axis_index("rep"), lax.axis_index("grp")]).astype(jnp.int32)
    return pl.pallas_call(
        functools.partial(pool_kernel, keys=keys, half=half),
        grid_spec=pltpu.PrefetchScalarGridSpec(
            num_scalar_prefetch=1,
            grid=(features + 1,),
            in_specs=[
                pl.BlockSpec((1, samples, rows), lambda f, place: (jnp.minimum(f, last), 0, 0)),
                low_block,
                low_block,
                high_block,
                high_block,
                pl.BlockSpec((samples, features), lambda f, place: (0, 0)),
                pl.BlockSpec((samples, width), lambda f, place: (0, 0)),
            ],
            out_specs=pl.BlockSpec((samples, width), lambda f, place: (0, f)),
            scratch_shapes=[pltpu.VMEM((group, 2 * halves, part, width), jnp.bfloat16)],
        ),
        out_shape=jax.ShapeDtypeStruct((samples, (features + 1) * width), jnp.float32),
        compiler_params=pltpu.CompilerParams(vmem_limit_bytes=VMEM_BYTES),
        cost_estimate=pl.CostEstimate(flops=1, bytes_accessed=1, transcendentals=0),
    )(place, hits, *first_half, *second_half, count_float, dense_input)


def cross_forward_kernel(
    anchor_in, down_ref, up_ref, bias_ref, low_ref, narrow_ref, last_ref, anchor_ref, stream_ref, sum_ref
):
    layer, phase, block = pl.program_id(0), pl.program_id(1), pl.program_id(2)
    layers = pl.num_programs(0)

    @pl.when((layer == 0) & (phase == 0))
    def _():
        anchor_ref[block] = anchor_in[...]
        stream_ref[block] = anchor_in[...]

    @pl.when(phase == 0)
    def _():
        low = stream_ref[block].astype(jnp.bfloat16)
        low_ref[0] = low
        part = product(low, down_ref[0])

        @pl.when(block == 0)
        def _():
            sum_ref[...] = part

        @pl.when(block > 0)
        def _():
            sum_ref[...] += part

    @pl.when((phase == 1) & (block == 0))
    def _():
        narrow_ref[0] = sum_ref[...].astype(jnp.bfloat16)

    @pl.when(phase == 1)
    def _():
        factor = product(narrow_ref[0], up_ref[0]) + bias_ref[0]
        stream = anchor_ref[block] * factor + stream_ref[block]
        stream_ref[block] = stream

        @pl.when(layer == layers - 1)
        def _():
            last_ref[...] = stream.astype(jnp.bfloat16)


def cross_forward(anchor, down, up, bias):
    samples, width = anchor.shape
    layers, unused, rank = down.shape
    blocks = 3
    piece = width // blocks
    final = blocks - 1
    return pl.pallas_call(
        cross_forward_kernel,
        grid=(layers, 2, blocks),
        in_specs=[
            pl.BlockSpec((samples, piece), lambda l, p, j: (0, jnp.where((l == 0) & (p == 0), j, final))),
            pl.BlockSpec((1, piece, rank), lambda l, p, j: (l, jnp.where(p == 0, j, final), 0)),
            pl.BlockSpec((1, rank, piece), lambda l, p, j: (l, 0, jnp.where(p == 1, j, 0))),
            pl.BlockSpec((1, 1, piece), lambda l, p, j: (l, 0, jnp.where(p == 1, j, 0))),
        ],
        out_specs=[
            pl.BlockSpec((1, samples, piece), lambda l, p, j: (l, 0, jnp.where(p == 0, j, final))),
            pl.BlockSpec((1, samples, rank), lambda l, p, j: (l, 0, 0)),
            pl.BlockSpec((samples, piece), lambda l, p, j: (0, jnp.where((l == layers - 1) & (p == 1), j, 0))),
        ],
        out_shape=[
            jax.ShapeDtypeStruct((layers, samples, width), jnp.bfloat16),
            jax.ShapeDtypeStruct((layers, samples, rank), jnp.bfloat16),
            jax.ShapeDtypeStruct((samples, width), jnp.bfloat16),
        ],
        scratch_shapes=[
            pltpu.VMEM((blocks, samples, piece), jnp.float32),
            pltpu.VMEM((blocks, samples, piece), jnp.float32),
            pltpu.VMEM((samples, rank), jnp.float32),
        ],
        compiler_params=pltpu.CompilerParams(vmem_limit_bytes=VMEM_BYTES),
        cost_estimate=pl.CostEstimate(flops=1, bytes_accessed=1, transcendentals=0),
    )(anchor, down, up, bias.reshape(layers, 1, width))


def head_kernel(
    input_ref,
    one_ref,
    late_ref,
    bias_one,
    bias_two,
    bias_three,
    head_ref,
    head_bias,
    target_ref,
    loss_ref,
    grad_head,
    grad_head_bias,
    grad_bias_one,
    grad_bias_two,
    grad_bias_three,
    grad_one,
    grad_late,
    grad_stream,
    sum_ref,
    back_ref,
    *,
    total
):
    step = pl.program_id(0)
    blocks = pl.num_programs(0) // 2

    @pl.when(step < blocks)
    def _():
        part = product(input_ref[...], one_ref[...])

        @pl.when(step == 0)
        def _():
            sum_ref[...] = part

        @pl.when(step > 0)
        def _():
            sum_ref[...] += part

    @pl.when(step == blocks)
    def _():
        pre_one = sum_ref[...] + bias_one[...]
        in_two = jax.nn.silu(pre_one).astype(jnp.bfloat16)
        two = late_ref[:, :H2]
        three = late_ref[:, H2:]
        pre_two = product(in_two, two) + bias_two[...]
        in_three = jax.nn.silu(pre_two).astype(jnp.bfloat16)
        pre_three = product(in_three, three) + bias_three[...]
        top = jax.nn.silu(pre_three)
        head = head_ref[...]
        target = target_ref[...]
        logit = jnp.sum(top * head, axis=1, keepdims=True) + head_bias[...]
        losses = jnp.maximum(logit, 0.0) + jnp.log1p(jnp.exp(-jnp.abs(logit))) - target * logit
        loss_ref[...] = jnp.sum(losses, axis=0, keepdims=True)
        grad_logit = (jax.nn.sigmoid(logit) - target) / total
        grad_head[...] = jnp.sum(grad_logit * top, axis=0, keepdims=True)
        grad_head_bias[...] = jnp.sum(grad_logit, axis=0, keepdims=True)
        back = (grad_logit * head * silu_slope(pre_three)).astype(jnp.bfloat16)
        grad_bias_three[...] = jnp.sum(back.astype(jnp.float32), axis=0, keepdims=True)
        grad_late[:, H2:] = left_product(in_three, back).astype(jnp.bfloat16)
        back = (right_product(back, three) * silu_slope(pre_two)).astype(jnp.bfloat16)
        grad_bias_two[...] = jnp.sum(back.astype(jnp.float32), axis=0, keepdims=True)
        grad_late[:, :H2] = left_product(in_two, back).astype(jnp.bfloat16)
        back = (right_product(back, two) * silu_slope(pre_one)).astype(jnp.bfloat16)
        grad_bias_one[...] = jnp.sum(back.astype(jnp.float32), axis=0, keepdims=True)
        back_ref[...] = back

    @pl.when(step >= blocks)
    def _():
        grad_one[...] = left_product(input_ref[...], back_ref[...]).astype(jnp.bfloat16)
        grad_stream[...] = right_product(back_ref[...], one_ref[...])


def head(inputs, one, late, biases, head_weight, head_bias, target, total):
    samples, width = inputs.shape
    blocks = 3
    piece = width // blocks

    def whole(shape):
        return pl.BlockSpec(shape, lambda s: (0,) * len(shape))

    rows = [bias.reshape(1, -1) for bias in biases] + [head_weight.reshape(1, -1), head_bias.reshape(1, 1)]
    small = [(1, 1), (1, H3), (1, 1), (1, H1), (1, H2), (1, H3)]
    return pl.pallas_call(
        functools.partial(head_kernel, total=total),
        grid=(2 * blocks,),
        in_specs=[
            pl.BlockSpec((samples, piece), lambda s: (0, lax.rem(s, blocks))),
            pl.BlockSpec((piece, H1), lambda s: (lax.rem(s, blocks), 0)),
            whole(late.shape),
        ]
        + [whole(row.shape) for row in rows]
        + [whole((samples, 1))],
        out_specs=[whole(shape) for shape in small]
        + [
            pl.BlockSpec((piece, H1), lambda s: (jnp.maximum(s - blocks, 0), 0)),
            whole(late.shape),
            pl.BlockSpec((samples, piece), lambda s: (0, jnp.maximum(s - blocks, 0))),
        ],
        out_shape=[jax.ShapeDtypeStruct(shape, jnp.float32) for shape in small]
        + [
            jax.ShapeDtypeStruct(one.shape, jnp.bfloat16),
            jax.ShapeDtypeStruct(late.shape, jnp.bfloat16),
            jax.ShapeDtypeStruct((samples, width), jnp.float32),
        ],
        scratch_shapes=[pltpu.VMEM((samples, H1), jnp.float32), pltpu.VMEM((samples, H1), jnp.bfloat16)],
        compiler_params=pltpu.CompilerParams(vmem_limit_bytes=VMEM_BYTES),
        cost_estimate=pl.CostEstimate(flops=1, bytes_accessed=1, transcendentals=0),
    )(inputs, one, late, *rows, target)


def cross_backward_kernel(
    core_ref,
    anchor_in,
    grad_in,
    low_ref,
    narrow_ref,
    down_ref,
    up_ref,
    bias_ref,
    counts_ref,
    send_ref,
    keep_ref,
    grad_down,
    grad_bias,
    grad_summed,
    anchor_ref,
    stream_ref,
    total_ref,
    sum_ref,
    back_ref,
    both_ref,
):
    layer, phase, block = pl.program_id(0), pl.program_id(1), pl.program_id(2)
    layers = pl.num_programs(0)

    @pl.when((layer == 0) & (phase == 0))
    def _():
        anchor_ref[block] = anchor_in[...]
        stream_ref[block] = grad_in[...]
        total_ref[block] = jnp.zeros(grad_in.shape, jnp.float32)

    @pl.when(phase == 0)
    def _():
        grad_next = stream_ref[block]
        grad_factor = (anchor_ref[block] * grad_next).astype(jnp.bfloat16)
        grad_bias[0] = jnp.sum(grad_factor.astype(jnp.float32), axis=0, keepdims=True)
        narrow = narrow_ref[0]
        both_ref[...] = left_product(narrow, grad_factor).astype(jnp.bfloat16).reshape(both_ref.shape)
        core = core_ref[0]
        send_ref[0] = both_ref[:, 1 - core]
        keep_ref[0] = both_ref[:, core]
        factor = product(narrow, up_ref[0]) + bias_ref[0]
        total_ref[block] += factor * grad_next
        part = right_product(grad_factor, up_ref[0])

        @pl.when(block == 0)
        def _():
            sum_ref[...] = part

        @pl.when(block > 0)
        def _():
            sum_ref[...] += part

    @pl.when((phase == 1) & (block == 0))
    def _():
        back_ref[...] = sum_ref[...].astype(jnp.bfloat16)

    @pl.when(phase == 1)
    def _():
        back = back_ref[...]
        grad_down[0] = left_product(low_ref[0], back).astype(jnp.bfloat16)
        grad_stream = stream_ref[block] + right_product(back, down_ref[0])
        stream_ref[block] = grad_stream

        @pl.when(layer == layers - 1)
        def _():
            features = grad_stream.shape[1] // LOW
            total = total_ref[block] + grad_stream
            for index in range(features):
                counts = jnp.maximum(feature_counts(counts_ref, block * features + index), 1.0)
                part = slice(index * LOW, (index + 1) * LOW)
                grad_summed[:, part] = (total[:, part] / counts).astype(jnp.bfloat16)


def cross_backward(anchor, grad_stream, lows, narrows, down, up, bias, count_float, core, repeats):
    samples, width = anchor.shape
    layers, unused, rank = down.shape
    blocks = 3
    piece = width // blocks
    final = blocks - 1
    share = rank // repeats

    def first_pass(l, p, j, core):
        return (0, jnp.where((l == 0) & (p == 0), j, final))

    def up_block(l, p, j, core):
        return (layers - 1 - l, 0, jnp.where(p == 0, j, final))

    def low_block(l, p, j, core):
        return (layers - 1 - l, 0, jnp.where(p == 1, j, 0))

    def down_block(l, p, j, core):
        return (layers - 1 - l, jnp.where(p == 1, j, 0), 0)

    half = jax.ShapeDtypeStruct((layers, repeats // 2, share, width), jnp.bfloat16)
    half_spec = pl.BlockSpec(
        (1, repeats // 2, share, piece),
        lambda l, p, j, core: (layers - 1 - l, 0, 0, jnp.where(p == 0, j, final)),
    )
    return pl.pallas_call(
        cross_backward_kernel,
        grid_spec=pltpu.PrefetchScalarGridSpec(
            num_scalar_prefetch=1,
            grid=(layers, 2, blocks),
            in_specs=[
                pl.BlockSpec((samples, piece), first_pass),
                pl.BlockSpec((samples, piece), first_pass),
                pl.BlockSpec((1, samples, piece), low_block),
                pl.BlockSpec((1, samples, rank), lambda l, p, j, core: (layers - 1 - l, 0, 0)),
                pl.BlockSpec((1, piece, rank), down_block),
                pl.BlockSpec((1, rank, piece), up_block),
                pl.BlockSpec((1, 1, piece), up_block),
                pl.BlockSpec(count_float.shape, lambda l, p, j, core: (0, 0)),
            ],
            out_specs=[
                half_spec,
                half_spec,
                pl.BlockSpec((1, piece, rank), down_block),
                pl.BlockSpec((1, 1, piece), up_block),
                pl.BlockSpec(
                    (samples, piece),
                    lambda l, p, j, core: (0, jnp.where((l == layers - 1) & (p == 1), j, 0)),
                ),
            ],
            scratch_shapes=[
                pltpu.VMEM((blocks, samples, piece), jnp.float32),
                pltpu.VMEM((blocks, samples, piece), jnp.float32),
                pltpu.VMEM((blocks, samples, piece), jnp.float32),
                pltpu.VMEM((samples, rank), jnp.float32),
                pltpu.VMEM((samples, rank), jnp.bfloat16),
                pltpu.VMEM((repeats // 2, 2, share, piece), jnp.bfloat16),
            ],
        ),
        out_shape=[
            half,
            half,
            jax.ShapeDtypeStruct(down.shape, jnp.bfloat16),
            jax.ShapeDtypeStruct((layers, 1, width), jnp.float32),
            jax.ShapeDtypeStruct((samples, width), jnp.bfloat16),
        ],
        compiler_params=pltpu.CompilerParams(vmem_limit_bytes=VMEM_BYTES),
        cost_estimate=pl.CostEstimate(
            flops=10**12,
            bytes_accessed=layers * width * (8 * rank + 2 * samples) + 10 * samples * width,
            transcendentals=0,
        ),
    )(core, anchor, grad_stream, lows, narrows, down, up, bias.reshape(layers, 1, width), count_float)


def row_kernel(earlier, core_ref, hits_ref, grad_ref, *refs):
    send_ref, keep_ref, both_ref = refs[earlier:]
    core = core_ref[0]
    for index in range(PAIR):
        grad = grad_ref[:, index * LOW : (index + 1) * LOW]
        rows = left_product(grad, hits_ref[index]).T
        both_ref[index] = rows.astype(jnp.bfloat16).reshape(both_ref.shape[1:])
        send_ref[index] = both_ref[index, :, 1 - core]
        keep_ref[index] = both_ref[index, :, core]


def row_gradient(hits, grad_summed, start, stop, group, core, pieces, hint):
    unused, samples, rows = hits.shape
    half = rows // group // 2
    shape = jax.ShapeDtypeStruct((stop - start, group, half, LOW), jnp.bfloat16)
    cuts = [start + (stop - start) // PAIR * piece // pieces * PAIR for piece in range(pieces + 1)]
    results = []
    for first, last in zip(cuts[:-1], cuts[1:]):
        spec = pl.BlockSpec((PAIR, group, half, LOW), functools.partial(row_block, (first - start) // PAIR))
        results = pl.pallas_call(
            functools.partial(row_kernel, len(results)),
            grid_spec=pltpu.PrefetchScalarGridSpec(
                num_scalar_prefetch=1,
                grid=((last - first) // PAIR,),
                in_specs=[
                    pl.BlockSpec((PAIR, samples, rows), functools.partial(hits_block, first // PAIR)),
                    pl.BlockSpec((samples, PAIR * LOW), functools.partial(column_block, first // PAIR)),
                ]
                + [pl.BlockSpec(memory_space=pl.ANY)] * len(results),
                out_specs=[spec, spec],
                scratch_shapes=[pltpu.VMEM((PAIR, group, 2, half, LOW), jnp.bfloat16)],
            ),
            out_shape=[shape, shape],
            input_output_aliases={3: 0, 4: 1} if results else {},
            compiler_params=pltpu.CompilerParams(vmem_limit_bytes=VMEM_BYTES),
            cost_estimate=pl.CostEstimate(flops=hint, bytes_accessed=1, transcendentals=0),
        )(core, hits, grad_summed, *results)
    return results


def row_block(first, feature, core):
    return (feature + first, 0, 0, 0)


def hits_block(first, feature, core):
    return (feature + first, 0, 0)


def column_block(first, feature, core):
    return (0, feature + first)


def flip(value, bit):
    return lax.ppermute(value, "rep", [(i, i ^ bit) for i in range(lax.axis_size("rep"))])


def shift(value, step):
    size = lax.axis_size("grp")
    return lax.ppermute(value, "grp", [(i, (i + step) % size) for i in range(size)])


def across():
    return [1 << i for i in range(1, lax.axis_size("rep").bit_length() - 1)]


def gather_across(value, order):
    keys = [0]
    for bit in order:
        value = jnp.concatenate([value, flip(value, bit)], axis=0)
        keys = keys + [key ^ bit for key in keys]
    return value, keys


def place(value, keys, axis, index_of):
    mine = lax.axis_index("rep")
    extent = value.shape[axis + 1]
    shape = list(value.shape[1:])
    shape[axis] = extent * len(keys)
    whole = jnp.zeros(shape, value.dtype)
    for position, key in enumerate(keys):
        whole = lax.dynamic_update_slice_in_dim(whole, value[position], index_of(mine ^ key) * extent, axis)
    return whole


def after(value, earlier):
    return lax.optimization_barrier((value, earlier))[0]


class HalvingSum:
    def __init__(self, keep, received, bits, order, axis):
        self.keep, self.received = keep, received
        self.left, self.order, self.axis = list(bits), list(order), axis

    def step(self, *earlier):
        bit = self.order.pop(0)
        position = self.axis + self.left.index(bit)
        self.left.remove(bit)
        mine = (lax.axis_index("rep") // bit) % 2
        pair = after((self.keep, self.received), earlier)
        send, keep = (
            sum(lax.dynamic_index_in_dim(item, index, position, keepdims=False) for item in pair)
            for index in (1 - mine, mine)
        )
        self.keep, self.sent = keep, send
        self.received = flip(self.sent, bit)

    def result(self):
        return self.keep + self.received


class GroupSum:
    def __init__(self, *shares):
        self.size = lax.axis_size("grp")
        self.mine = lax.axis_index("grp")
        self.shares = shares

    def scatter(self, *earlier):
        chunks = [share.reshape(self.size, -1, LOW) for share in after(self.shares, earlier)]
        self.lengths = [chunk.shape[1] for chunk in chunks]
        sent = []
        for step in range(self.size):
            index = lax.rem(self.mine + step, self.size)
            parts = [lax.dynamic_index_in_dim(chunk, index, 0, keepdims=False) for chunk in chunks]
            sent.append(jnp.concatenate(parts, axis=0) if len(parts) > 1 else parts[0])
        self.sent = sent
        self.received = [shift(part, step) for step, part in enumerate(self.sent) if step]
        self.total = sum(part.astype(jnp.float32) for part in [self.sent[0]] + self.received).astype(sent[0].dtype)

    def gather(self, *earlier):
        self.sent = after(self.total, earlier)
        self.received = [shift(self.sent, step) for step in range(1, self.size)]

    def result(self):
        whole = jnp.zeros((self.size,) + self.total.shape, self.total.dtype)
        for step, part in enumerate([self.sent] + self.received):
            index = lax.rem(self.mine + self.size - step, self.size)
            whole = lax.dynamic_update_index_in_dim(whole, part, index, 0)
        results = []
        offset = 0
        for share, length in zip(self.shares, self.lengths):
            part = whole[:, offset : offset + length]
            results.append(part.reshape(share.shape).astype(jnp.float32))
            offset = offset + length
        return results


class SmallSum:
    def __init__(self, value):
        self.value, self.received = value, None
        self.left = [("rep", bit) for bit in [1] + across()]
        bit = 1
        while bit < lax.axis_size("grp"):
            self.left.append(("grp", bit))
            bit = 2 * bit

    def step(self):
        if self.received is not None:
            self.value = self.value + self.received
        axis, bit = self.left.pop(0)
        self.sent = self.value
        self.received = lax.ppermute(self.value, axis, [(i, i ^ bit) for i in range(lax.axis_size(axis))])

    def finish(self):
        while self.left:
            self.step()
        self.value = self.value + self.received


def adamw(weight, grad, first, second, rate):
    first = BETA_ONE * first + (1.0 - BETA_ONE) * grad
    second = BETA_TWO * second + (1.0 - BETA_TWO) * grad * grad
    corr_one = 1.0 - BETA_ONE**STEP
    corr_two = 1.0 - BETA_TWO**STEP
    moved = first / corr_one / (jnp.sqrt(second / corr_two) + EPSILON) + DECAY * weight
    return (weight - rate * moved, first, second)


def on_device(
    row_ids,
    bag_counts,
    labels,
    dense_input,
    tables,
    table_first,
    table_second,
    cross_down,
    down_first,
    down_second,
    cross_up,
    up_first,
    up_second,
    hidden_one,
    one_first,
    one_second,
    hidden_two,
    two_first,
    two_second,
    hidden_three,
    three_first,
    three_second,
    smalls,
    small_first,
    small_second,
):
    up_down = across()
    down_up = up_down[::-1]
    down_all = lax.all_gather(cross_down.astype(jnp.bfloat16), "rep", axis=1, tiled=True)
    up_all = lax.all_gather(cross_up.astype(jnp.bfloat16), "rep", axis=1, tiled=True)
    one_all = lax.all_gather(hidden_one.astype(jnp.bfloat16), "rep", axis=0, tiled=True)
    cross_bias, bias_one, bias_two, bias_three, head_weight, head_bias = split_smalls(smalls)
    group = lax.axis_size("grp")
    samples = row_ids.shape[0]
    repeats = lax.axis_size("rep")
    features, extent, width = tables.shape
    part = extent // repeats
    own_part = lax.dynamic_slice_in_dim(tables, lax.axis_index("rep") * part, part, axis=1)
    own_part = own_part.astype(jnp.bfloat16)
    own_parts = [own_part] + [shift(own_part, step) for step in range(1, group)]
    half = features // 2
    even = (half + 1) // PAIR * PAIR
    row_spans = ((0, even, up_down), (even, features, down_up))
    spans = ((0, half, up_down), (half, features, down_up))
    table_halves = []
    table_keys = []
    for first, last, order in spans:
        rows = jnp.stack([piece[first:last] for piece in own_parts])[None]
        rows, keys = gather_across(rows, order)
        table_halves.append((rows, flip(rows, 1)))
        table_keys.append(keys)
    late = jnp.concatenate([hidden_two, hidden_three], axis=1).astype(jnp.bfloat16)
    late_all = place(*gather_across(late[None], up_down + [1]), 0, lambda index: index)
    count_float = bag_counts.astype(jnp.float32)
    hits = count(slot_ids(row_ids, bag_counts), group * extent, 4)
    anchor = pool(hits, table_halves[0], table_halves[1], table_keys, count_float, dense_input)
    lows, narrows, in_one = cross_forward(anchor, down_all, up_all, cross_bias)
    total_samples = samples * lax.axis_size("rep") * group
    target = labels.astype(jnp.float32)[:, None]
    (
        loss_local,
        grad_head,
        grad_head_bias,
        bias_grad_one,
        bias_grad_two,
        bias_grad_three,
        grad_one,
        grad_late,
        grad_stream,
    ) = head(
        in_one, one_all, late_all, (bias_one, bias_two, bias_three), head_weight, head_bias, target, total_samples
    )
    share_one = lax.psum_scatter(grad_one, "rep", scatter_dimension=0, tiled=True)
    core = (lax.axis_index("rep") % 2).astype(jnp.int32).reshape(1)
    bits = up_down[::-1]
    late_blocks = grad_late.reshape((2,) * len(bits) + (2, -1) + grad_late.shape[1:])
    late_send, late_keep = (
        lax.dynamic_index_in_dim(late_blocks, index, len(bits), keepdims=False) for index in (1 - core[0], core[0])
    )
    late_sum = HalvingSum(late_keep, flip(late_send, 1), bits, up_down, 0)
    late_sum.step()
    send_up, keep_up, grad_down, bias_grads, grad_summed = cross_backward(
        anchor,
        after(grad_stream, late_sum.sent),
        lows,
        narrows,
        down_all,
        up_all,
        cross_bias,
        count_float,
        core,
        repeats,
    )
    share_down = lax.psum_scatter(grad_down, "rep", scatter_dimension=1, tiled=True)
    received_up = flip(send_up, 1)
    share_rows = keep_up.shape[2] // 2
    shape = (CROSS,) + (2,) * len(bits) + (2, share_rows, D_IN)
    up_sums = [
        HalvingSum(
            lax.index_in_dim(keep_up.reshape(shape), index, len(bits) + 1, keepdims=False),
            lax.index_in_dim(received_up.reshape(shape), index, len(bits) + 1, keepdims=False),
            bits,
            order,
            1,
        )
        for index, order in ((0, up_down), (1, down_up))
    ]
    small_grad = jnp.concatenate(
        [
            item.reshape(-1)
            for item in (
                bias_grads,
                bias_grad_one,
                bias_grad_two,
                bias_grad_three,
                grad_head,
                grad_head_bias,
                loss_local,
            )
        ]
    )
    up_p, up_q = up_sums
    row_sums = []
    grad_rows = after(grad_summed, late_sum.received)
    for first, last, order in row_spans:
        send, keep = row_gradient(hits, grad_rows, first, last, group, core, 1, 10**12 if first == 0 else HINT)
        shape = (last - first, group) + (2,) * len(bits) + (part, width)
        row_sums.append(HalvingSum(keep.reshape(shape), flip(send, 1).reshape(shape), bits, order, 2))
        if len(row_sums) == 1:
            for step in bits[1:]:
                late_sum.step(keep)
            for item in up_sums:
                item.step(late_sum.sent)
            grad_rows = after(grad_rows, [item.sent for item in up_sums] + [late_sum.sent, share_one])
    row_p, row_q = row_sums
    one_total = GroupSum(share_one, late_sum.result())
    one_total.scatter(keep, row_p.received)
    one_total.gather()
    for step in bits[1:]:
        for item in up_sums:
            item.step(one_total.sent)
    for item in row_sums:
        item.step(up_p.sent, up_q.sent)
    share_up = jnp.concatenate([item.result() for item in up_sums], axis=1)
    share_up, share_down = lax.psum((share_up, share_down), "grp")
    for step in bits[1:]:
        for item in row_sums:
            item.step(up_p.received, up_q.received)
    row_parts = [item.result() for item in row_sums]
    row_total = GroupSum(jnp.concatenate(row_parts, axis=0).transpose(1, 0, 2, 3))
    row_total.scatter(share_up, share_down)
    small = SmallSum(after(small_grad, row_parts))
    small.step()
    small.step()
    small.value = after(small.value, row_total.sent)
    small.finish()
    row_share = row_total.total.reshape(features, part, width)
    share_one, share_late = one_total.result()
    share_up, share_down = share_up.astype(jnp.float32), share_down.astype(jnp.float32)
    share_two, share_three = share_late[:, :H2], share_late[:, H2:]
    small_sum, loss_sum = small.value[:-1], small.value[-1]
    new_one, new_one_first, new_one_second = adamw(
        hidden_one, share_one, one_first, one_second, D_IN ** (-0.5)
    )
    new_two, new_two_first, new_two_second = adamw(
        hidden_two, share_two, two_first, two_second, H1 ** (-0.5)
    )
    new_three, new_three_first, new_three_second = adamw(
        hidden_three, share_three, three_first, three_second, H2 ** (-0.5)
    )
    table_grads = []
    for first, last, order in spans:
        value, keys = gather_across(row_share[None, first:last], order + [1])
        table_grads.append(place(value, keys, 1, lambda index: (index % 2) * (repeats // 2) + index // 2))
    table_grad = jnp.concatenate(table_grads, axis=0).astype(jnp.float32)
    new_up, new_up_first, new_up_second = adamw(
        cross_up, share_up, up_first, up_second, RANK ** (-0.5)
    )
    new_tables, new_table_first, new_table_second = adamw(
        tables, table_grad, table_first, table_second, 1.0
    )
    new_down, new_down_first, new_down_second = adamw(
        cross_down, share_down, down_first, down_second, D_IN ** (-0.5)
    )
    new_smalls, new_small_first, new_small_second = adamw(
        smalls, small_sum, small_first, small_second, 0.1
    )
    return (
        loss_sum,
        new_tables,
        new_table_first,
        new_table_second,
        new_down,
        new_down_first,
        new_down_second,
        new_up,
        new_up_first,
        new_up_second,
        new_one,
        new_one_first,
        new_one_second,
        new_two,
        new_two_first,
        new_two_second,
        new_three,
        new_three_first,
        new_three_second,
        new_smalls,
        new_small_first,
        new_small_second,
    )


def solution(mesh):
    return jax.shard_map(
        on_device,
        mesh=mesh,
        in_specs=(
            P(("rep", "grp"), None, None),
            P(("rep", "grp"), None),
            P(("rep", "grp")),
            P(("rep", "grp"), None),
            P(None, "grp", None),
            P(None, "grp", None),
            P(None, "grp", None),
            P(None, "rep", None),
            P(None, "rep", None),
            P(None, "rep", None),
            P(None, "rep", None),
            P(None, "rep", None),
            P(None, "rep", None),
            P("rep", None),
            P("rep", None),
            P("rep", None),
            P("rep", None),
            P("rep", None),
            P("rep", None),
            P("rep", None),
            P("rep", None),
            P("rep", None),
            P(),
            P(),
            P(),
        ),
        out_specs=(
            P(),
            P(None, "grp", None),
            P(None, "grp", None),
            P(None, "grp", None),
            P(None, "rep", None),
            P(None, "rep", None),
            P(None, "rep", None),
            P(None, "rep", None),
            P(None, "rep", None),
            P(None, "rep", None),
            P("rep", None),
            P("rep", None),
            P("rep", None),
            P("rep", None),
            P("rep", None),
            P("rep", None),
            P("rep", None),
            P("rep", None),
            P("rep", None),
            P(),
            P(),
            P(),
        ),
        check_vma=False,
    )
```
